128 devices in a mesh: sec: 16 (over z_hi, x, core), tile: 8 (over z_lo, y).
Axes of the slice: x: 4, y: 4, z: 4 (z_hi: 2, z_lo: 2; z = z_hi * 2 + z_lo), core: 2. Of those that a mesh axis runs over, the one named last changes fastest.
Arguments:
- section_image: bfloat16 [32, 256, 1024], P('sec', 'tile'), may hold values from -6 to 6
- partner_row: int32 [32], P('sec'), may hold values from 0 to 31, as said below
- base_shift: int32 [32, 2, 128, 512], P('sec', None, 'tile'), may hold values from -4 to 3
- bilinear_frac: float32 [32, 2, 128, 512], P('sec', None, 'tile'), may hold values from 0 to 1
- first_kernel: bfloat16 [64, 16], replicated, may hold values from -1.5 to 1.5
- initial_conv_bias: float32 [64], replicated, may hold values from -3 to 3
- second_kernel: bfloat16 [64, 256], replicated, may hold values from -0.375 to 0.375
- second_bias: float32 [64], replicated, may hold values from -3 to 3
- edge_ends: int32 [32, 2, 2048], P('sec', None, 'tile'), may hold values from 0 to 255, as said below
- edge_count: int32 [32, 8], P('sec', 'tile'), may hold values from 64 to 256, as said below
- stiffness: float32 [32, 2048], P('sec', 'tile'), may hold values from 0.05 to 0.5
Outputs:
- correlation: bfloat16 [32, 81, 64, 256], P('sec', None, 'tile')
- mismatch: float32 [32, 128, 512], P('sec', 'tile')
- forces: float32 [32, 2, 256], P('sec', None, 'tile')
The draws below stay inside these ranges and needn't reach their ends.
Inputs may be any that keep to these rules, and one draw needn't show every extreme that they name: Row p holds section z = (p mod 2) * 16 + floor(p / 2). partner_row[p] is the row of section z + 1, or of section z + 2 where section z + 1 is unusable, counted modulo 32. Among the 2 rows of every index of sec, both kinds occur. edge_ends[s, 1, e] is edge_ends[s, 0, e] plus 1, 32, 33 or 31, modulo 256. `edge_count`: in every section one block of slots is fully live and another has 64 live slots.
All inputs are finite; a program needn't handle non-finite values.
Results may differ from the reference program's by a relative error of at most 0.0036.
Values may be sent and summed in bfloat16 or wider, within the bound.
A program may use at most 128 MiB of HBM per device.

```python
import math
import jax
import jax.numpy as jnp
from jax import lax

C = 64
REACH = 4
WARP_MAX = 4
SPACING = 16
SEC_DEV = 2
COLS = 1024
E_DEV = 256
NSEC = 32
ROWS = 256
H0 = 128
W0 = 512
VCOL = 32
VERT = 256
EDGES = 2048


def draw_partner_row(key, part):
    dev_count = NSEC // SEC_DEV
    sections = jnp.arange(NSEC, dtype=jnp.int32)
    coin_key = jax.random.fold_in(key, 5)
    distant_random_key = jax.random.fold_in(key, 7)
    near_key = jax.random.fold_in(key, 9)
    coin_flip = (jax.random.randint(coin_key, (NSEC,), 0, 10) < 3).astype(jnp.int32)
    far_slot = jax.random.randint(distant_random_key, (dev_count,), 0, SEC_DEV)
    near_step = jax.random.randint(near_key, (dev_count,), 0, SEC_DEV - 1)
    near_slot = (far_slot + 1 + near_step) % SEC_DEV
    holder_dev = sections % dev_count
    holder_slot = sections // dev_count
    skipped = jnp.where(holder_slot == far_slot[holder_dev], 1, jnp.where(holder_slot == near_slot[holder_dev], 0, coin_flip))
    follower = (sections + 1 + skipped) % NSEC
    holder_row = holder_dev * SEC_DEV + holder_slot
    return jnp.zeros((NSEC,), jnp.int32).at[holder_row].set(holder_row[follower]).astype(jnp.int32)


def draw_edge_ends(key, part):
    first_key = jax.random.fold_in(key, 11)
    second_key = jax.random.fold_in(key, 23)
    start_ids = jax.random.randint(first_key, (NSEC, EDGES), 0, VERT)
    step_pick = jax.random.randint(second_key, (NSEC, EDGES), 0, 4)
    steps_table = jnp.array([1, VCOL, VCOL + 1, VCOL - 1], jnp.int32)
    end_ids = (start_ids + steps_table[step_pick]) % VERT
    return jnp.stack([start_ids, end_ids], axis=1).astype(jnp.int32)


def draw_edge_count(key, part):
    tile_count = EDGES // E_DEV
    counts = jax.random.randint(key, (NSEC, tile_count), E_DEV // 4, E_DEV + 1)
    row_ids = jnp.arange(NSEC, dtype=jnp.int32)
    counts = counts.at[row_ids, row_ids % tile_count].set(E_DEV)
    counts = counts.at[row_ids, (row_ids + 1) % tile_count].set(E_DEV // 4)
    return counts.astype(jnp.int32)


def with_ends(drawn, key, smallest, high):
    spot = [jax.random.randint(jax.random.fold_in(key, axis), (), 0, length) for axis, length in enumerate(drawn.shape)]
    main_axis = drawn.shape.index(max(drawn.shape))
    next_to = spot[:main_axis] + [(spot[main_axis] + 1) % drawn.shape[main_axis]] + spot[main_axis + 1:]
    return drawn.at[tuple(spot)].set(smallest).at[tuple(next_to)].set(high)


def block_levels(stream_key, dims, shards, low, high):
    def one(axis_at, parts):
        steps = jax.random.uniform(jax.random.fold_in(jax.random.fold_in(stream_key, 6), axis_at), (parts,), jnp.float32, low / len(shards), high / len(shards))
        return jnp.repeat(jnp.exp(steps), dims[axis_at] // parts).reshape((-1,) + (1,) * (len(dims) - axis_at - 1))

    loudness = one(*shards[0])
    for cut in shards[1:]:
        loudness = loudness * one(*cut)
    return loudness


def bell_draw(rng, dims, width, most, split=(), kind=jnp.bfloat16):
    gain = block_levels(rng, dims, split, -0.22, 0.18) if split else 1.0
    entries = jax.random.normal(rng, dims, jnp.float32) * width * gain
    return jnp.minimum(jnp.maximum(entries, -most), most).astype(kind)


def setup_inputs(seed: int = 0) -> dict:
    key_list = jax.random.split(jax.random.key(seed), 12)
    section_image = bell_draw(key_list[0], (NSEC, ROWS, COLS), 1.0, 6.0, ((0, 16), (1, 8)))
    partner_row = draw_partner_row(jax.random.fold_in(key_list[11], 71), 0)
    base_shift = with_ends(jax.random.randint(key_list[2], (NSEC, 2, H0, W0), 0 - WARP_MAX, WARP_MAX), jax.random.fold_in(key_list[2], 1), 0 - WARP_MAX, WARP_MAX - 1).astype(jnp.int32)
    bilinear_frac = jnp.clip(1.0 * jax.random.uniform(key_list[3], (NSEC, 2, H0, W0), jnp.float32) ** block_levels(key_list[3], (NSEC, 2, H0, W0), ((0, 16), (2, 8)), -0.2, 0.2), 0.0, 1.0)
    first_kernel = bell_draw(key_list[4], (C, 16), 16 ** -0.5, 1.5)
    initial_conv_bias = bell_draw(key_list[5], (C,), 0.5, 3.0, (), jnp.float32)
    second_kernel = bell_draw(key_list[6], (C, 4 * C), (4 * C) ** -0.5, 0.375)
    second_bias = bell_draw(key_list[7], (C,), 0.5, 3.0, (), jnp.float32)
    edge_ends = draw_edge_ends(jax.random.fold_in(key_list[11], 71), 0)
    edge_count = draw_edge_count(jax.random.fold_in(key_list[11], 71), 0)
    stiffness = jnp.clip(jnp.exp(math.log(0.5) - 2.3025851 * jax.random.uniform(key_list[10], (NSEC, EDGES), jnp.float32) ** block_levels(key_list[10], (NSEC, EDGES), ((0, 16), (1, 8)), -0.2, 0.2)), 0.05, 0.5)
    return {"section_image": section_image, "partner_row": partner_row, "base_shift": base_shift, "bilinear_frac": bilinear_frac, "first_kernel": first_kernel, "initial_conv_bias": initial_conv_bias, "second_kernel": second_kernel, "second_bias": second_bias, "edge_ends": edge_ends, "edge_count": edge_count, "stiffness": stiffness}


def coarsen(fine_map, second_kernel, second_bias):
    sections, channels, fine_rows, fine_cols = fine_map.shape
    blocks = fine_map.reshape(sections, channels, fine_rows // 2, 2, fine_cols // 2, 2)
    kernel_grid = second_kernel.reshape(second_kernel.shape[0], 2, 2, channels)
    coarse_pre = jnp.einsum("oabc,scyaxb->soyx", kernel_grid.astype(jnp.float32), blocks.astype(jnp.float32))
    return jax.nn.relu(coarse_pre + second_bias[None, :, None, None]).astype(jnp.bfloat16)


def encode_frame(framed_image, first_kernel, initial_conv_bias, second_kernel, second_bias):
    sections, frame_rows, columns = framed_image.shape
    inner_rows = frame_rows - 2
    bordered = jnp.pad(framed_image, ((0, 0), (0, 0), (1, 1)))
    pieces = []
    for row_off in range(4):
        for col_off in range(4):
            pieces.append(bordered[:, row_off:row_off + inner_rows:2, col_off:col_off + columns:2])
    patches = jnp.stack(pieces, axis=0)
    fine_pre = jnp.einsum("ck,ksyx->scyx", first_kernel.astype(jnp.float32), patches.astype(jnp.float32))
    fine_map = jax.nn.relu(fine_pre + initial_conv_bias[None, :, None, None]).astype(jnp.bfloat16)
    return fine_map, coarsen(fine_map, second_kernel, second_bias)


def correlate(coarse_own, coarse_wide):
    sections, channels, coarse_rows, coarse_cols = coarse_own.shape
    window = 2 * REACH + 1
    results = []
    own_wide = coarse_own.astype(jnp.float32)
    for row_off in range(window):
        row_band = coarse_wide[:, :, row_off:row_off + coarse_rows, :]
        stacked = jnp.stack([row_band[:, :, :, col_off:col_off + coarse_cols] for col_off in range(window)], axis=1)
        results.append(jnp.einsum("scyx,sjcyx->sjyx", own_wide, stacked.astype(jnp.float32)))
    return (jnp.concatenate(results, axis=1) / channels).astype(jnp.bfloat16)


def compare(fine_own, fine_tall, base_shift, bilinear_frac):
    sections, channels, fine_rows, fine_cols = fine_own.shape
    stride = fine_cols + 2 * WARP_MAX
    framed = jnp.pad(fine_tall, ((0, 0), (0, 0), (0, 0), (WARP_MAX, WARP_MAX))).reshape(sections, channels, -1)
    row_ids = lax.broadcasted_iota(jnp.int32, (fine_rows, fine_cols), 0)
    col_ids = lax.broadcasted_iota(jnp.int32, (fine_rows, fine_cols), 1)

    def single(operands):
        own_map, source_section, offsets, weights = operands
        anchor = (row_ids + offsets[0] + WARP_MAX) * stride + col_ids + offsets[1] + WARP_MAX
        row_weights = (1.0 - weights[0], weights[0])
        col_weights = (1.0 - weights[1], weights[1])
        warped = jnp.zeros((channels, fine_rows, fine_cols), jnp.float32)
        for row_off in range(2):
            for col_off in range(2):
                flat_index = (anchor + row_off * stride + col_off).reshape(-1).astype(jnp.int32)
                picked = jnp.take(source_section, flat_index, axis=1).reshape(channels, fine_rows, fine_cols)
                warped = warped + (row_weights[row_off] * col_weights[col_off])[None] * picked.astype(jnp.float32)
        differ = own_map.astype(jnp.float32) - warped
        return jnp.mean(differ * differ, axis=0)

    return lax.map(single, (fine_own, framed, base_shift, bilinear_frac))


def edge_pull(displaced_vertex, edge_ends, live, stiffness):
    sections, edge_slots = stiffness.shape
    vertex_total = displaced_vertex.shape[2]
    start_ids = jnp.broadcast_to(edge_ends[:, 0][:, None, :], (sections, 2, edge_slots))
    end_ids = jnp.broadcast_to(edge_ends[:, 1][:, None, :], (sections, 2, edge_slots))
    spread_radius = jnp.take_along_axis(displaced_vertex, end_ids, axis=2) - jnp.take_along_axis(displaced_vertex, start_ids, axis=2)
    spring_tension = jnp.where(live, stiffness, 0.0)[:, None, :] * spread_radius

    def per_section(pull_one, start_one, end_one):
        gained = jax.ops.segment_sum(pull_one.T, start_one, num_segments=vertex_total)
        lost = jax.ops.segment_sum(pull_one.T, end_one, num_segments=vertex_total)
        return (gained - lost).T

    return jax.vmap(per_section)(spring_tension, edge_ends[:, 0], edge_ends[:, 1])


def reference(section_image, partner_row, base_shift, bilinear_frac, first_kernel, initial_conv_bias, second_kernel, second_bias, edge_ends, edge_count, stiffness):
    def one_row(row_id):
        own_image = lax.dynamic_index_in_dim(section_image, row_id, 0, keepdims=True)
        other_image = lax.dynamic_index_in_dim(section_image, partner_row[row_id], 0, keepdims=True)
        fine_own, coarse_own = encode_frame(jnp.pad(own_image, ((0, 0), (1, 1), (0, 0))), first_kernel, initial_conv_bias, second_kernel, second_bias)
        fine_other, coarse_other = encode_frame(jnp.pad(other_image, ((0, 0), (1, 1), (0, 0))), first_kernel, initial_conv_bias, second_kernel, second_bias)
        coarse_wide = jnp.pad(coarse_other, ((0, 0), (0, 0), (REACH, REACH), (REACH, REACH)))
        correlation = correlate(coarse_own, coarse_wide)
        fine_tall = jnp.pad(fine_other, ((0, 0), (0, 0), (WARP_MAX, WARP_MAX), (0, 0)))
        shift_one = lax.dynamic_index_in_dim(base_shift, row_id, 0, keepdims=True)
        frac_one = lax.dynamic_index_in_dim(bilinear_frac, row_id, 0, keepdims=True)
        mismatch = compare(fine_own, fine_tall, shift_one, frac_one)
        return correlation[0], mismatch[0]

    correlation, mismatch = lax.map(one_row, jnp.arange(NSEC, dtype=jnp.int32))
    anchors = base_shift[:, :, ::SPACING, ::SPACING].astype(jnp.float32) + bilinear_frac[:, :, ::SPACING, ::SPACING]
    displaced_vertex = anchors.reshape(NSEC, 2, -1)
    live_count = jnp.repeat(edge_count, E_DEV, axis=1)
    edge_slot = lax.broadcasted_iota(jnp.int32, (NSEC, EDGES), 1) % E_DEV
    live = edge_slot < live_count
    forces = edge_pull(displaced_vertex, edge_ends, live, stiffness)
    return correlation, mismatch, forces
```

```python
import functools

import jax
import jax.numpy as jnp
import numpy as np
from jax import lax
from jax.experimental import pallas as pl
from jax.experimental.pallas import tpu as pltpu
from jax.sharding import PartitionSpec as P

BF = jnp.bfloat16
F32 = jnp.float32
MESH = pl.DeviceIdType.MESH
BIG = -1e30
VMEM_BYTES = 56 * 1024 * 1024

PT = 132
QUADS = PT // 4


def _tables():
    lane = np.arange(128)
    a, b, xx, yy = lane // 64, (lane // 32) % 2, (lane // 16) % 2, lane % 16
    x4, y2 = 2 * xx + b, 2 * yy + a
    ep = np.zeros((4, 96, 6, 128), np.float32)
    for p in range(6):
        ep[x4, 2 * y2 + 15 + p, p, lane] = 1
    oa, ob, ox, oy = lane // 64, (lane // 32) % 2, (lane // 8) % 4, lane % 8
    x8, y1 = 2 * ox + ob, 2 * oy + oa
    eo = np.zeros((8, 64, 6, 128), np.float32)
    for p in range(6):
        eo[x8, 2 * y1 + 15 + p, p, lane] = 1
    wsel = np.zeros((2, 2, 2, 16, 112), np.float32)
    wconst = np.zeros((2, 2, 2, 1, 112), np.float32)
    for e in range(2):
        for ta in range(2):
            for tb in range(2):
                for u in range(4):
                    for v in range(4):
                        wsel[e, ta, tb, 4 * u + v, (u + 2 * ta) * 16 + 8 * e + 2 * tb + v] = 1
                wconst[e, ta, tb, 0, 96 + 4 * e + 2 * ta + tb] = BIG
    extra = np.zeros((3, 3, 16, 256), np.float32)
    cmask = np.zeros((3, 3, 8, 128), np.float32)
    for tk in range(3):
        for gk, g in enumerate((0, 1, QUADS - 1)):
            for half in range(2):
                for e in range(2):
                    for ta in range(2):
                        for tb in range(2):
                            col = 4 * (4 * g + 2 * half + e) - 8 + x4 + tb
                            row = y2 - 8 + ta
                            bad = (col < 0) | (col > 511)
                            if tk == 0:
                                bad = bad | (row < 0)
                            if tk == 2:
                                bad = bad | (row > 15)
                            extra[tk, gk, 4 * e + 2 * ta + tb, 128 * half : 128 * half + 128] = bad
            extra[tk, gk, 8:11] = 1
            ccol, crow = 8 * g - 4 + lane // 16, lane % 16 - 4
            bad = (ccol < 0) | (ccol > 255)
            if tk == 0:
                bad = bad | (crow < 0)
            if tk == 2:
                bad = bad | (crow > 7)
            cmask[tk, gk] = np.where(bad, BIG, 0.0)
    src = np.arange(1024)
    unflat = np.zeros((1024, 1024), np.float32)
    unflat[src, (src % 8) * 128 + src // 8] = 1
    l2 = np.arange(256)
    lx = 8 * (l2 // 128) + 2 * ((l2 // 8) % 4) + (l2 // 32) % 2
    ly = 2 * (l2 % 8) + (l2 // 64) % 2
    home = np.stack([ly + 8, lx + 4]).astype(np.float32)
    return dict(
        ep=ep.reshape(384, 768),
        eo=eo.reshape(512, 768),
        wsel=wsel.reshape(8, 16, 112),
        wconst=wconst.reshape(8, 1, 112),
        extra=extra,
        cmask=cmask,
        unflat=unflat,
        home=home,
    )


def _split3(x):
    hi = x.astype(BF)
    rest = x - hi.astype(F32)
    mid = rest.astype(BF)
    low = (rest - mid.astype(F32)).astype(BF)
    return hi, mid, low


def _dot(x, y):
    return jnp.dot(x, y, preferred_element_type=F32)


def _comm_kernel(
    pr_ref, img_ref, anch_ref, ends_ref, cnt_ref, stiff_ref,
    j_ref, i_ref, f_ref,
    rbuf, gbuf, pbuf, pstage, send_sem, recv_sem,
):
    sec = lax.axis_index("sec")
    tile = lax.axis_index("tile")
    back1 = lax.rem(sec + 15, 16)
    back2 = lax.rem(sec + 14, 16)
    fwd1 = lax.rem(sec + 1, 16)
    fwd2 = lax.rem(sec + 2, 16)
    peers = [lax.rem(tile + r, 8) for r in range(8)]

    barrier = pltpu.get_barrier_semaphore()
    for other in (back1, back2, fwd1, fwd2):
        pl.semaphore_signal(barrier, inc=1, device_id=(other, tile), device_id_type=MESH)
    for r in range(1, 8):
        pl.semaphore_signal(barrier, inc=1, device_id=(sec, peers[r]), device_id_type=MESH)
    pl.semaphore_wait(barrier, 11)

    def remote(src, dst, k, target):
        return pltpu.make_async_remote_copy(
            src_ref=src, dst_ref=dst, send_sem=send_sem.at[k], recv_sem=recv_sem.at[k],
            device_id=target, device_id_type=MESH,
        )

    near = remote(img_ref, rbuf.at[0], 0, (back1, tile))
    far = remote(img_ref, rbuf.at[1], 1, (back2, tile))
    far.start()
    near.start()
    down_tile = (sec, lax.rem(tile + 1, 8))
    up_tile = (sec, lax.rem(tile + 7, 8))
    own_down = remote(img_ref.at[:, 16:32], i_ref.at[:, 0:16], 2, down_tile)
    own_up = remote(img_ref.at[:, 0:16], i_ref.at[:, 48:64], 3, up_tile)
    has_down = tile < 7
    has_up = tile > 0
    pl.when(has_down)(own_down.start)
    pl.when(has_up)(own_up.start)
    anchor_sends = [remote(anch_ref, gbuf.at[r], 4 + r, (sec, peers[r])) for r in range(1, 8)]
    for c in anchor_sends:
        c.start()

    i_ref[:, 16:48, :] = img_ref[...]

    @pl.when(tile == 0)
    def _():
        i_ref[:, 0:16, :] = jnp.zeros((2, 16, 1024), BF)
        j_ref[:, 0:32, :] = jnp.zeros((2, 32, 1024), BF)

    @pl.when(tile == 7)
    def _():
        i_ref[:, 48:64, :] = jnp.zeros((2, 16, 1024), BF)
        j_ref[:, 64:96, :] = jnp.zeros((2, 32, 1024), BF)

    near.wait()
    far.wait()
    for s in range(2):
        p = pr_ref[s]
        which = jnp.where(lax.shift_right_logical(p, 1) == fwd1, 0, 1)
        slot = lax.bitwise_and(p, 1)
        j_ref[s, 32:64, :] = rbuf[which, slot]
    part_down = remote(j_ref.at[:, 32:64], j_ref.at[:, 0:32], 12, down_tile)
    part_up = remote(j_ref.at[:, 32:64], j_ref.at[:, 64:96], 13, up_tile)
    pl.when(has_down)(part_down.start)
    pl.when(has_up)(part_up.start)

    for c in anchor_sends:
        c.wait()
    disp = anch_ref[...]
    for r in range(1, 8):
        disp = disp + gbuf[r]
    vert = lax.broadcasted_iota(jnp.int32, (256, 256), 0)
    live = lax.broadcasted_iota(jnp.int32, (2, 256), 1) < cnt_ref[...]
    stiff = jnp.where(live, stiff_ref[...], 0.0)
    row_of = lax.broadcasted_iota(jnp.int32, (8, 256), 0)
    parts = jnp.concatenate(_split3(disp), axis=0)
    total = jnp.zeros((8, 256), F32)
    for s in range(2):
        table = (vert == ends_ref[s, 1:2, :]).astype(F32) - (vert == ends_ref[s, 0:1, :]).astype(F32)
        table = table.astype(BF)
        got = _dot(parts, table)
        spread = (got[16:24] + got[8:16]) + got[0:8]
        pull = stiff[s : s + 1, :] * spread
        back = lax.dot_general(
            jnp.concatenate(_split3(pull), axis=0), table, (((1,), (1,)), ((), ())),
            preferred_element_type=F32,
        )
        back = (back[16:24] + back[8:16]) + back[0:8]
        total = total - jnp.where(lax.shift_right_logical(row_of, 1) == s, back, 0.0)
    pstage[...] = total
    force_sends = [remote(pstage, pbuf.at[r], 14 + r, (sec, peers[r])) for r in range(1, 8)]
    for c in force_sends:
        c.start()
    for c in force_sends:
        c.wait()
    for r in range(1, 8):
        total = total + pbuf[r]
    turned = pltpu.roll(total, lax.rem(256 - 32 * tile, 256), 1)
    f_ref[...] = turned[:, 0:128]

    pl.when(has_down)(own_down.wait_send)
    pl.when(has_up)(own_up.wait_send)
    pl.when(has_up)(own_down.wait_recv)
    pl.when(has_down)(own_up.wait_recv)
    pl.when(has_down)(part_down.wait_send)
    pl.when(has_up)(part_up.wait_send)
    pl.when(has_up)(part_down.wait_recv)
    pl.when(has_down)(part_up.wait_recv)


def _exchange(partner_row, image, anchors, ends, count, stiffness):
    vm = pl.BlockSpec(memory_space=pltpu.VMEM)
    return pl.pallas_call(
        _comm_kernel,
        out_shape=(
            jax.ShapeDtypeStruct((2, 96, 1024), BF),
            jax.ShapeDtypeStruct((2, 64, 1024), BF),
            jax.ShapeDtypeStruct((8, 128), F32),
        ),
        in_specs=[pl.BlockSpec(memory_space=pltpu.SMEM)] + [vm] * 5,
        out_specs=(vm, vm, vm),
        scratch_shapes=[
            pltpu.VMEM((2, 2, 32, 1024), BF),
            pltpu.VMEM((8, 8, 256), F32),
            pltpu.VMEM((8, 8, 256), F32),
            pltpu.VMEM((8, 256), F32),
            pltpu.SemaphoreType.DMA((22,)),
            pltpu.SemaphoreType.DMA((22,)),
        ],
        compiler_params=pltpu.CompilerParams(
            collective_id=0, has_side_effects=True, vmem_limit_bytes=24 * 1024 * 1024
        ),
        name="exchange",
    )(partner_row, image, anchors, ends, count, stiffness)


def _work_kernel(
    tk_ref, j_ref, i_ref, sh_ref, fr_ref, w1_ref, b1_ref, w2_ref, b2_ref,
    ep_ref, eo_ref, wsel_ref, wconst_ref, extra_ref, cmask_ref, unflat_ref, home_ref,
    corr_ref, mis_ref,
    pad, qp, qo, p4, cpt, obuf, cbuf, wq,
):
    tk = tk_ref[0]
    lane = lax.broadcasted_iota(jnp.int32, (64, 112), 1)
    hi, mid, low = (x.astype(F32) for x in _split3(b1_ref[...]))
    base = (
        jnp.where(lane == 104, hi, 0.0) + jnp.where(lane == 105, mid, 0.0) + jnp.where(lane == 106, low, 0.0)
    )
    for m in range(8):
        wq[64 * m : 64 * m + 64, :] = (_dot(w1_ref[...], wsel_ref[m]) + base + wconst_ref[m]).astype(BF)

    lane128 = lax.broadcasted_iota(jnp.int32, (1, 128), 1)
    x_bit = [lax.bitwise_and(lax.shift_right_logical(lane128, 3 + k), 1) == 1 for k in range(4)]
    y_bit = [lax.bitwise_and(lax.shift_right_logical(lane128, k), 1) == 1 for k in range(3)]
    row16 = lax.broadcasted_iota(jnp.int32, (16, 256), 0)

    def section(s, carry):
        pad[0:64, 0:1024] = i_ref[s].astype(F32)
        pad[0:96, 1024:1152] = jnp.zeros((96, 128), F32)
        wide = pad[0:64, :]
        stack = jnp.concatenate(
            [pltpu.roll(wide, (1 - 2 * k) % 1152, 1)[:, 0:1024] for k in range(8)], axis=0
        )
        qo[...] = _dot(stack.T.astype(BF), eo_ref[...]).astype(BF)
        pad[0:96, 0:1024] = j_ref[s].astype(F32)
        wide = pad[...]
        stack = jnp.concatenate([pltpu.roll(wide, (17 - 2 * k) % 1152, 1) for k in range(4)], axis=0)
        qp[...] = _dot(stack.T.astype(BF), ep_ref[...])[0:1056].astype(BF)

        def partner(g, carry):
            r0 = pl.multiple_of(32 * g, 32)
            left = qp[pl.ds(r0, 16), :]
            right = qp[pl.ds(r0 + 16, 16), :]
            kind = jnp.where(g == 0, 0, jnp.where(g == QUADS - 1, 2, 1))
            patches = jnp.concatenate(
                [
                    jnp.concatenate([left[:, 128 * p : 128 * p + 128], right[:, 128 * p : 128 * p + 128]], axis=1)
                    for p in range(6)
                ]
                + [extra_ref[tk, kind]],
                axis=0,
            )
            got = jnp.maximum(_dot(wq[...], patches).astype(BF), 0)
            l0 = pl.multiple_of(512 * g, 512)
            quad = jnp.concatenate(
                [got[0:256, 0:128], got[256:512, 0:128], got[0:256, 128:256], got[256:512, 128:256]], axis=1
            )
            p4[:, pl.ds(l0, 512)] = quad
            pre = _dot(w2_ref[...], quad)
            pre = jnp.concatenate([pre[:, 128 * k : 128 * k + 32] for k in range(4)], axis=1)
            coarse = jnp.maximum(pre + b2_ref[...] + cmask_ref[tk, kind][0:1, :], 0.0)
            coarse = coarse.astype(BF).astype(F32)
            cpt[pl.ds(pl.multiple_of(128 * g, 128), 128), 0:64] = coarse.T.astype(BF)
            return carry

        lax.fori_loop(0, QUADS, partner, 0)

        def block(c, carry):
            coarse_parts = []
            for half in range(2):
                b = 2 * c + half
                r0 = pl.multiple_of(32 * b, 32)
                left = qo[pl.ds(r0, 16), :]
                right = qo[pl.ds(r0 + 16, 16), :]
                patches = jnp.concatenate(
                    [
                        jnp.concatenate([left[:, 128 * p : 128 * p + 128], right[:, 128 * p : 128 * p + 128]], axis=1)
                        for p in range(6)
                    ]
                    + [extra_ref[1, 1]],
                    axis=0,
                )
                own4 = jnp.maximum(_dot(wq[0:256, :], patches).astype(BF), 0)
                own = own4[0:64, :].astype(F32)
                pre = _dot(w2_ref[...], own4)
                coarse_parts += [pre[:, 0:32], pre[:, 128:160]]

                row = home_ref[0:1, :] + sh_ref[s, 0, pl.ds(b, 1), :].astype(F32)
                col = home_ref[1:2, :] + sh_ref[s, 1, pl.ds(b, 1), :].astype(F32)
                fy = fr_ref[s, 0, pl.ds(b, 1), :]
                fx = fr_ref[s, 1, pl.ds(b, 1), :]
                row = jnp.broadcast_to(row.astype(jnp.int32), (16, 256))
                col = jnp.broadcast_to(col, (16, 256)).astype(BF)
                oy = [(row == 2 * row16 + a).astype(F32).astype(BF) for a in range(2)]
                zero = jnp.zeros((16, 256), BF)
                picks = []
                for k in range(6):
                    hit = {}
                    for bb in range(2):
                        for xx in range(2):
                            hit[bb, xx] = col == float(4 * k + 2 * xx + bb)
                    for a in range(2):
                        for bb in range(2):
                            for xx in range(2):
                                picks.append(jnp.where(hit[bb, xx], oy[a], zero))
                choose = jnp.concatenate(picks, axis=0)
                l0 = pl.multiple_of(512 * b + 128, 128)
                taps = _dot(p4[:, pl.ds(l0, 768)], choose)
                gy, gx = 1.0 - fy, 1.0 - fx
                warped = (
                    (gy * gx) * taps[0:64] + (gy * fx) * taps[64:128]
                    + (fy * gx) * taps[128:192] + (fy * fx) * taps[192:256]
                )
                differ = own - warped
                mis_ref[s, pl.ds(b, 1), :] = jnp.sum(differ * differ, axis=0, keepdims=True) * (1.0 / 64)

            coarse = jnp.maximum(jnp.concatenate(coarse_parts, axis=1) + b2_ref[...], 0.0).astype(BF)
            near = cpt[pl.ds(pl.multiple_of(256 * c, 256), 384), 0:64]
            gram = _dot(near, coarse).reshape(24, 16, 128)
            for k, keep in ((3, 16), (2, 12), (1, 10), (0, 9)):
                step = 1 << k
                gram = jnp.where(x_bit[k][None], gram[step : step + keep], gram[0:keep])
            gram = gram.reshape(144, 128)
            cols = []
            for j in range(9):
                v = gram[16 * j : 16 * j + 16]
                for k in (2, 1, 0):
                    v = jnp.where(y_bit[k], pltpu.roll(v, 16 - (1 << k), 0), v)
                cols.append(v)
            gram = jnp.concatenate(cols, axis=0) * (1.0 / 64)
            obuf[:, pl.ds(pl.multiple_of(128 * c, 128), 128)] = gram.astype(BF)
            return carry

        lax.fori_loop(0, 16, block, 0)

        for h in range(2):
            flat = _dot(obuf[:, 1024 * h : 1024 * h + 1024], unflat_ref[...])
            for j in range(9):
                for y in range(8):
                    cbuf[h, pl.ds(8 * j + y, 9, stride=72), :] = flat[16 * j : 16 * j + 9, 128 * y : 128 * y + 128]
        for h in range(2):
            corr_ref[s, :, :, 128 * h : 128 * h + 128] = cbuf[h].reshape(81, 8, 128).astype(BF)
        return carry

    lax.fori_loop(0, 2, section, 0)


def _work(tile_kind, j, i, shift_px, frac_px, w1, b1, w2, b2, interpret=False):
    t = _tables()
    vm = pl.BlockSpec(memory_space=pltpu.VMEM)
    consts = [
        jnp.asarray(t["ep"], BF), jnp.asarray(t["eo"], BF), jnp.asarray(t["wsel"], BF),
        jnp.asarray(t["wconst"], F32), jnp.asarray(t["extra"], BF), jnp.asarray(t["cmask"], F32),
        jnp.asarray(t["unflat"], BF), jnp.asarray(t["home"], F32),
    ]
    return pl.pallas_call(
        _work_kernel,
        out_shape=(
            jax.ShapeDtypeStruct((2, 81, 8, 256), BF),
            jax.ShapeDtypeStruct((2, 32, 256), F32),
        ),
        in_specs=[pl.BlockSpec(memory_space=pltpu.SMEM)] + [vm] * 16,
        out_specs=(vm, vm),
        scratch_shapes=[
            pltpu.VMEM((96, 1152), F32),
            pltpu.VMEM((1056, 768), BF),
            pltpu.VMEM((1024, 768), BF),
            pltpu.VMEM((256, PT * 128), BF),
            pltpu.VMEM((PT * 32, 128), BF),
            pltpu.VMEM((144, 2048), BF),
            pltpu.VMEM((2, 648, 128), F32),
            pltpu.VMEM((512, 112), BF),
        ],
        compiler_params=pltpu.CompilerParams(vmem_limit_bytes=VMEM_BYTES),
        interpret=interpret,
        name="work",
    )(tile_kind, j, i, shift_px, frac_px, w1, b1, w2, b2, *consts)


def _to_px(x):
    x = x.reshape(2, 2, 8, 2, 32, 2, 4, 2)
    return x.transpose(0, 1, 4, 5, 3, 7, 6, 2).reshape(2, 2, 32, 256)


def _from_px(x):
    x = x.reshape(2, 32, 2, 2, 2, 4, 8)
    return x.transpose(0, 6, 3, 1, 2, 5, 4).reshape(2, 16, 512)


def local(
    section_image, partner_row, base_shift, bilinear_frac, first_kernel, initial_conv_bias,
    second_kernel, second_bias, edge_ends, edge_count, stiffness,
):
    tile = lax.axis_index("tile")
    anchors = base_shift[:, :, 0, ::16].astype(F32) + bilinear_frac[:, :, 0, ::16]
    anchors = jnp.pad(anchors.reshape(4, 32), ((0, 4), (0, 224)))
    lanes = lax.broadcasted_iota(jnp.int32, (8, 256), 1)
    anchors = jnp.where(lanes // 32 == tile, jnp.tile(anchors[:, 0:32], (1, 8)), 0.0)
    j, i, force = _exchange(partner_row, section_image, anchors, edge_ends, edge_count, stiffness)
    kind = jnp.where(tile == 0, 0, jnp.where(tile == 7, 2, 1)).astype(jnp.int32).reshape(1)
    corr, mis = _work(
        kind, j, i, _to_px(base_shift), _to_px(bilinear_frac), first_kernel,
        initial_conv_bias.reshape(64, 1), second_kernel, second_bias.reshape(64, 1),
    )
    return corr, _from_px(mis), force[0:4, 0:32].reshape(2, 2, 32)


def solution(mesh):
    in_specs = (
        P("sec", "tile", None), P("sec"), P("sec", None, "tile", None), P("sec", None, "tile", None),
        P(), P(), P(), P(), P("sec", None, "tile"), P("sec", "tile"), P("sec", "tile"),
    )
    out_specs = (P("sec", None, "tile", None), P("sec", "tile", None), P("sec", None, "tile"))
    return jax.shard_map(local, mesh=mesh, in_specs=in_specs, out_specs=out_specs, check_vma=False)
```

```python
import functools

import jax
import jax.numpy as jnp
import numpy as np
from jax import lax
from jax.experimental import pallas as pl
from jax.experimental.pallas import tpu as pltpu
from jax.sharding import PartitionSpec as P

BF = jnp.bfloat16
F32 = jnp.float32
MESH = pl.DeviceIdType.MESH
BIG = -1e30
VMEM_BYTES = 56 * 1024 * 1024

PT = 132
QUADS = PT // 4


def _tables():
    lane = np.arange(128)
    a, b, xx, yy = lane // 64, (lane // 32) % 2, (lane // 16) % 2, lane % 16
    x4, y2 = 2 * xx + b, 2 * yy + a
    ep = np.zeros((4, 96, 6, 128), np.float32)
    for p in range(6):
        ep[x4, 2 * y2 + 15 + p, p, lane] = 1
    oa, ob, ox, oy = lane // 64, (lane // 32) % 2, (lane // 8) % 4, lane % 8
    x8, y1 = 2 * ox + ob, 2 * oy + oa
    eo = np.zeros((8, 64, 6, 128), np.float32)
    for p in range(6):
        eo[x8, 2 * y1 + 15 + p, p, lane] = 1
    wsel = np.zeros((2, 2, 2, 16, 112), np.float32)
    wconst = np.zeros((2, 2, 2, 1, 112), np.float32)
    for e in range(2):
        for ta in range(2):
            for tb in range(2):
                for u in range(4):
                    for v in range(4):
                        wsel[e, ta, tb, 4 * u + v, (u + 2 * ta) * 16 + 8 * e + 2 * tb + v] = 1
                wconst[e, ta, tb, 0, 96 + 4 * e + 2 * ta + tb] = BIG
    extra = np.zeros((3, 3, 16, 256), np.float32)
    cmask = np.zeros((3, 3, 8, 128), np.float32)
    for tk in range(3):
        for gk, g in enumerate((0, 1, QUADS - 1)):
            for half in range(2):
                for e in range(2):
                    for ta in range(2):
                        for tb in range(2):
                            col = 4 * (4 * g + 2 * half + e) - 8 + x4 + tb
                            row = y2 - 8 + ta
                            bad = (col < 0) | (col > 511)
                            if tk == 0:
                                bad = bad | (row < 0)
                            if tk == 2:
                                bad = bad | (row > 15)
                            extra[tk, gk, 4 * e + 2 * ta + tb, 128 * half : 128 * half + 128] = bad
            extra[tk, gk, 8:11] = 1
            ccol, crow = 8 * g - 4 + lane // 16, lane % 16 - 4
            bad = (ccol < 0) | (ccol > 255)
            if tk == 0:
                bad = bad | (crow < 0)
            if tk == 2:
                bad = bad | (crow > 7)
            cmask[tk, gk] = np.where(bad, BIG, 0.0)
    src = np.arange(1024)
    unflat = np.zeros((1024, 1024), np.float32)
    unflat[src, (src % 8) * 128 + src // 8] = 1
    l2 = np.arange(256)
    lx = 8 * (l2 // 128) + 2 * ((l2 // 8) % 4) + (l2 // 32) % 2
    ly = 2 * (l2 % 8) + (l2 // 64) % 2
    perm = np.zeros((256, 256), np.float32)
    perm[16 * lx + ly, l2] = 1
    home = np.stack([ly + 8, lx + 4]).astype(np.float32)
    return dict(
        ep=ep.reshape(384, 768),
        eo=eo.reshape(512, 768),
        wsel=wsel.reshape(8, 16, 112),
        wconst=wconst.reshape(8, 1, 112),
        extra=extra,
        cmask=cmask,
        unflat=unflat,
        home=home,
        perm=perm,
    )


def _split3(x):
    hi = x.astype(BF)
    rest = x - hi.astype(F32)
    mid = rest.astype(BF)
    low = (rest - mid.astype(F32)).astype(BF)
    return hi, mid, low


def _dot(x, y):
    return jnp.dot(x, y, preferred_element_type=F32)


def _comm_kernel(
    pr_ref, img_ref, anch_ref, ends_ref, cnt_ref, stiff_ref,
    j_ref, i_ref, f_ref,
    rbuf, gbuf, pbuf, pstage, send_sem, recv_sem,
):
    sec = lax.axis_index("sec")
    tile = lax.axis_index("tile")
    back1 = lax.rem(sec + 15, 16)
    back2 = lax.rem(sec + 14, 16)
    fwd1 = lax.rem(sec + 1, 16)
    fwd2 = lax.rem(sec + 2, 16)
    peers = [lax.rem(tile + r, 8) for r in range(8)]

    barrier = pltpu.get_barrier_semaphore()
    for other in (back1, back2, fwd1, fwd2):
        pl.semaphore_signal(barrier, inc=1, device_id=(other, tile), device_id_type=MESH)
    for r in range(1, 8):
        pl.semaphore_signal(barrier, inc=1, device_id=(sec, peers[r]), device_id_type=MESH)
    pl.semaphore_wait(barrier, 11)

    def remote(src, dst, k, target):
        return pltpu.make_async_remote_copy(
            src_ref=src, dst_ref=dst, send_sem=send_sem.at[k], recv_sem=recv_sem.at[k],
            device_id=target, device_id_type=MESH,
        )

    near = remote(img_ref, rbuf.at[0], 0, (back1, tile))
    far = remote(img_ref, rbuf.at[1], 1, (back2, tile))
    far.start()
    near.start()
    down_tile = (sec, lax.rem(tile + 1, 8))
    up_tile = (sec, lax.rem(tile + 7, 8))
    own_down = remote(img_ref.at[:, 16:32], i_ref.at[:, 0:16], 2, down_tile)
    own_up = remote(img_ref.at[:, 0:16], i_ref.at[:, 48:64], 3, up_tile)
    has_down = tile < 7
    has_up = tile > 0
    pl.when(has_down)(own_down.start)
    pl.when(has_up)(own_up.start)
    anchor_sends = [remote(anch_ref, gbuf.at[r], 4 + r, (sec, peers[r])) for r in range(1, 8)]
    for c in anchor_sends:
        c.start()

    i_ref[:, 16:48, :] = img_ref[...]

    @pl.when(tile == 0)
    def _():
        i_ref[:, 0:16, :] = jnp.zeros((2, 16, 1024), BF)
        j_ref[:, 0:32, :] = jnp.zeros((2, 32, 1024), BF)

    @pl.when(tile == 7)
    def _():
        i_ref[:, 48:64, :] = jnp.zeros((2, 16, 1024), BF)
        j_ref[:, 64:96, :] = jnp.zeros((2, 32, 1024), BF)

    near.wait()
    far.wait()
    for s in range(2):
        p = pr_ref[s]
        which = jnp.where(lax.shift_right_logical(p, 1) == fwd1, 0, 1)
        slot = lax.bitwise_and(p, 1)
        j_ref[s, 32:64, :] = rbuf[which, slot]
    part_down = remote(j_ref.at[:, 32:64], j_ref.at[:, 0:32], 12, down_tile)
    part_up = remote(j_ref.at[:, 32:64], j_ref.at[:, 64:96], 13, up_tile)
    pl.when(has_down)(part_down.start)
    pl.when(has_up)(part_up.start)

    for c in anchor_sends:
        c.wait()
    disp = anch_ref[...]
    for r in range(1, 8):
        disp = disp + gbuf[r]
    vert = lax.broadcasted_iota(jnp.int32, (256, 256), 0)
    live = lax.broadcasted_iota(jnp.int32, (2, 256), 1) < cnt_ref[...]
    stiff = jnp.where(live, stiff_ref[...], 0.0)
    row_of = lax.broadcasted_iota(jnp.int32, (8, 256), 0)
    parts = jnp.concatenate(_split3(disp), axis=0)
    total = jnp.zeros((8, 256), F32)
    for s in range(2):
        table = (vert == ends_ref[s, 1:2, :]).astype(F32) - (vert == ends_ref[s, 0:1, :]).astype(F32)
        table = table.astype(BF)
        got = _dot(parts, table)
        spread = (got[16:24] + got[8:16]) + got[0:8]
        pull = stiff[s : s + 1, :] * spread
        back = lax.dot_general(
            jnp.concatenate(_split3(pull), axis=0), table, (((1,), (1,)), ((), ())),
            preferred_element_type=F32,
        )
        back = (back[16:24] + back[8:16]) + back[0:8]
        total = total - jnp.where(lax.shift_right_logical(row_of, 1) == s, back, 0.0)
    pstage[...] = total
    force_sends = [remote(pstage, pbuf.at[r], 14 + r, (sec, peers[r])) for r in range(1, 8)]
    for c in force_sends:
        c.start()
    for c in force_sends:
        c.wait()
    for r in range(1, 8):
        total = total + pbuf[r]
    turned = pltpu.roll(total, lax.rem(256 - 32 * tile, 256), 1)
    f_ref[...] = turned[:, 0:128]

    pl.when(has_down)(own_down.wait_send)
    pl.when(has_up)(own_up.wait_send)
    pl.when(has_up)(own_down.wait_recv)
    pl.when(has_down)(own_up.wait_recv)
    pl.when(has_down)(part_down.wait_send)
    pl.when(has_up)(part_up.wait_send)
    pl.when(has_up)(part_down.wait_recv)
    pl.when(has_down)(part_up.wait_recv)


def _exchange(partner_row, image, anchors, ends, count, stiffness):
    vm = pl.BlockSpec(memory_space=pltpu.VMEM)
    return pl.pallas_call(
        _comm_kernel,
        out_shape=(
            jax.ShapeDtypeStruct((2, 96, 1024), BF),
            jax.ShapeDtypeStruct((2, 64, 1024), BF),
            jax.ShapeDtypeStruct((8, 128), F32),
        ),
        in_specs=[pl.BlockSpec(memory_space=pltpu.SMEM)] + [vm] * 5,
        out_specs=(vm, vm, vm),
        scratch_shapes=[
            pltpu.VMEM((2, 2, 32, 1024), BF),
            pltpu.VMEM((8, 8, 256), F32),
            pltpu.VMEM((8, 8, 256), F32),
            pltpu.VMEM((8, 256), F32),
            pltpu.SemaphoreType.DMA((22,)),
            pltpu.SemaphoreType.DMA((22,)),
        ],
        compiler_params=pltpu.CompilerParams(
            collective_id=0, has_side_effects=True, vmem_limit_bytes=24 * 1024 * 1024
        ),
        name="exchange",
    )(partner_row, image, anchors, ends, count, stiffness)


def _work_kernel(
    tk_ref, j_ref, i_ref, sh_ref, fr_ref, w1_ref, b1_ref, w2_ref, b2_ref,
    ep_ref, eo_ref, wsel_ref, wconst_ref, extra_ref, cmask_ref, unflat_ref, home_ref, perm_ref,
    corr_ref, mis_ref,
    pad, qp, qo, p4, cpt, obuf, cbuf, wq, tbuf, px, mpx,
):
    tk = tk_ref[0]
    lane = lax.broadcasted_iota(jnp.int32, (64, 112), 1)
    hi, mid, low = (x.astype(F32) for x in _split3(b1_ref[...]))
    base = (
        jnp.where(lane == 104, hi, 0.0) + jnp.where(lane == 105, mid, 0.0) + jnp.where(lane == 106, low, 0.0)
    )
    for m in range(8):
        wq[64 * m : 64 * m + 64, :] = (_dot(w1_ref[...], wsel_ref[m]) + base + wconst_ref[m]).astype(BF)

    lane128 = lax.broadcasted_iota(jnp.int32, (1, 128), 1)
    x_bit = [lax.bitwise_and(lax.shift_right_logical(lane128, 3 + k), 1) == 1 for k in range(4)]
    y_bit = [lax.bitwise_and(lax.shift_right_logical(lane128, k), 1) == 1 for k in range(3)]
    row16 = lax.broadcasted_iota(jnp.int32, (16, 256), 0)

    def section(s, carry):
        planes = [sh_ref[s, k].astype(F32) for k in range(2)] + [fr_ref[s, k] for k in range(2)]
        tbuf[:, 0:64] = jnp.concatenate(planes, axis=0).T
        runs = [tbuf[pl.ds(x, 32, stride=16), :] for x in range(16)]
        planes = [jnp.concatenate([r[:, 16 * k : 16 * k + 16] for r in runs], axis=1) for k in range(4)]
        parts = [planes[0].astype(BF), planes[1].astype(BF), *_split3(planes[2]), *_split3(planes[3])]
        got = _dot(jnp.concatenate(parts, axis=0), perm_ref[...])
        px[0] = got[0:32] + home_ref[0:1, :]
        px[1] = got[32:64] + home_ref[1:2, :]
        px[2] = (got[128:160] + got[96:128]) + got[64:96]
        px[3] = (got[224:256] + got[192:224]) + got[160:192]

        pad[0:64, 0:1024] = i_ref[s].astype(F32)
        pad[0:96, 1024:1152] = jnp.zeros((96, 128), F32)
        wide = pad[0:64, :]
        stack = jnp.concatenate(
            [pltpu.roll(wide, (1 - 2 * k) % 1152, 1)[:, 0:1024] for k in range(8)], axis=0
        )
        qo[...] = _dot(stack.T.astype(BF), eo_ref[...]).astype(BF)
        pad[0:96, 0:1024] = j_ref[s].astype(F32)
        wide = pad[...]
        stack = jnp.concatenate([pltpu.roll(wide, (17 - 2 * k) % 1152, 1) for k in range(4)], axis=0)
        qp[...] = _dot(stack.T.astype(BF), ep_ref[...])[0:1056].astype(BF)

        def partner(g, carry):
            r0 = pl.multiple_of(32 * g, 32)
            left = qp[pl.ds(r0, 16), :]
            right = qp[pl.ds(r0 + 16, 16), :]
            kind = jnp.where(g == 0, 0, jnp.where(g == QUADS - 1, 2, 1))
            patches = jnp.concatenate(
                [
                    jnp.concatenate([left[:, 128 * p : 128 * p + 128], right[:, 128 * p : 128 * p + 128]], axis=1)
                    for p in range(6)
                ]
                + [extra_ref[tk, kind]],
                axis=0,
            )
            got = jnp.maximum(_dot(wq[...], patches).astype(BF), 0)
            l0 = pl.multiple_of(512 * g, 512)
            quad = jnp.concatenate(
                [got[0:256, 0:128], got[256:512, 0:128], got[0:256, 128:256], got[256:512, 128:256]], axis=1
            )
            p4[:, pl.ds(l0, 512)] = quad
            return carry

        lax.fori_loop(0, QUADS, partner, 0, unroll=3)

        def coarsen(q, count):
            tiles = p4[:, pl.ds(pl.multiple_of(512 * q, 512), 512 * count)]
            tiles = jnp.concatenate([tiles[:, 128 * k : 128 * k + 32] for k in range(4 * count)], axis=1)
            pre = _dot(w2_ref[...], tiles) + b2_ref[...]
            for n in range(count):
                kind = jnp.where(q + n == 0, 0, jnp.where(q + n == QUADS - 1, 2, 1))
                coarse = jnp.maximum(pre[:, 128 * n : 128 * n + 128] + cmask_ref[tk, kind][0:1, :], 0.0)
                coarse = coarse.astype(BF).astype(F32)
                cpt[pl.ds(pl.multiple_of(128 * (q + n), 128), 128), 0:64] = coarse.T.astype(BF)

        def coarsen_pair(g, carry):
            coarsen(2 * g, 2)
            return carry

        lax.fori_loop(0, QUADS // 2, coarsen_pair, 0, unroll=2)
        coarsen(QUADS - 1, 1)

        def block(c, carry):
            coarse_parts = []
            for half in range(2):
                b = 2 * c + half
                r0 = pl.multiple_of(32 * b, 32)
                left = qo[pl.ds(r0, 16), :]
                right = qo[pl.ds(r0 + 16, 16), :]
                patches = jnp.concatenate(
                    [
                        jnp.concatenate([left[:, 128 * p : 128 * p + 128], right[:, 128 * p : 128 * p + 128]], axis=1)
                        for p in range(6)
                    ]
                    + [extra_ref[1, 1]],
                    axis=0,
                )
                own4 = jnp.maximum(_dot(wq[0:256, :], patches).astype(BF), 0)
                own = own4[0:64, :].astype(F32)
                pre = _dot(w2_ref[...], own4)
                coarse_parts += [pre[:, 0:32], pre[:, 128:160]]

                row = px[0, pl.ds(b, 1), :]
                col = px[1, pl.ds(b, 1), :]
                fy = px[2, pl.ds(b, 1), :]
                fx = px[3, pl.ds(b, 1), :]
                row = jnp.broadcast_to(row.astype(jnp.int32), (16, 256))
                col = jnp.broadcast_to(col, (16, 256)).astype(BF)
                oy = [(row == 2 * row16 + a).astype(F32).astype(BF) for a in range(2)]
                zero = jnp.zeros((16, 256), BF)
                picks = []
                for k in range(6):
                    hit = {}
                    for bb in range(2):
                        for xx in range(2):
                            hit[bb, xx] = col == float(4 * k + 2 * xx + bb)
                    for a in range(2):
                        for bb in range(2):
                            for xx in range(2):
                                picks.append(jnp.where(hit[bb, xx], oy[a], zero))
                choose = jnp.concatenate(picks, axis=0)
                l0 = pl.multiple_of(512 * b + 128, 128)
                taps = _dot(p4[:, pl.ds(l0, 768)], choose)
                gy, gx = 1.0 - fy, 1.0 - fx
                warped = (
                    (gy * gx) * taps[0:64] + (gy * fx) * taps[64:128]
                    + (fy * gx) * taps[128:192] + (fy * fx) * taps[192:256]
                )
                differ = own - warped
                mpx[pl.ds(b, 1), :] = jnp.sum(differ * differ, axis=0, keepdims=True) * (1.0 / 64)

            coarse = jnp.maximum(jnp.concatenate(coarse_parts, axis=1) + b2_ref[...], 0.0).astype(BF)
            near = cpt[pl.ds(pl.multiple_of(256 * c, 256), 384), 0:64]
            gram = _dot(near, coarse).reshape(24, 16, 128)
            for k, keep in ((3, 16), (2, 12), (1, 10), (0, 9)):
                step = 1 << k
                gram = jnp.where(x_bit[k][None], gram[step : step + keep], gram[0:keep])
            gram = gram.reshape(144, 128)
            cols = []
            for j in range(9):
                v = gram[16 * j : 16 * j + 16]
                for k in (2, 1, 0):
                    v = jnp.where(y_bit[k], pltpu.roll(v, 16 - (1 << k), 0), v)
                cols.append(v)
            gram = jnp.concatenate(cols, axis=0) * (1.0 / 64)
            obuf[:, pl.ds(pl.multiple_of(128 * c, 128), 128)] = gram.astype(BF)
            return carry

        lax.fori_loop(0, 16, block, 0)

        got = lax.dot_general(
            jnp.concatenate(_split3(mpx[...]), axis=0), perm_ref[...], (((1,), (1,)), ((), ())),
            preferred_element_type=F32,
        )
        got = (got[64:96] + got[32:64]) + got[0:32]
        for x in range(16):
            tbuf[pl.ds(x, 32, stride=16), 0:16] = got[:, 16 * x : 16 * x + 16]
        mis_ref[s] = tbuf[...].T[0:16, :]

        for h in range(2):
            flat = _dot(obuf[:, 1024 * h : 1024 * h + 1024], unflat_ref[...])
            for j in range(9):
                for y in range(8):
                    cbuf[h, pl.ds(8 * j + y, 9, stride=72), :] = flat[16 * j : 16 * j + 9, 128 * y : 128 * y + 128]
        for h in range(2):
            corr_ref[s, :, :, 128 * h : 128 * h + 128] = cbuf[h].reshape(81, 8, 128).astype(BF)
        return carry

    lax.fori_loop(0, 2, section, 0)


def _work(tile_kind, j, i, shift, frac, w1, b1, w2, b2, interpret=False):
    t = _tables()
    vm = pl.BlockSpec(memory_space=pltpu.VMEM)
    consts = [
        jnp.asarray(t["ep"], BF), jnp.asarray(t["eo"], BF), jnp.asarray(t["wsel"], BF),
        jnp.asarray(t["wconst"], F32), jnp.asarray(t["extra"], BF), jnp.asarray(t["cmask"], F32),
        jnp.asarray(t["unflat"], BF), jnp.asarray(t["home"], F32),
        jnp.asarray(t["perm"], BF),
    ]
    return pl.pallas_call(
        _work_kernel,
        out_shape=(
            jax.ShapeDtypeStruct((2, 81, 8, 256), BF),
            jax.ShapeDtypeStruct((2, 16, 512), F32),
        ),
        in_specs=[pl.BlockSpec(memory_space=pltpu.SMEM)] + [vm] * 17,
        out_specs=(vm, vm),
        scratch_shapes=[
            pltpu.VMEM((96, 1152), F32),
            pltpu.VMEM((1056, 768), BF),
            pltpu.VMEM((1024, 768), BF),
            pltpu.VMEM((256, PT * 128), BF),
            pltpu.VMEM((PT * 32, 128), BF),
            pltpu.VMEM((144, 2048), BF),
            pltpu.VMEM((2, 648, 128), F32),
            pltpu.VMEM((512, 112), BF),
            pltpu.VMEM((512, 128), F32),
            pltpu.VMEM((4, 32, 256), F32),
            pltpu.VMEM((32, 256), F32),
        ],
        compiler_params=pltpu.CompilerParams(vmem_limit_bytes=VMEM_BYTES),
        interpret=interpret,
        name="work",
    )(tile_kind, j, i, shift, frac, w1, b1, w2, b2, *consts)


def local(
    section_image, partner_row, base_shift, bilinear_frac, first_kernel, initial_conv_bias,
    second_kernel, second_bias, edge_ends, edge_count, stiffness,
):
    tile = lax.axis_index("tile")
    anchors = base_shift[:, :, 0, ::16].astype(F32) + bilinear_frac[:, :, 0, ::16]
    anchors = jnp.pad(anchors.reshape(4, 32), ((0, 4), (0, 224)))
    lanes = lax.broadcasted_iota(jnp.int32, (8, 256), 1)
    anchors = jnp.where(lanes // 32 == tile, jnp.tile(anchors[:, 0:32], (1, 8)), 0.0)
    j, i, force = _exchange(partner_row, section_image, anchors, edge_ends, edge_count, stiffness)
    kind = jnp.where(tile == 0, 0, jnp.where(tile == 7, 2, 1)).astype(jnp.int32).reshape(1)
    corr, mis = _work(
        kind, j, i, base_shift, bilinear_frac, first_kernel,
        initial_conv_bias.reshape(64, 1), second_kernel, second_bias.reshape(64, 1),
    )
    return corr, mis, force[0:4, 0:32].reshape(2, 2, 32)


def solution(mesh):
    in_specs = (
        P("sec", "tile", None), P("sec"), P("sec", None, "tile", None), P("sec", None, "tile", None),
        P(), P(), P(), P(), P("sec", None, "tile"), P("sec", "tile"), P("sec", "tile"),
    )
    out_specs = (P("sec", None, "tile", None), P("sec", "tile", None), P("sec", None, "tile"))
    return jax.shard_map(local, mesh=mesh, in_specs=in_specs, out_specs=out_specs, check_vma=False)
```

```python
import jax
import jax.numpy as jnp
import numpy as np
from jax import lax
from jax.experimental import pallas as pl
from jax.experimental.pallas import tpu as pltpu
from jax.sharding import PartitionSpec as P

BF = jnp.bfloat16
F32 = jnp.float32
MESH = pl.DeviceIdType.MESH
BIG = -1e30
VMEM_BYTES = 56 * 1024 * 1024

PT = 132
QUADS = PT // 4


def _tables():
    lane = np.arange(128)
    a, b, xx, yy = lane // 64, (lane // 32) % 2, (lane // 16) % 2, lane % 16
    x4, y2 = 2 * xx + b, 2 * yy + a
    ep = np.zeros((4, 96, 6, 128), np.float32)
    for p in range(6):
        ep[x4, 2 * y2 + 15 + p, p, lane] = 1
    oa, ob, ox, oy = lane // 64, (lane // 32) % 2, (lane // 8) % 4, lane % 8
    x8, y1 = 2 * ox + ob, 2 * oy + oa
    eo = np.zeros((8, 64, 6, 128), np.float32)
    for p in range(6):
        eo[x8, 2 * y1 + 15 + p, p, lane] = 1
    wsel = np.zeros((2, 2, 2, 16, 112), np.float32)
    wconst = np.zeros((2, 2, 2, 1, 112), np.float32)
    for e in range(2):
        for ta in range(2):
            for tb in range(2):
                for u in range(4):
                    for v in range(4):
                        wsel[e, ta, tb, 4 * u + v, (u + 2 * ta) * 16 + 8 * e + 2 * tb + v] = 1
                wconst[e, ta, tb, 0, 96 + 4 * e + 2 * ta + tb] = BIG
    extra = np.zeros((3, 3, 16, 256), np.float32)
    cmask = np.zeros((3, 3, 8, 128), np.float32)
    for tk in range(3):
        for gk, g in enumerate((0, 1, QUADS - 1)):
            for half in range(2):
                for e in range(2):
                    for ta in range(2):
                        for tb in range(2):
                            col = 4 * (4 * g + 2 * half + e) - 8 + x4 + tb
                            row = y2 - 8 + ta
                            bad = (col < 0) | (col > 511)
                            if tk == 0:
                                bad = bad | (row < 0)
                            if tk == 2:
                                bad = bad | (row > 15)
                            extra[tk, gk, 4 * e + 2 * ta + tb, 128 * half : 128 * half + 128] = bad
            extra[tk, gk, 8:11] = 1
            ccol, crow = 8 * g - 4 + lane // 16, lane % 16 - 4
            bad = (ccol < 0) | (ccol > 255)
            if tk == 0:
                bad = bad | (crow < 0)
            if tk == 2:
                bad = bad | (crow > 7)
            cmask[tk, gk] = np.where(bad, BIG, 0.0)
    src = np.arange(1024)
    unflat = np.zeros((1024, 1024), np.float32)
    unflat[src, (src % 8) * 128 + src // 8] = 1
    l2 = np.arange(256)
    lx = 8 * (l2 // 128) + 2 * ((l2 // 8) % 4) + (l2 // 32) % 2
    ly = 2 * (l2 % 8) + (l2 // 64) % 2
    perm = np.zeros((256, 256), np.float32)
    perm[16 * lx + ly, l2] = 1
    home = np.stack([ly + 8, lx + 4]).astype(np.float32)
    return dict(
        ep=ep.reshape(384, 768),
        eo=eo.reshape(512, 768),
        wsel=wsel.reshape(8, 16, 112),
        wconst=wconst.reshape(8, 1, 112),
        extra=extra,
        cmask=cmask,
        unflat=unflat,
        home=home,
        perm=perm,
    )


def _split3(x):
    hi = x.astype(BF)
    rest = x - hi.astype(F32)
    mid = rest.astype(BF)
    low = (rest - mid.astype(F32)).astype(BF)
    return hi, mid, low


def _dot(x, y):
    return jnp.dot(x, y, preferred_element_type=F32)


def _kernel(
    pr_ref, cnt_ref, img_ref, sh_ref, fr_ref, ends_ref, stiff_ref, w1_ref, b1_ref, w2_ref, b2_ref,
    wsel_ref, wconst_ref, extra_ref, cmask_ref, home_ref, perm_ref, ep_hbm, eo_hbm, unflat_hbm,
    corr_ref, mis_ref, force_ref,
    j_ref, i_ref, rbuf, anch, gbuf, pbuf, pstage, ep_ref, eo_ref, unflat_ref,
    pad, qp, qo, p4, cpt, obuf, cbuf, wq, bias2, tbuf, px, mpx, fown, cown,
    send_sem, recv_sem, load_sem,
):
    sec = lax.axis_index("sec")
    tile = lax.axis_index("tile")
    back1 = lax.rem(sec + 15, 16)
    back2 = lax.rem(sec + 14, 16)
    fwd1 = lax.rem(sec + 1, 16)
    fwd2 = lax.rem(sec + 2, 16)
    peers = [lax.rem(tile + r, 8) for r in range(8)]
    has_down = tile < 7
    has_up = tile > 0
    tk = jnp.where(tile == 0, 0, jnp.where(tile == 7, 2, 1))

    barrier = pltpu.get_barrier_semaphore()
    for other in (back1, back2, fwd1, fwd2):
        pl.semaphore_signal(barrier, inc=1, device_id=(other, tile), device_id_type=MESH)
    for r in range(1, 8):
        pl.semaphore_signal(barrier, inc=1, device_id=(sec, peers[r]), device_id_type=MESH)

    loads = [
        pltpu.make_async_copy(src, dst, load_sem.at[k])
        for k, (src, dst) in enumerate(((eo_hbm, eo_ref), (ep_hbm, ep_ref), (unflat_hbm, unflat_ref)))
    ]
    for c in loads:
        c.start()

    rows = [sh_ref[s, k, 0:1, :].astype(F32) + fr_ref[s, k, 0:1, :] for s in range(2) for k in range(2)]
    rows = jnp.concatenate(rows + [jnp.zeros((4, 512), F32)], axis=0)
    x_at = lax.broadcasted_iota(jnp.int32, (512, 256), 0)
    v_at = lax.broadcasted_iota(jnp.int32, (512, 256), 1)
    select = jnp.where(x_at == 16 * (v_at - 32 * tile), 1.0, 0.0).astype(BF)
    got = _dot(jnp.concatenate(_split3(rows), axis=0).astype(BF), select)
    anch[...] = (got[16:24] + got[8:16]) + got[0:8]

    pl.semaphore_wait(barrier, 11)

    def remote(src, dst, k, target):
        return pltpu.make_async_remote_copy(
            src_ref=src, dst_ref=dst, send_sem=send_sem.at[k], recv_sem=recv_sem.at[k],
            device_id=target, device_id_type=MESH,
        )

    near = remote(img_ref, rbuf.at[0], 0, (back1, tile))
    far = remote(img_ref, rbuf.at[1], 1, (back2, tile))
    far.start()
    near.start()
    down_tile = (sec, lax.rem(tile + 1, 8))
    up_tile = (sec, lax.rem(tile + 7, 8))
    own_down = remote(img_ref.at[:, 16:32], i_ref.at[:, 0:16], 2, down_tile)
    own_up = remote(img_ref.at[:, 0:16], i_ref.at[:, 48:64], 3, up_tile)
    pl.when(has_down)(own_down.start)
    pl.when(has_up)(own_up.start)
    anchor_sends = [remote(anch, gbuf.at[r], 4 + r, (sec, peers[r])) for r in range(1, 8)]
    for c in anchor_sends:
        c.start()

    i_ref[:, 16:48, :] = img_ref[...]

    @pl.when(tile == 0)
    def _():
        i_ref[:, 0:16, :] = jnp.zeros((2, 16, 1024), BF)
        j_ref[:, 0:32, :] = jnp.zeros((2, 32, 1024), BF)

    @pl.when(tile == 7)
    def _():
        i_ref[:, 48:64, :] = jnp.zeros((2, 16, 1024), BF)
        j_ref[:, 64:96, :] = jnp.zeros((2, 32, 1024), BF)

    lane = lax.broadcasted_iota(jnp.int32, (64, 112), 1)
    bias1 = jnp.broadcast_to(b1_ref[...], (128, 64)).T[:, 0:112]
    hi, mid, low = (x.astype(F32) for x in _split3(bias1))
    base = (
        jnp.where(lane == 104, hi, 0.0) + jnp.where(lane == 105, mid, 0.0) + jnp.where(lane == 106, low, 0.0)
    )
    for m in range(8):
        spread = lax.dot_general(
            w1_ref[...], wsel_ref[m], (((0,), (0,)), ((), ())), preferred_element_type=F32
        )
        wq[64 * m : 64 * m + 64, :] = (spread + base + wconst_ref[m]).astype(BF)
    bias2[...] = jnp.broadcast_to(b2_ref[...], (128, 64)).T

    lane128 = lax.broadcasted_iota(jnp.int32, (1, 128), 1)
    x_bit = [lax.bitwise_and(lax.shift_right_logical(lane128, 3 + k), 1) == 1 for k in range(4)]
    y_bit = [lax.bitwise_and(lax.shift_right_logical(lane128, k), 1) == 1 for k in range(3)]
    row16 = lax.broadcasted_iota(jnp.int32, (16, 256), 0)

    def pixels(s, carry):
        planes = [sh_ref[s, k].astype(F32) for k in range(2)] + [fr_ref[s, k] for k in range(2)]
        tbuf[:, 0:64] = jnp.concatenate(planes, axis=0).T
        runs = [tbuf[pl.ds(x, 32, stride=16), :] for x in range(16)]
        planes = [jnp.concatenate([r[:, 16 * k : 16 * k + 16] for r in runs], axis=1) for k in range(4)]
        parts = [planes[0].astype(BF), planes[1].astype(BF), *_split3(planes[2]), *_split3(planes[3])]
        got = _dot(jnp.concatenate(parts, axis=0), perm_ref[...])
        px[s, 0] = got[0:32] + home_ref[0:1, :]
        px[s, 1] = got[32:64] + home_ref[1:2, :]
        px[s, 2] = (got[128:160] + got[96:128]) + got[64:96]
        px[s, 3] = (got[224:256] + got[192:224]) + got[160:192]
        return carry

    lax.fori_loop(0, 2, pixels, 0)

    for c in anchor_sends:
        c.wait()
    disp = anch[...]
    for r in range(1, 8):
        disp = disp + gbuf[r]
    vert = lax.broadcasted_iota(jnp.int32, (256, 256), 0)
    slot_at = lax.broadcasted_iota(jnp.int32, (1, 256), 1)
    row_of = lax.broadcasted_iota(jnp.int32, (8, 256), 0)
    parts = jnp.concatenate(_split3(disp), axis=0)
    total = jnp.zeros((8, 256), F32)
    for s in range(2):
        table = (vert == ends_ref[s, 1:2, :]).astype(F32) - (vert == ends_ref[s, 0:1, :]).astype(F32)
        table = table.astype(BF)
        got = _dot(parts, table)
        spread = (got[16:24] + got[8:16]) + got[0:8]
        pull = jnp.where(slot_at < cnt_ref[0, s], stiff_ref[s : s + 1, :], 0.0) * spread
        back = lax.dot_general(
            jnp.concatenate(_split3(pull), axis=0), table, (((1,), (1,)), ((), ())),
            preferred_element_type=F32,
        )
        back = (back[16:24] + back[8:16]) + back[0:8]
        total = total - jnp.where(lax.shift_right_logical(row_of, 1) == s, back, 0.0)
    pstage[...] = total
    force_sends = [remote(pstage, pbuf.at[r], 14 + r, (sec, peers[r])) for r in range(1, 8)]
    for c in force_sends:
        c.start()

    near.wait()
    far.wait()
    for s in range(2):
        p = pr_ref[s]
        which = jnp.where(lax.shift_right_logical(p, 1) == fwd1, 0, 1)
        slot = lax.bitwise_and(p, 1)
        j_ref[s, 32:64, :] = rbuf[which, slot]
    part_down = remote(j_ref.at[:, 32:64], j_ref.at[:, 0:32], 12, down_tile)
    part_up = remote(j_ref.at[:, 32:64], j_ref.at[:, 64:96], 13, up_tile)
    pl.when(has_down)(part_down.start)
    pl.when(has_up)(part_up.start)

    pl.when(has_down)(own_down.wait_send)
    pl.when(has_up)(own_up.wait_send)
    pl.when(has_up)(own_down.wait_recv)
    pl.when(has_down)(own_up.wait_recv)
    loads[0].wait()

    def side_by_side(left, right, more):
        return jnp.concatenate(
            [
                jnp.concatenate([left[:, 128 * p : 128 * p + 128], right[:, 128 * p : 128 * p + 128]], axis=1)
                for p in range(6)
            ]
            + [more],
            axis=0,
        )

    def own(s, carry):
        pad[0:64, 0:1024] = i_ref[s].astype(F32)
        pad[0:96, 1024:1152] = jnp.zeros((96, 128), F32)
        wide = pad[0:64, :]
        stack = jnp.concatenate(
            [pltpu.roll(wide, (1 - 2 * k) % 1152, 1)[:, 0:1024] for k in range(8)], axis=0
        )
        qo[...] = _dot(stack.T.astype(BF), eo_ref[...]).astype(BF)

        def encode(c, carry):
            small = []
            for n in range(4):
                r0 = pl.multiple_of(128 * c + 32 * n, 32)
                patches = side_by_side(qo[pl.ds(r0, 16), :], qo[pl.ds(r0 + 16, 16), :], extra_ref[1, 1])
                own4 = jnp.maximum(_dot(wq[0:256, :], patches).astype(BF), 0)
                fown[s, :, pl.ds(pl.multiple_of(1024 * c + 256 * n, 256), 256)] = own4[0:64, :]
                small += [own4[:, 0:32], own4[:, 128:160]]
            pre = _dot(w2_ref[...], jnp.concatenate(small, axis=1))
            pre = jnp.maximum(pre + jnp.concatenate([bias2[...]] * 2, axis=1), 0.0)
            cown[s, :, pl.ds(pl.multiple_of(256 * c, 256), 256)] = pre.astype(BF)
            return carry

        return lax.fori_loop(0, 8, encode, carry)

    lax.fori_loop(0, 2, own, 0)

    for c in force_sends:
        c.wait()
    total = pstage[...]
    for r in range(1, 8):
        total = total + pbuf[r]
    turned = pltpu.roll(total, lax.rem(256 - 32 * tile, 256), 1)
    for s in range(2):
        force_ref[s] = turned[2 * s : 2 * s + 2, 0:32]

    pl.when(has_down)(part_down.wait_send)
    pl.when(has_up)(part_up.wait_send)
    pl.when(has_up)(part_down.wait_recv)
    pl.when(has_down)(part_up.wait_recv)
    loads[1].wait()
    loads[2].wait()

    def section(s, carry):
        pad[0:96, 0:1024] = j_ref[s].astype(F32)
        wide = pad[...]
        stack = jnp.concatenate([pltpu.roll(wide, (17 - 2 * k) % 1152, 1) for k in range(4)], axis=0)
        qp[...] = _dot(stack.T.astype(BF), ep_ref[...])[0:1056].astype(BF)

        def partner(g, carry):
            r0 = pl.multiple_of(32 * g, 32)
            kind = jnp.where(g == 0, 0, jnp.where(g == QUADS - 1, 2, 1))
            patches = side_by_side(qp[pl.ds(r0, 16), :], qp[pl.ds(r0 + 16, 16), :], extra_ref[tk, kind])
            got = jnp.maximum(_dot(wq[...], patches).astype(BF), 0)
            l0 = pl.multiple_of(512 * g, 512)
            p4[:, pl.ds(l0, 512)] = jnp.concatenate(
                [got[0:256, 0:128], got[256:512, 0:128], got[0:256, 128:256], got[256:512, 128:256]], axis=1
            )
            return carry

        lax.fori_loop(0, QUADS, partner, 0, unroll=3)

        def coarsen(q, count):
            tiles = p4[:, pl.ds(pl.multiple_of(512 * q, 512), 512 * count)]
            tiles = jnp.concatenate([tiles[:, 128 * k : 128 * k + 32] for k in range(4 * count)], axis=1)
            pre = _dot(w2_ref[...], tiles)
            for n in range(count):
                kind = jnp.where(q + n == 0, 0, jnp.where(q + n == QUADS - 1, 2, 1))
                coarse = pre[:, 128 * n : 128 * n + 128] + bias2[...] + cmask_ref[tk, kind][0:1, :]
                coarse = jnp.maximum(coarse, 0.0).astype(BF).astype(F32)
                cpt[pl.ds(pl.multiple_of(128 * (q + n), 128), 128), 0:64] = coarse.T.astype(BF)

        def coarsen_four(g, carry):
            coarsen(4 * g, 4)
            return carry

        lax.fori_loop(0, QUADS // 4, coarsen_four, 0, unroll=2)
        coarsen(QUADS - 1, 1)

        def block(c, carry):
            for half in range(2):
                b = 2 * c + half
                own_map = fown[s, :, pl.ds(pl.multiple_of(256 * b, 256), 256)].astype(F32)
                row = px[s, 0, pl.ds(b, 1), :]
                col = px[s, 1, pl.ds(b, 1), :]
                fy = px[s, 2, pl.ds(b, 1), :]
                fx = px[s, 3, pl.ds(b, 1), :]
                row = jnp.broadcast_to(row.astype(jnp.int32), (16, 256))
                col = jnp.broadcast_to(col, (16, 256)).astype(BF)
                oy = [(row == 2 * row16 + a).astype(F32).astype(BF) for a in range(2)]
                zero = jnp.zeros((16, 256), BF)
                picks = []
                for k in range(6):
                    hit = {}
                    for bb in range(2):
                        for xx in range(2):
                            hit[bb, xx] = col == float(4 * k + 2 * xx + bb)
                    for a in range(2):
                        for bb in range(2):
                            for xx in range(2):
                                picks.append(jnp.where(hit[bb, xx], oy[a], zero))
                choose = jnp.concatenate(picks, axis=0)
                l0 = pl.multiple_of(512 * b + 128, 128)
                taps = _dot(p4[:, pl.ds(l0, 768)], choose)
                gy, gx = 1.0 - fy, 1.0 - fx
                warped = (
                    (gy * gx) * taps[0:64] + (gy * fx) * taps[64:128]
                    + (fy * gx) * taps[128:192] + (fy * fx) * taps[192:256]
                )
                differ = own_map - warped
                mpx[pl.ds(b, 1), :] = jnp.sum(differ * differ, axis=0, keepdims=True) * (1.0 / 64)

            coarse = cown[s, :, pl.ds(pl.multiple_of(128 * c, 128), 128)]
            there = cpt[pl.ds(pl.multiple_of(256 * c, 256), 384), 0:64]
            gram = _dot(there, coarse).reshape(24, 16, 128)
            for k, keep in ((3, 16), (2, 12), (1, 10), (0, 9)):
                step = 1 << k
                gram = jnp.where(x_bit[k][None], gram[step : step + keep], gram[0:keep])
            gram = gram.reshape(144, 128)
            cols = []
            for j in range(9):
                v = gram[16 * j : 16 * j + 16]
                for k in (2, 1, 0):
                    v = jnp.where(y_bit[k], pltpu.roll(v, 16 - (1 << k), 0), v)
                cols.append(v)
            gram = jnp.concatenate(cols, axis=0) * (1.0 / 64)
            obuf[:, pl.ds(pl.multiple_of(128 * c, 128), 128)] = gram.astype(BF)
            return carry

        lax.fori_loop(0, 16, block, 0)

        got = lax.dot_general(
            jnp.concatenate(_split3(mpx[...]), axis=0), perm_ref[...], (((1,), (1,)), ((), ())),
            preferred_element_type=F32,
        )
        got = (got[64:96] + got[32:64]) + got[0:32]
        for x in range(16):
            tbuf[pl.ds(x, 32, stride=16), 0:16] = got[:, 16 * x : 16 * x + 16]
        mis_ref[s] = tbuf[...].T[0:16, :]

        for h in range(2):
            flat = _dot(obuf[:, 1024 * h : 1024 * h + 1024], unflat_ref[...])
            for j in range(9):
                for y in range(8):
                    cbuf[h, pl.ds(8 * j + y, 9, stride=72), :] = flat[16 * j : 16 * j + 9, 128 * y : 128 * y + 128]
        for h in range(2):
            corr_ref[s, :, :, 128 * h : 128 * h + 128] = cbuf[h].reshape(81, 8, 128).astype(BF)
        return carry

    lax.fori_loop(0, 2, section, 0)


def local(
    section_image, partner_row, base_shift, bilinear_frac, first_kernel, initial_conv_bias,
    second_kernel, second_bias, edge_ends, edge_count, stiffness,
):
    t = _tables()
    vm = pl.BlockSpec(memory_space=pltpu.VMEM)
    sm = pl.BlockSpec(memory_space=pltpu.SMEM)
    hbm = pl.BlockSpec(memory_space=pl.ANY)
    consts = [
        jnp.asarray(t["wsel"], BF), jnp.asarray(t["wconst"], F32), jnp.asarray(t["extra"], BF),
        jnp.asarray(t["cmask"], F32), jnp.asarray(t["home"], F32), jnp.asarray(t["perm"], BF),
        jnp.asarray(t["ep"], BF), jnp.asarray(t["eo"], BF), jnp.asarray(t["unflat"], BF),
    ]
    return pl.pallas_call(
        _kernel,
        out_shape=(
            jax.ShapeDtypeStruct((2, 81, 8, 256), BF),
            jax.ShapeDtypeStruct((2, 16, 512), F32),
            jax.ShapeDtypeStruct((2, 2, 32), F32),
        ),
        in_specs=[sm, sm] + [vm] * 15 + [hbm] * 3,
        out_specs=(vm, vm, vm),
        scratch_shapes=[
            pltpu.VMEM((2, 96, 1024), BF),
            pltpu.VMEM((2, 64, 1024), BF),
            pltpu.VMEM((2, 2, 32, 1024), BF),
            pltpu.VMEM((8, 256), F32),
            pltpu.VMEM((8, 8, 256), F32),
            pltpu.VMEM((8, 8, 256), F32),
            pltpu.VMEM((8, 256), F32),
            pltpu.VMEM((384, 768), BF),
            pltpu.VMEM((512, 768), BF),
            pltpu.VMEM((1024, 1024), BF),
            pltpu.VMEM((96, 1152), F32),
            pltpu.VMEM((1056, 768), BF),
            pltpu.VMEM((1024, 768), BF),
            pltpu.VMEM((256, PT * 128), BF),
            pltpu.VMEM((PT * 32, 128), BF),
            pltpu.VMEM((144, 2048), BF),
            pltpu.VMEM((2, 648, 128), F32),
            pltpu.VMEM((512, 112), BF),
            pltpu.VMEM((64, 128), F32),
            pltpu.VMEM((512, 128), F32),
            pltpu.VMEM((2, 4, 32, 256), F32),
            pltpu.VMEM((32, 256), F32),
            pltpu.VMEM((2, 64, 8192), BF),
            pltpu.VMEM((2, 64, 2048), BF),
            pltpu.SemaphoreType.DMA((22,)),
            pltpu.SemaphoreType.DMA((22,)),
            pltpu.SemaphoreType.DMA((3,)),
        ],
        compiler_params=pltpu.CompilerParams(
            collective_id=0, has_side_effects=True, vmem_limit_bytes=VMEM_BYTES
        ),
        name="align",
    )(
        partner_row, edge_count.T, section_image, base_shift, bilinear_frac, edge_ends, stiffness,
        first_kernel.T, initial_conv_bias.reshape(1, 64), second_kernel, second_bias.reshape(1, 64), *consts,
    )


def solution(mesh):
    in_specs = (
        P("sec", "tile", None), P("sec"), P("sec", None, "tile", None), P("sec", None, "tile", None),
        P(), P(), P(), P(), P("sec", None, "tile"), P("sec", "tile"), P("sec", "tile"),
    )
    out_specs = (P("sec", None, "tile", None), P("sec", "tile", None), P("sec", None, "tile"))
    return jax.shard_map(local, mesh=mesh, in_specs=in_specs, out_specs=out_specs, check_vma=False)
```

```python
import jax
import jax.numpy as jnp
import numpy as np
from jax import lax
from jax.experimental import pallas as pl
from jax.experimental.pallas import tpu as pltpu
from jax.sharding import PartitionSpec as P

BF = jnp.bfloat16
F32 = jnp.float32
MESH = pl.DeviceIdType.MESH
BIG = -1e30
VMEM_BYTES = 56 * 1024 * 1024

PT = 132
QUADS = PT // 4


def _tables():
    lane = np.arange(128)
    a, b, xx, yy = lane // 64, (lane // 32) % 2, (lane // 16) % 2, lane % 16
    x4, y2 = 2 * xx + b, 2 * yy + a
    ep = np.zeros((4, 96, 6, 128), np.float32)
    for p in range(6):
        ep[x4, 2 * y2 + 15 + p, p, lane] = 1
    oa, ob, ox, oy = lane // 64, (lane // 32) % 2, (lane // 8) % 4, lane % 8
    x8, y1 = 2 * ox + ob, 2 * oy + oa
    eo = np.zeros((8, 64, 6, 128), np.float32)
    for p in range(6):
        eo[x8, 2 * y1 + 15 + p, p, lane] = 1
    wsel = np.zeros((2, 2, 2, 16, 112), np.float32)
    wconst = np.zeros((2, 2, 2, 1, 112), np.float32)
    for e in range(2):
        for ta in range(2):
            for tb in range(2):
                for u in range(4):
                    for v in range(4):
                        wsel[e, ta, tb, 4 * u + v, (u + 2 * ta) * 16 + 8 * e + 2 * tb + v] = 1
                wconst[e, ta, tb, 0, 96 + 4 * e + 2 * ta + tb] = BIG
    extra = np.zeros((3, 3, 16, 256), np.float32)
    cmask = np.zeros((3, 3, 8, 128), np.float32)
    for tk in range(3):
        for gk, g in enumerate((0, 1, QUADS - 1)):
            for half in range(2):
                for e in range(2):
                    for ta in range(2):
                        for tb in range(2):
                            col = 4 * (4 * g + 2 * half + e) - 8 + x4 + tb
                            row = y2 - 8 + ta
                            bad = (col < 0) | (col > 511)
                            if tk == 0:
                                bad = bad | (row < 0)
                            if tk == 2:
                                bad = bad | (row > 15)
                            extra[tk, gk, 4 * e + 2 * ta + tb, 128 * half : 128 * half + 128] = bad
            extra[tk, gk, 8:11] = 1
            ccol, crow = 8 * g - 4 + lane // 16, lane % 16 - 4
            bad = (ccol < 0) | (ccol > 255)
            if tk == 0:
                bad = bad | (crow < 0)
            if tk == 2:
                bad = bad | (crow > 7)
            cmask[tk, gk] = np.where(bad, BIG, 0.0)
    src = np.arange(1024)
    unflat = np.zeros((1024, 1024), np.float32)
    unflat[src, (src % 8) * 128 + src // 8] = 1
    l2 = np.arange(256)
    lx = 8 * (l2 // 128) + 2 * ((l2 // 8) % 4) + (l2 // 32) % 2
    ly = 2 * (l2 % 8) + (l2 // 64) % 2
    perm = np.zeros((256, 256), np.float32)
    perm[16 * lx + ly, l2] = 1
    home = np.stack([ly + 8, lx + 4]).astype(np.float32)
    return dict(
        ep=ep.reshape(384, 768),
        eo=eo.reshape(512, 768),
        wsel=wsel.reshape(8, 16, 112),
        wconst=wconst.reshape(8, 1, 112),
        extra=extra,
        cmask=cmask,
        unflat=unflat,
        home=home,
        perm=perm,
    )


def _split3(x):
    hi = x.astype(BF)
    rest = x - hi.astype(F32)
    mid = rest.astype(BF)
    low = (rest - mid.astype(F32)).astype(BF)
    return hi, mid, low


def _dot(x, y):
    return jnp.dot(x, y, preferred_element_type=F32)


def _kernel(
    pr_ref, cnt_ref, img_ref, sh_ref, fr_ref, ends_ref, stiff_ref, w1_ref, b1_ref, w2_ref, b2_ref,
    wsel_ref, wconst_ref, extra_ref, cmask_ref, home_ref, perm_ref, ep_hbm, eo_hbm, unflat_hbm,
    corr_ref, mis_ref, force_ref,
    j_ref, i_ref, rbuf, anch, gbuf, pbuf, pstage, ep_ref, eo_ref, unflat_ref,
    pad, qp, qo, p4, cpt, obuf, cbuf, wq, bias2, tbuf, px, mpx, fown, cown,
    send_sem, recv_sem, load_sem,
):
    sec = lax.axis_index("sec")
    tile = lax.axis_index("tile")
    back1 = lax.rem(sec + 15, 16)
    back2 = lax.rem(sec + 14, 16)
    fwd1 = lax.rem(sec + 1, 16)
    fwd2 = lax.rem(sec + 2, 16)
    peers = [lax.rem(tile + r, 8) for r in range(8)]
    has_down = tile < 7
    has_up = tile > 0
    tk = jnp.where(tile == 0, 0, jnp.where(tile == 7, 2, 1))

    barrier = pltpu.get_barrier_semaphore()
    for other in (back1, back2, fwd1, fwd2):
        pl.semaphore_signal(barrier, inc=1, device_id=(other, tile), device_id_type=MESH)
    for r in range(1, 8):
        pl.semaphore_signal(barrier, inc=1, device_id=(sec, peers[r]), device_id_type=MESH)

    loads = [
        pltpu.make_async_copy(src, dst, load_sem.at[k])
        for k, (src, dst) in enumerate(((eo_hbm, eo_ref), (ep_hbm, ep_ref), (unflat_hbm, unflat_ref)))
    ]
    for c in loads:
        c.start()

    rows = [sh_ref[s, k, 0:1, :].astype(F32) + fr_ref[s, k, 0:1, :] for s in range(2) for k in range(2)]
    rows = jnp.concatenate(rows + [jnp.zeros((4, 512), F32)], axis=0)
    x_at = lax.broadcasted_iota(jnp.int32, (512, 256), 0)
    v_at = lax.broadcasted_iota(jnp.int32, (512, 256), 1)
    select = jnp.where(x_at == 16 * (v_at - 32 * tile), 1.0, 0.0).astype(BF)
    got = _dot(jnp.concatenate(_split3(rows), axis=0).astype(BF), select)
    anch[...] = (got[16:24] + got[8:16]) + got[0:8]

    lane = lax.broadcasted_iota(jnp.int32, (64, 112), 1)
    bias1 = jnp.broadcast_to(b1_ref[...], (128, 64)).T[:, 0:112]
    hi, mid, low = (x.astype(F32) for x in _split3(bias1))
    base = (
        jnp.where(lane == 104, hi, 0.0) + jnp.where(lane == 105, mid, 0.0) + jnp.where(lane == 106, low, 0.0)
    )
    for m in range(8):
        spread = lax.dot_general(
            w1_ref[...], wsel_ref[m], (((0,), (0,)), ((), ())), preferred_element_type=F32
        )
        wq[64 * m : 64 * m + 64, :] = (spread + base + wconst_ref[m]).astype(BF)
    bias2[...] = jnp.broadcast_to(b2_ref[...], (128, 64)).T

    lane128 = lax.broadcasted_iota(jnp.int32, (1, 128), 1)
    x_bit = [lax.bitwise_and(lax.shift_right_logical(lane128, 3 + k), 1) == 1 for k in range(4)]
    y_bit = [lax.bitwise_and(lax.shift_right_logical(lane128, k), 1) == 1 for k in range(3)]
    row16 = lax.broadcasted_iota(jnp.int32, (16, 256), 0)

    def pixels(s, carry):
        planes = [sh_ref[s, k].astype(F32) for k in range(2)] + [fr_ref[s, k] for k in range(2)]
        tbuf[:, 0:64] = jnp.concatenate(planes, axis=0).T
        runs = [tbuf[pl.ds(x, 32, stride=16), :] for x in range(16)]
        planes = [jnp.concatenate([r[:, 16 * k : 16 * k + 16] for r in runs], axis=1) for k in range(4)]
        parts = [planes[0].astype(BF), planes[1].astype(BF), *_split3(planes[2]), *_split3(planes[3])]
        got = _dot(jnp.concatenate(parts, axis=0), perm_ref[...])
        px[s, 0] = got[0:32] + home_ref[0:1, :]
        px[s, 1] = got[32:64] + home_ref[1:2, :]
        px[s, 2] = (got[128:160] + got[96:128]) + got[64:96]
        px[s, 3] = (got[224:256] + got[192:224]) + got[160:192]
        return carry

    lax.fori_loop(0, 2, pixels, 0)

    pl.semaphore_wait(barrier, 11)

    def remote(src, dst, k, target):
        return pltpu.make_async_remote_copy(
            src_ref=src, dst_ref=dst, send_sem=send_sem.at[k], recv_sem=recv_sem.at[k],
            device_id=target, device_id_type=MESH,
        )

    near = remote(img_ref, rbuf.at[0], 0, (back1, tile))
    far = remote(img_ref, rbuf.at[1], 1, (back2, tile))
    far.start()
    near.start()
    down_tile = (sec, lax.rem(tile + 1, 8))
    up_tile = (sec, lax.rem(tile + 7, 8))
    own_down = remote(img_ref.at[:, 16:32], i_ref.at[:, 0:16], 2, down_tile)
    own_up = remote(img_ref.at[:, 0:16], i_ref.at[:, 48:64], 3, up_tile)
    pl.when(has_down)(own_down.start)
    pl.when(has_up)(own_up.start)
    anchor_sends = [remote(anch, gbuf.at[r], 4 + r, (sec, peers[r])) for r in range(1, 8)]
    for c in anchor_sends:
        c.start()

    i_ref[:, 16:48, :] = img_ref[...]

    @pl.when(tile == 0)
    def _():
        i_ref[:, 0:16, :] = jnp.zeros((2, 16, 1024), BF)
        j_ref[:, 0:32, :] = jnp.zeros((2, 32, 1024), BF)

    @pl.when(tile == 7)
    def _():
        i_ref[:, 48:64, :] = jnp.zeros((2, 16, 1024), BF)
        j_ref[:, 64:96, :] = jnp.zeros((2, 32, 1024), BF)

    for c in anchor_sends:
        c.wait()
    disp = anch[...]
    for r in range(1, 8):
        disp = disp + gbuf[r]
    vert = lax.broadcasted_iota(jnp.int32, (256, 256), 0)
    slot_at = lax.broadcasted_iota(jnp.int32, (1, 256), 1)
    row_of = lax.broadcasted_iota(jnp.int32, (8, 256), 0)
    parts = jnp.concatenate(_split3(disp), axis=0)
    total = jnp.zeros((8, 256), F32)
    for s in range(2):
        table = (vert == ends_ref[s, 1:2, :]).astype(F32) - (vert == ends_ref[s, 0:1, :]).astype(F32)
        table = table.astype(BF)
        got = _dot(parts, table)
        spread = (got[16:24] + got[8:16]) + got[0:8]
        pull = jnp.where(slot_at < cnt_ref[0, s], stiff_ref[s : s + 1, :], 0.0) * spread
        back = lax.dot_general(
            jnp.concatenate(_split3(pull), axis=0), table, (((1,), (1,)), ((), ())),
            preferred_element_type=F32,
        )
        back = (back[16:24] + back[8:16]) + back[0:8]
        total = total - jnp.where(lax.shift_right_logical(row_of, 1) == s, back, 0.0)
    pstage[...] = total
    force_sends = [remote(pstage, pbuf.at[r], 14 + r, (sec, peers[r])) for r in range(1, 8)]
    for c in force_sends:
        c.start()

    pl.when(has_down)(own_down.wait_send)
    pl.when(has_up)(own_up.wait_send)
    pl.when(has_up)(own_down.wait_recv)
    pl.when(has_down)(own_up.wait_recv)
    loads[0].wait()

    def side_by_side(left, right, more):
        return jnp.concatenate(
            [
                jnp.concatenate([left[:, 128 * p : 128 * p + 128], right[:, 128 * p : 128 * p + 128]], axis=1)
                for p in range(6)
            ]
            + [more],
            axis=0,
        )

    def own(s, carry):
        pad[0:64, 0:1024] = i_ref[s].astype(F32)
        pad[0:96, 1024:1152] = jnp.zeros((96, 128), F32)
        wide = pad[0:64, :]
        stack = jnp.concatenate(
            [pltpu.roll(wide, (1 - 2 * k) % 1152, 1)[:, 0:1024] for k in range(8)], axis=0
        )
        qo[...] = _dot(stack.T.astype(BF), eo_ref[...]).astype(BF)

        def encode(c, carry):
            small = []
            for n in range(4):
                r0 = pl.multiple_of(128 * c + 32 * n, 32)
                patches = side_by_side(qo[pl.ds(r0, 16), :], qo[pl.ds(r0 + 16, 16), :], extra_ref[1, 1])
                own4 = jnp.maximum(_dot(wq[0:256, :], patches).astype(BF), 0)
                fown[s, :, pl.ds(pl.multiple_of(1024 * c + 256 * n, 256), 256)] = own4[0:64, :]
                small += [own4[:, 0:32], own4[:, 128:160]]
            pre = _dot(w2_ref[...], jnp.concatenate(small, axis=1))
            pre = jnp.maximum(pre + jnp.concatenate([bias2[...]] * 2, axis=1), 0.0)
            cown[s, :, pl.ds(pl.multiple_of(256 * c, 256), 256)] = pre.astype(BF)
            return carry

        return lax.fori_loop(0, 8, encode, carry, unroll=4)

    own(0, 0)

    near.wait()
    far.wait()
    for s in range(2):
        p = pr_ref[s]
        which = jnp.where(lax.shift_right_logical(p, 1) == fwd1, 0, 1)
        slot = lax.bitwise_and(p, 1)
        j_ref[s, 32:64, :] = rbuf[which, slot]
    part_down = remote(j_ref.at[:, 32:64], j_ref.at[:, 0:32], 12, down_tile)
    part_up = remote(j_ref.at[:, 32:64], j_ref.at[:, 64:96], 13, up_tile)
    pl.when(has_down)(part_down.start)
    pl.when(has_up)(part_up.start)

    own(1, 0)

    for c in force_sends:
        c.wait()
    total = pstage[...]
    for r in range(1, 8):
        total = total + pbuf[r]
    turned = pltpu.roll(total, lax.rem(256 - 32 * tile, 256), 1)
    for s in range(2):
        force_ref[s] = turned[2 * s : 2 * s + 2, 0:32]

    pl.when(has_down)(part_down.wait_send)
    pl.when(has_up)(part_up.wait_send)
    pl.when(has_up)(part_down.wait_recv)
    pl.when(has_down)(part_up.wait_recv)
    loads[1].wait()
    loads[2].wait()

    def section(s, carry):
        pad[0:96, 0:1024] = j_ref[s].astype(F32)
        wide = pad[...]
        stack = jnp.concatenate([pltpu.roll(wide, (17 - 2 * k) % 1152, 1) for k in range(4)], axis=0)
        qp[...] = _dot(stack.T.astype(BF), ep_ref[...])[0:1056].astype(BF)

        def partner(g, carry):
            r0 = pl.multiple_of(32 * g, 32)
            kind = jnp.where(g == 0, 0, jnp.where(g == QUADS - 1, 2, 1))
            patches = side_by_side(qp[pl.ds(r0, 16), :], qp[pl.ds(r0 + 16, 16), :], extra_ref[tk, kind])
            got = jnp.maximum(_dot(wq[...], patches).astype(BF), 0)
            l0 = pl.multiple_of(512 * g, 512)
            p4[:, pl.ds(l0, 512)] = jnp.concatenate(
                [got[0:256, 0:128], got[256:512, 0:128], got[0:256, 128:256], got[256:512, 128:256]], axis=1
            )
            return carry

        def coarsen(q, count):
            tiles = p4[:, pl.ds(pl.multiple_of(512 * q, 512), 512 * count)]
            tiles = jnp.concatenate([tiles[:, 128 * k : 128 * k + 32] for k in range(4 * count)], axis=1)
            pre = _dot(w2_ref[...], tiles)
            for n in range(count):
                kind = jnp.where(q + n == 0, 0, jnp.where(q + n == QUADS - 1, 2, 1))
                coarse = pre[:, 128 * n : 128 * n + 128] + bias2[...] + cmask_ref[tk, kind][0:1, :]
                coarse = jnp.maximum(coarse, 0.0).astype(BF).astype(F32)
                cpt[pl.ds(pl.multiple_of(128 * (q + n), 128), 128), 0:64] = coarse.T.astype(BF)

        def both(g, carry):
            coarsen(4 * g - 4, 4)
            for n in range(4):
                partner(4 * g + n, carry)
            return carry

        for n in range(4):
            partner(n, 0)
        lax.fori_loop(1, QUADS // 4, both, 0)
        coarsen(QUADS - 5, 4)
        partner(QUADS - 1, 0)
        coarsen(QUADS - 1, 1)

        def block(c, carry):
            for half in range(2):
                b = 2 * c + half
                own_map = fown[s, :, pl.ds(pl.multiple_of(256 * b, 256), 256)].astype(F32)
                row = px[s, 0, pl.ds(b, 1), :]
                col = px[s, 1, pl.ds(b, 1), :]
                fy = px[s, 2, pl.ds(b, 1), :]
                fx = px[s, 3, pl.ds(b, 1), :]
                row = jnp.broadcast_to(row.astype(jnp.int32), (16, 256))
                col = jnp.broadcast_to(col, (16, 256)).astype(BF)
                oy = [(row == 2 * row16 + a).astype(F32).astype(BF) for a in range(2)]
                zero = jnp.zeros((16, 256), BF)
                picks = []
                for k in range(6):
                    hit = {}
                    for bb in range(2):
                        for xx in range(2):
                            hit[bb, xx] = col == float(4 * k + 2 * xx + bb)
                    for a in range(2):
                        for bb in range(2):
                            for xx in range(2):
                                picks.append(jnp.where(hit[bb, xx], oy[a], zero))
                choose = jnp.concatenate(picks, axis=0)
                l0 = pl.multiple_of(512 * b + 128, 128)
                taps = _dot(p4[:, pl.ds(l0, 768)], choose)
                gy, gx = 1.0 - fy, 1.0 - fx
                warped = (
                    (gy * gx) * taps[0:64] + (gy * fx) * taps[64:128]
                    + (fy * gx) * taps[128:192] + (fy * fx) * taps[192:256]
                )
                differ = own_map - warped
                mpx[pl.ds(b, 1), :] = jnp.sum(differ * differ, axis=0, keepdims=True) * (1.0 / 64)

            coarse = cown[s, :, pl.ds(pl.multiple_of(128 * c, 128), 128)]
            there = cpt[pl.ds(pl.multiple_of(256 * c, 256), 384), 0:64]
            gram = _dot(there, coarse).reshape(24, 16, 128)
            for k, keep in ((3, 16), (2, 12), (1, 10), (0, 9)):
                step = 1 << k
                gram = jnp.where(x_bit[k][None], gram[step : step + keep], gram[0:keep])
            gram = gram.reshape(144, 128)
            cols = []
            for j in range(9):
                v = gram[16 * j : 16 * j + 16]
                for k in (2, 1, 0):
                    v = jnp.where(y_bit[k], pltpu.roll(v, 16 - (1 << k), 0), v)
                cols.append(v)
            gram = jnp.concatenate(cols, axis=0) * (1.0 / 64)
            obuf[pl.ds(pl.multiple_of(144 * s, 16), 144), pl.ds(pl.multiple_of(128 * c, 128), 128)] = gram.astype(BF)
            return carry

        lax.fori_loop(0, 16, block, 0, unroll=2)

        got = lax.dot_general(
            jnp.concatenate(_split3(mpx[...]), axis=0), perm_ref[...], (((1,), (1,)), ((), ())),
            preferred_element_type=F32,
        )
        got = (got[64:96] + got[32:64]) + got[0:32]
        for x in range(16):
            tbuf[pl.ds(x, 32, stride=16), 0:16] = got[:, 16 * x : 16 * x + 16]
        mis_ref[s] = tbuf[...].T[0:16, :]

        return carry

    lax.fori_loop(0, 2, section, 0)

    for h in range(2):
        flat = _dot(obuf[:, 1024 * h : 1024 * h + 1024], unflat_ref[...])
        for s in range(2):
            for j in range(9):
                r0 = 144 * s + 16 * j
                for y in range(8):
                    cbuf[s, pl.ds(8 * j + y, 9, stride=72), :] = flat[r0 : r0 + 9, 128 * y : 128 * y + 128]
        for s in range(2):
            corr_ref[s, :, :, 128 * h : 128 * h + 128] = cbuf[s].reshape(81, 8, 128).astype(BF)


def _hand_on(a, b, c, x, y, z):
    x[...] = a[...]
    y[...] = b[...]
    z[...] = c[...]


def local(
    section_image, partner_row, base_shift, bilinear_frac, first_kernel, initial_conv_bias,
    second_kernel, second_bias, edge_ends, edge_count, stiffness,
):
    t = _tables()
    vm = pl.BlockSpec(memory_space=pltpu.VMEM)
    sm = pl.BlockSpec(memory_space=pltpu.SMEM)
    hbm = pl.BlockSpec(memory_space=pl.ANY)
    consts = [
        jnp.asarray(t["wsel"], BF), jnp.asarray(t["wconst"], F32), jnp.asarray(t["extra"], BF),
        jnp.asarray(t["cmask"], F32), jnp.asarray(t["home"], F32), jnp.asarray(t["perm"], BF),
        jnp.asarray(t["ep"], BF), jnp.asarray(t["eo"], BF), jnp.asarray(t["unflat"], BF),
    ]
    results = pl.pallas_call(
        _kernel,
        out_shape=(
            jax.ShapeDtypeStruct((2, 81, 8, 256), BF),
            jax.ShapeDtypeStruct((2, 16, 512), F32),
            jax.ShapeDtypeStruct((2, 2, 32), F32),
        ),
        in_specs=[sm, sm] + [vm] * 15 + [hbm] * 3,
        out_specs=(vm, vm, vm),
        scratch_shapes=[
            pltpu.VMEM((2, 96, 1024), BF),
            pltpu.VMEM((2, 64, 1024), BF),
            pltpu.VMEM((2, 2, 32, 1024), BF),
            pltpu.VMEM((8, 256), F32),
            pltpu.VMEM((8, 8, 256), F32),
            pltpu.VMEM((8, 8, 256), F32),
            pltpu.VMEM((8, 256), F32),
            pltpu.VMEM((384, 768), BF),
            pltpu.VMEM((512, 768), BF),
            pltpu.VMEM((1024, 1024), BF),
            pltpu.VMEM((96, 1152), F32),
            pltpu.VMEM((1056, 768), BF),
            pltpu.VMEM((1024, 768), BF),
            pltpu.VMEM((256, PT * 128), BF),
            pltpu.VMEM((PT * 32, 128), BF),
            pltpu.VMEM((288, 2048), BF),
            pltpu.VMEM((2, 648, 128), F32),
            pltpu.VMEM((512, 112), BF),
            pltpu.VMEM((64, 128), F32),
            pltpu.VMEM((512, 128), F32),
            pltpu.VMEM((2, 4, 32, 256), F32),
            pltpu.VMEM((32, 256), F32),
            pltpu.VMEM((2, 64, 8192), BF),
            pltpu.VMEM((2, 64, 2048), BF),
            pltpu.SemaphoreType.DMA((22,)),
            pltpu.SemaphoreType.DMA((22,)),
            pltpu.SemaphoreType.DMA((3,)),
        ],
        compiler_params=pltpu.CompilerParams(
            collective_id=0, has_side_effects=True, vmem_limit_bytes=VMEM_BYTES
        ),
        name="align",
    )(
        partner_row, edge_count.T, section_image, base_shift, bilinear_frac, edge_ends, stiffness,
        first_kernel.T, initial_conv_bias.reshape(1, 64), second_kernel, second_bias.reshape(1, 64), *consts,
    )
    return pl.pallas_call(
        _hand_on,
        out_shape=tuple(jax.ShapeDtypeStruct(r.shape, r.dtype) for r in results),
        in_specs=[vm] * 3,
        out_specs=(vm,) * 3,
        name="hand_on",
    )(*results)


def solution(mesh):
    in_specs = (
        P("sec", "tile", None), P("sec"), P("sec", None, "tile", None), P("sec", None, "tile", None),
        P(), P(), P(), P(), P("sec", None, "tile"), P("sec", "tile"), P("sec", "tile"),
    )
    out_specs = (P("sec", None, "tile", None), P("sec", "tile", None), P("sec", None, "tile"))
    return jax.shard_map(local, mesh=mesh, in_specs=in_specs, out_specs=out_specs, check_vma=False)
```

```python
import jax
import jax.numpy as jnp
import numpy as np
from jax import lax
from jax.experimental import pallas as pl
from jax.experimental.pallas import tpu as pltpu
from jax.sharding import PartitionSpec as P

BF = jnp.bfloat16
F32 = jnp.float32
MESH = pl.DeviceIdType.MESH
BIG = -1e30
VMEM_BYTES = 56 * 1024 * 1024

PT = 132
QUADS = PT // 4


def _tables():
    lane = np.arange(128)
    a, b, xx, yy = lane // 64, (lane // 32) % 2, (lane // 16) % 2, lane % 16
    x4, y2 = 2 * xx + b, 2 * yy + a
    ep = np.zeros((4, 128, 6, 128), np.float32)
    for p in range(6):
        ep[x4, 2 * y2 + 15 + p, p, lane] = 1
    oa, ob, ox, oy = lane // 64, (lane // 32) % 2, (lane // 8) % 4, lane % 8
    x8, y1 = 2 * ox + ob, 2 * oy + oa
    eo = np.zeros((8, 64, 6, 128), np.float32)
    for p in range(6):
        eo[x8, 2 * y1 + 15 + p, p, lane] = 1
    wsel = np.zeros((2, 2, 2, 16, 112), np.float32)
    wconst = np.zeros((2, 2, 2, 1, 112), np.float32)
    for e in range(2):
        for ta in range(2):
            for tb in range(2):
                for u in range(4):
                    for v in range(4):
                        wsel[e, ta, tb, 4 * u + v, (u + 2 * ta) * 16 + 8 * e + 2 * tb + v] = 1
                wconst[e, ta, tb, 0, 96 + 4 * e + 2 * ta + tb] = BIG
    extra = np.zeros((3, 3, 16, 256), np.float32)
    cmask = np.zeros((3, 3, 8, 128), np.float32)
    for tk in range(3):
        for gk, g in enumerate((0, 1, QUADS - 1)):
            for half in range(2):
                for e in range(2):
                    for ta in range(2):
                        for tb in range(2):
                            col = 4 * (4 * g + 2 * half + e) - 8 + x4 + tb
                            row = y2 - 8 + ta
                            bad = (col < 0) | (col > 511)
                            if tk == 0:
                                bad = bad | (row < 0)
                            if tk == 2:
                                bad = bad | (row > 15)
                            extra[tk, gk, 4 * e + 2 * ta + tb, 128 * half : 128 * half + 128] = bad
            extra[tk, gk, 8:11] = 1
            ccol, crow = 8 * g - 4 + lane // 16, lane % 16 - 4
            bad = (ccol < 0) | (ccol > 255)
            if tk == 0:
                bad = bad | (crow < 0)
            if tk == 2:
                bad = bad | (crow > 7)
            cmask[tk, gk] = np.where(bad, BIG, 0.0)
    src = np.arange(1024)
    unflat = np.zeros((1024, 1024), np.float32)
    unflat[src, (src % 8) * 128 + src // 8] = 1
    l2 = np.arange(256)
    lx = 8 * (l2 // 128) + 2 * ((l2 // 8) % 4) + (l2 // 32) % 2
    ly = 2 * (l2 % 8) + (l2 // 64) % 2
    perm = np.zeros((256, 256), np.float32)
    perm[16 * lx + ly, l2] = 1
    home = np.stack([ly + 8, lx + 4]).astype(np.float32)
    return dict(
        ep=ep.reshape(512, 768),
        eo=eo.reshape(512, 768),
        wsel=wsel.reshape(8, 16, 112),
        wconst=wconst.reshape(8, 1, 112),
        extra=extra,
        cmask=cmask,
        unflat=unflat,
        home=home,
        perm=perm,
    )


def _split3(x):
    hi = x.astype(BF)
    rest = x - hi.astype(F32)
    mid = rest.astype(BF)
    low = (rest - mid.astype(F32)).astype(BF)
    return hi, mid, low


def _dot(x, y):
    return jnp.dot(x, y, preferred_element_type=F32)


def _kernel(
    pr_ref, cnt_ref, img_ref, sh_ref, fr_ref, ends_ref, stiff_ref, w1_ref, b1_ref, w2_ref, b2_ref,
    wsel_ref, wconst_ref, extra_ref, cmask_ref, home_ref, perm_ref, ep_hbm, eo_hbm, unflat_hbm,
    corr_ref, mis_ref, force_ref,
    j_ref, i_ref, rbuf, anch, gbuf, pbuf, pstage, ep_ref, eo_ref, unflat_ref,
    tall, qp, qo, p4, cpt, obuf, cbuf, wq, bias2, tbuf, px, mpx, fown, cown,
    send_sem, recv_sem, load_sem,
):
    sec = lax.axis_index("sec")
    tile = lax.axis_index("tile")
    back1 = lax.rem(sec + 15, 16)
    back2 = lax.rem(sec + 14, 16)
    fwd1 = lax.rem(sec + 1, 16)
    fwd2 = lax.rem(sec + 2, 16)
    peers = [lax.rem(tile + r, 8) for r in range(8)]
    has_down = tile < 7
    has_up = tile > 0
    tk = jnp.where(tile == 0, 0, jnp.where(tile == 7, 2, 1))

    barrier = pltpu.get_barrier_semaphore()
    for other in (back1, back2, fwd1, fwd2):
        pl.semaphore_signal(barrier, inc=1, device_id=(other, tile), device_id_type=MESH)
    for r in range(1, 8):
        pl.semaphore_signal(barrier, inc=1, device_id=(sec, peers[r]), device_id_type=MESH)

    loads = [
        pltpu.make_async_copy(src, dst, load_sem.at[k])
        for k, (src, dst) in enumerate(((eo_hbm, eo_ref), (ep_hbm, ep_ref), (unflat_hbm, unflat_ref)))
    ]
    for c in loads:
        c.start()

    rows = [sh_ref[s, k, 0:1, :].astype(F32) + fr_ref[s, k, 0:1, :] for s in range(2) for k in range(2)]
    rows = jnp.concatenate(rows + [jnp.zeros((4, 512), F32)], axis=0)
    x_at = lax.broadcasted_iota(jnp.int32, (512, 256), 0)
    v_at = lax.broadcasted_iota(jnp.int32, (512, 256), 1)
    select = jnp.where(x_at == 16 * (v_at - 32 * tile), 1.0, 0.0).astype(BF)
    got = _dot(jnp.concatenate(_split3(rows), axis=0).astype(BF), select)
    anch[...] = (got[16:24] + got[8:16]) + got[0:8]

    lane = lax.broadcasted_iota(jnp.int32, (64, 112), 1)
    bias1 = jnp.broadcast_to(b1_ref[...], (128, 64)).T[:, 0:112]
    hi, mid, low = (x.astype(F32) for x in _split3(bias1))
    base = (
        jnp.where(lane == 104, hi, 0.0) + jnp.where(lane == 105, mid, 0.0) + jnp.where(lane == 106, low, 0.0)
    )
    for m in range(8):
        spread = lax.dot_general(
            w1_ref[...], wsel_ref[m], (((0,), (0,)), ((), ())), preferred_element_type=F32
        )
        wq[64 * m : 64 * m + 64, :] = (spread + base + wconst_ref[m]).astype(BF)
    bias2[...] = jnp.broadcast_to(b2_ref[...], (128, 64)).T

    lane128 = lax.broadcasted_iota(jnp.int32, (1, 128), 1)
    x_bit = [lax.bitwise_and(lax.shift_right_logical(lane128, 3 + k), 1) == 1 for k in range(4)]
    y_bit = [lax.bitwise_and(lax.shift_right_logical(lane128, k), 1) == 1 for k in range(3)]
    row16 = lax.broadcasted_iota(jnp.int32, (16, 256), 0)

    def pixels(s, carry):
        planes = [sh_ref[s, k].astype(F32) for k in range(2)] + [fr_ref[s, k] for k in range(2)]
        tbuf[:, 0:64] = jnp.concatenate(planes, axis=0).T
        runs = [tbuf[pl.ds(x, 32, stride=16), :] for x in range(16)]
        planes = [jnp.concatenate([r[:, 16 * k : 16 * k + 16] for r in runs], axis=1) for k in range(4)]
        parts = [planes[0].astype(BF), planes[1].astype(BF), *_split3(planes[2]), *_split3(planes[3])]
        got = _dot(jnp.concatenate(parts, axis=0), perm_ref[...])
        px[s, 0] = got[0:32] + home_ref[0:1, :]
        px[s, 1] = got[32:64] + home_ref[1:2, :]
        px[s, 2] = (got[128:160] + got[96:128]) + got[64:96]
        px[s, 3] = (got[224:256] + got[192:224]) + got[160:192]
        return carry

    lax.fori_loop(0, 2, pixels, 0)

    pl.semaphore_wait(barrier, 11)

    def remote(src, dst, k, target):
        return pltpu.make_async_remote_copy(
            src_ref=src, dst_ref=dst, send_sem=send_sem.at[k], recv_sem=recv_sem.at[k],
            device_id=target, device_id_type=MESH,
        )

    near = remote(img_ref, rbuf.at[0], 0, (back1, tile))
    far = remote(img_ref, rbuf.at[1], 1, (back2, tile))
    far.start()
    near.start()
    down_tile = (sec, lax.rem(tile + 1, 8))
    up_tile = (sec, lax.rem(tile + 7, 8))
    own_down = remote(img_ref.at[:, 16:32], i_ref.at[:, 0:16], 2, down_tile)
    own_up = remote(img_ref.at[:, 0:16], i_ref.at[:, 48:64], 3, up_tile)
    pl.when(has_down)(own_down.start)
    pl.when(has_up)(own_up.start)
    anchor_sends = [remote(anch, gbuf.at[r], 4 + r, (sec, peers[r])) for r in range(1, 8)]
    for c in anchor_sends:
        c.start()

    i_ref[:, 16:48, :] = img_ref[...]

    @pl.when(tile == 0)
    def _():
        i_ref[:, 0:16, :] = jnp.zeros((2, 16, 1024), BF)
        j_ref[:, 0:32, :] = jnp.zeros((2, 32, 1024), BF)

    @pl.when(tile == 7)
    def _():
        i_ref[:, 48:64, :] = jnp.zeros((2, 16, 1024), BF)
        j_ref[:, 64:96, :] = jnp.zeros((2, 32, 1024), BF)

    for c in anchor_sends:
        c.wait()
    disp = anch[...]
    for r in range(1, 8):
        disp = disp + gbuf[r]
    vert = lax.broadcasted_iota(jnp.int32, (256, 256), 0)
    slot_at = lax.broadcasted_iota(jnp.int32, (1, 256), 1)
    row_of = lax.broadcasted_iota(jnp.int32, (8, 256), 0)
    parts = jnp.concatenate(_split3(disp), axis=0)
    total = jnp.zeros((8, 256), F32)
    for s in range(2):
        table = (vert == ends_ref[s, 1:2, :]).astype(F32) - (vert == ends_ref[s, 0:1, :]).astype(F32)
        table = table.astype(BF)
        got = _dot(parts, table)
        spread = (got[16:24] + got[8:16]) + got[0:8]
        pull = jnp.where(slot_at < cnt_ref[0, s], stiff_ref[s : s + 1, :], 0.0) * spread
        back = lax.dot_general(
            jnp.concatenate(_split3(pull), axis=0), table, (((1,), (1,)), ((), ())),
            preferred_element_type=F32,
        )
        back = (back[16:24] + back[8:16]) + back[0:8]
        total = total - jnp.where(lax.shift_right_logical(row_of, 1) == s, back, 0.0)
    pstage[...] = total
    force_sends = [remote(pstage, pbuf.at[r], 14 + r, (sec, peers[r])) for r in range(1, 8)]
    for c in force_sends:
        c.start()

    pl.when(has_down)(own_down.wait_send)
    pl.when(has_up)(own_up.wait_send)
    pl.when(has_up)(own_down.wait_recv)
    pl.when(has_down)(own_up.wait_recv)
    loads[0].wait()

    def side_by_side(left, right, more):
        return jnp.concatenate(
            [
                jnp.concatenate([left[:, 128 * p : 128 * p + 128], right[:, 128 * p : 128 * p + 128]], axis=1)
                for p in range(6)
            ]
            + [more],
            axis=0,
        )

    def own(s, carry):
        wide = jnp.concatenate([i_ref[s].astype(F32), jnp.zeros((64, 128), F32)], axis=1)
        turned = jnp.concatenate([pltpu.roll(wide, 1, 1), pltpu.roll(wide, 1151, 1)], axis=0)
        tall[...] = turned.T
        stack = jnp.concatenate([tall[4 * k : 4 * k + 1024, :].astype(BF) for k in range(4)], axis=1)
        qo[...] = _dot(stack, eo_ref[...]).astype(BF)

        def encode(c, carry):
            small = []
            for n in range(4):
                r0 = pl.multiple_of(128 * c + 32 * n, 32)
                patches = side_by_side(qo[pl.ds(r0, 16), :], qo[pl.ds(r0 + 16, 16), :], extra_ref[1, 1])
                got = jnp.maximum(_dot(wq[0:64, :], patches).astype(BF), 0)
                fown[s, :, pl.ds(pl.multiple_of(1024 * c + 256 * n, 256), 256)] = got
                small += [patches[:, 0:32], patches[:, 128:160]]
            own4 = jnp.maximum(_dot(wq[0:256, :], jnp.concatenate(small, axis=1)).astype(BF), 0)
            pre = _dot(w2_ref[...], own4)
            pre = jnp.maximum(pre + jnp.concatenate([bias2[...]] * 2, axis=1), 0.0)
            cown[s, :, pl.ds(pl.multiple_of(256 * c, 256), 256)] = pre.astype(BF)
            return carry

        return lax.fori_loop(0, 8, encode, carry, unroll=4)

    own(0, 0)

    near.wait()
    far.wait()
    for s in range(2):
        p = pr_ref[s]
        which = jnp.where(lax.shift_right_logical(p, 1) == fwd1, 0, 1)
        slot = lax.bitwise_and(p, 1)
        j_ref[s, 32:64, :] = rbuf[which, slot]
    part_down = remote(j_ref.at[:, 32:64], j_ref.at[:, 0:32], 12, down_tile)
    part_up = remote(j_ref.at[:, 32:64], j_ref.at[:, 64:96], 13, up_tile)
    pl.when(has_down)(part_down.start)
    pl.when(has_up)(part_up.start)

    own(1, 0)

    for c in force_sends:
        c.wait()
    total = pstage[...]
    for r in range(1, 8):
        total = total + pbuf[r]
    turned = pltpu.roll(total, lax.rem(256 - 32 * tile, 256), 1)
    for s in range(2):
        force_ref[s] = turned[2 * s : 2 * s + 2, 0:32]

    pl.when(has_down)(part_down.wait_send)
    pl.when(has_up)(part_up.wait_send)
    pl.when(has_up)(part_down.wait_recv)
    pl.when(has_down)(part_up.wait_recv)
    loads[1].wait()
    loads[2].wait()

    def section(s, carry):
        wide = jnp.concatenate([j_ref[s].astype(F32), jnp.zeros((96, 128), F32)], axis=1)
        turned = jnp.concatenate([pltpu.roll(wide, 17, 1), jnp.zeros((32, 1152), F32)], axis=0)
        tall[...] = turned.T
        stack = jnp.concatenate([tall[2 * k : 2 * k + 1056, :].astype(BF) for k in range(4)], axis=1)
        qp[...] = _dot(stack, ep_ref[...]).astype(BF)

        def partner(g, carry):
            r0 = pl.multiple_of(32 * g, 32)
            kind = jnp.where(g == 0, 0, jnp.where(g == QUADS - 1, 2, 1))
            patches = side_by_side(qp[pl.ds(r0, 16), :], qp[pl.ds(r0 + 16, 16), :], extra_ref[tk, kind])
            got = jnp.maximum(_dot(wq[...], patches).astype(BF), 0)
            l0 = pl.multiple_of(512 * g, 512)
            p4[:, pl.ds(l0, 512)] = jnp.concatenate(
                [got[0:256, 0:128], got[256:512, 0:128], got[0:256, 128:256], got[256:512, 128:256]], axis=1
            )
            return carry

        def coarsen(q, count):
            tiles = p4[:, pl.ds(pl.multiple_of(512 * q, 512), 512 * count)]
            tiles = jnp.concatenate([tiles[:, 128 * k : 128 * k + 32] for k in range(4 * count)], axis=1)
            pre = _dot(w2_ref[...], tiles)
            for n in range(count):
                kind = jnp.where(q + n == 0, 0, jnp.where(q + n == QUADS - 1, 2, 1))
                coarse = pre[:, 128 * n : 128 * n + 128] + bias2[...] + cmask_ref[tk, kind][0:1, :]
                coarse = jnp.maximum(coarse, 0.0).astype(BF).astype(F32)
                cpt[pl.ds(pl.multiple_of(128 * (q + n), 128), 128), 0:64] = coarse.T.astype(BF)

        def both(g, carry):
            coarsen(4 * g - 4, 4)
            for n in range(4):
                partner(4 * g + n, carry)
            return carry

        for n in range(4):
            partner(n, 0)
        lax.fori_loop(1, QUADS // 4, both, 0)
        coarsen(QUADS - 5, 4)
        partner(QUADS - 1, 0)
        coarsen(QUADS - 1, 1)

        def block(c, carry):
            for half in range(2):
                b = 2 * c + half
                own_map = fown[s, :, pl.ds(pl.multiple_of(256 * b, 256), 256)].astype(F32)
                row = px[s, 0, pl.ds(b, 1), :]
                col = px[s, 1, pl.ds(b, 1), :]
                fy = px[s, 2, pl.ds(b, 1), :]
                fx = px[s, 3, pl.ds(b, 1), :]
                row = jnp.broadcast_to(row.astype(jnp.int32), (16, 256))
                col = jnp.broadcast_to(col, (16, 256)).astype(BF)
                oy = [(row == 2 * row16 + a).astype(F32).astype(BF) for a in range(2)]
                zero = jnp.zeros((16, 256), BF)
                picks = []
                for k in range(6):
                    hit = {}
                    for bb in range(2):
                        for xx in range(2):
                            hit[bb, xx] = col == float(4 * k + 2 * xx + bb)
                    for a in range(2):
                        for bb in range(2):
                            for xx in range(2):
                                picks.append(jnp.where(hit[bb, xx], oy[a], zero))
                choose = jnp.concatenate(picks, axis=0)
                l0 = pl.multiple_of(512 * b + 128, 128)
                taps = _dot(p4[:, pl.ds(l0, 768)], choose)
                gy, gx = 1.0 - fy, 1.0 - fx
                warped = (
                    (gy * gx) * taps[0:64] + (gy * fx) * taps[64:128]
                    + (fy * gx) * taps[128:192] + (fy * fx) * taps[192:256]
                )
                differ = own_map - warped
                mpx[pl.ds(b, 1), :] = jnp.sum(differ * differ, axis=0, keepdims=True) * (1.0 / 64)

            coarse = cown[s, :, pl.ds(pl.multiple_of(128 * c, 128), 128)]
            there = cpt[pl.ds(pl.multiple_of(256 * c, 256), 384), 0:64]
            gram = _dot(there, coarse).reshape(24, 16, 128)
            for k, keep in ((3, 16), (2, 12), (1, 10), (0, 9)):
                step = 1 << k
                gram = jnp.where(x_bit[k][None], gram[step : step + keep], gram[0:keep])
            gram = gram.reshape(144, 128)
            cols = []
            for j in range(9):
                v = gram[16 * j : 16 * j + 16]
                for k in (2, 1, 0):
                    v = jnp.where(y_bit[k], pltpu.roll(v, 16 - (1 << k), 0), v)
                cols.append(v)
            gram = jnp.concatenate(cols, axis=0) * (1.0 / 64)
            obuf[pl.ds(pl.multiple_of(144 * s, 16), 144), pl.ds(pl.multiple_of(128 * c, 128), 128)] = gram.astype(BF)
            return carry

        lax.fori_loop(0, 16, block, 0, unroll=4)

        got = lax.dot_general(
            jnp.concatenate(_split3(mpx[...]), axis=0), perm_ref[...], (((1,), (1,)), ((), ())),
            preferred_element_type=F32,
        )
        got = (got[64:96] + got[32:64]) + got[0:32]
        for x in range(16):
            tbuf[pl.ds(x, 32, stride=16), 0:16] = got[:, 16 * x : 16 * x + 16]
        mis_ref[s] = tbuf[...].T[0:16, :]

        return carry

    lax.fori_loop(0, 2, section, 0)

    for h in range(2):
        flat = _dot(obuf[:, 1024 * h : 1024 * h + 1024], unflat_ref[...])
        for s in range(2):
            for j in range(9):
                r0 = 144 * s + 16 * j
                for y in range(8):
                    cbuf[s, pl.ds(8 * j + y, 9, stride=72), :] = flat[r0 : r0 + 9, 128 * y : 128 * y + 128]
        for s in range(2):
            corr_ref[s, :, :, 128 * h : 128 * h + 128] = cbuf[s].reshape(81, 8, 128).astype(BF)


def _hand_on(a, b, c, x, y, z):
    x[...] = a[...]
    y[...] = b[...]
    z[...] = c[...]


def local(
    section_image, partner_row, base_shift, bilinear_frac, first_kernel, initial_conv_bias,
    second_kernel, second_bias, edge_ends, edge_count, stiffness,
):
    t = _tables()
    vm = pl.BlockSpec(memory_space=pltpu.VMEM)
    sm = pl.BlockSpec(memory_space=pltpu.SMEM)
    hbm = pl.BlockSpec(memory_space=pl.ANY)
    consts = [
        jnp.asarray(t["wsel"], BF), jnp.asarray(t["wconst"], F32), jnp.asarray(t["extra"], BF),
        jnp.asarray(t["cmask"], F32), jnp.asarray(t["home"], F32), jnp.asarray(t["perm"], BF),
        jnp.asarray(t["ep"], BF), jnp.asarray(t["eo"], BF), jnp.asarray(t["unflat"], BF),
    ]
    results = pl.pallas_call(
        _kernel,
        out_shape=(
            jax.ShapeDtypeStruct((2, 81, 8, 256), BF),
            jax.ShapeDtypeStruct((2, 16, 512), F32),
            jax.ShapeDtypeStruct((2, 2, 32), F32),
        ),
        in_specs=[sm, sm] + [vm] * 15 + [hbm] * 3,
        out_specs=(vm, vm, vm),
        scratch_shapes=[
            pltpu.VMEM((2, 96, 1024), BF),
            pltpu.VMEM((2, 64, 1024), BF),
            pltpu.VMEM((2, 2, 32, 1024), BF),
            pltpu.VMEM((8, 256), F32),
            pltpu.VMEM((8, 8, 256), F32),
            pltpu.VMEM((8, 8, 256), F32),
            pltpu.VMEM((8, 256), F32),
            pltpu.VMEM((512, 768), BF),
            pltpu.VMEM((512, 768), BF),
            pltpu.VMEM((1024, 1024), BF),
            pltpu.VMEM((1152, 128), F32),
            pltpu.VMEM((1056, 768), BF),
            pltpu.VMEM((1024, 768), BF),
            pltpu.VMEM((256, PT * 128), BF),
            pltpu.VMEM((PT * 32, 128), BF),
            pltpu.VMEM((288, 2048), BF),
            pltpu.VMEM((2, 648, 128), F32),
            pltpu.VMEM((512, 112), BF),
            pltpu.VMEM((64, 128), F32),
            pltpu.VMEM((512, 128), F32),
            pltpu.VMEM((2, 4, 32, 256), F32),
            pltpu.VMEM((32, 256), F32),
            pltpu.VMEM((2, 64, 8192), BF),
            pltpu.VMEM((2, 64, 2048), BF),
            pltpu.SemaphoreType.DMA((22,)),
            pltpu.SemaphoreType.DMA((22,)),
            pltpu.SemaphoreType.DMA((3,)),
        ],
        compiler_params=pltpu.CompilerParams(
            collective_id=0, has_side_effects=True, vmem_limit_bytes=VMEM_BYTES
        ),
        name="align",
    )(
        partner_row, edge_count.T, section_image, base_shift, bilinear_frac, edge_ends, stiffness,
        first_kernel.T, initial_conv_bias.reshape(1, 64), second_kernel, second_bias.reshape(1, 64), *consts,
    )
    return pl.pallas_call(
        _hand_on,
        out_shape=tuple(jax.ShapeDtypeStruct(r.shape, r.dtype) for r in results),
        in_specs=[vm] * 3,
        out_specs=(vm,) * 3,
        name="hand_on",
    )(*results)


def solution(mesh):
    in_specs = (
        P("sec", "tile", None), P("sec"), P("sec", None, "tile", None), P("sec", None, "tile", None),
        P(), P(), P(), P(), P("sec", None, "tile"), P("sec", "tile"), P("sec", "tile"),
    )
    out_specs = (P("sec", None, "tile", None), P("sec", "tile", None), P("sec", None, "tile"))
    return jax.shard_map(local, mesh=mesh, in_specs=in_specs, out_specs=out_specs, check_vma=False)
```

```python
import jax
import jax.numpy as jnp
import numpy as np
from jax import lax
from jax.experimental import pallas as pl
from jax.experimental.pallas import tpu as pltpu
from jax.sharding import PartitionSpec as P

BF = jnp.bfloat16
F32 = jnp.float32
MESH = pl.DeviceIdType.MESH
BIG = -1e30
VMEM_BYTES = 56 * 1024 * 1024

PT = 132
QUADS = PT // 4


def _tables():
    lane = np.arange(128)
    a, b, xx, yy = lane // 64, (lane // 32) % 2, (lane // 16) % 2, lane % 16
    x4, y2 = 2 * xx + b, 2 * yy + a
    ep = np.zeros((4, 128, 6, 128), np.float32)
    for p in range(6):
        ep[x4, 2 * y2 + 15 + p, p, lane] = 1
    oa, ob, ox, oy = lane // 64, (lane // 32) % 2, (lane // 8) % 4, lane % 8
    x8, y1 = 2 * ox + ob, 2 * oy + oa
    eo = np.zeros((8, 64, 6, 128), np.float32)
    for p in range(6):
        eo[x8, 2 * y1 + 15 + p, p, lane] = 1
    wsel = np.zeros((2, 2, 2, 16, 112), np.float32)
    wconst = np.zeros((2, 2, 2, 1, 112), np.float32)
    for e in range(2):
        for ta in range(2):
            for tb in range(2):
                for u in range(4):
                    for v in range(4):
                        wsel[e, ta, tb, 4 * u + v, (u + 2 * ta) * 16 + 8 * e + 2 * tb + v] = 1
                wconst[e, ta, tb, 0, 96 + 4 * e + 2 * ta + tb] = BIG
    extra = np.zeros((3, 3, 16, 256), np.float32)
    cmask = np.zeros((3, 3, 8, 128), np.float32)
    for tk in range(3):
        for gk, g in enumerate((0, 1, QUADS - 1)):
            for half in range(2):
                for e in range(2):
                    for ta in range(2):
                        for tb in range(2):
                            col = 4 * (4 * g + 2 * half + e) - 8 + x4 + tb
                            row = y2 - 8 + ta
                            bad = (col < 0) | (col > 511)
                            if tk == 0:
                                bad = bad | (row < 0)
                            if tk == 2:
                                bad = bad | (row > 15)
                            extra[tk, gk, 4 * e + 2 * ta + tb, 128 * half : 128 * half + 128] = bad
            extra[tk, gk, 8:11] = 1
            ccol, crow = 8 * g - 4 + lane // 16, lane % 16 - 4
            bad = (ccol < 0) | (ccol > 255)
            if tk == 0:
                bad = bad | (crow < 0)
            if tk == 2:
                bad = bad | (crow > 7)
            cmask[tk, gk] = np.where(bad, BIG, 0.0)
    src = np.arange(1024)
    unflat = np.zeros((1024, 1024), np.float32)
    unflat[src, (src % 8) * 128 + src // 8] = 1
    l2 = np.arange(256)
    lx = 8 * (l2 // 128) + 2 * ((l2 // 8) % 4) + (l2 // 32) % 2
    ly = 2 * (l2 % 8) + (l2 // 64) % 2
    perm = np.zeros((256, 256), np.float32)
    perm[16 * lx + ly, l2] = 1
    home = np.stack([ly + 8, lx + 4]).astype(np.float32)
    return dict(
        ep=ep.reshape(512, 768),
        eo=eo.reshape(512, 768),
        wsel=wsel.reshape(8, 16, 112),
        wconst=wconst.reshape(8, 1, 112),
        extra=extra,
        cmask=cmask,
        unflat=unflat,
        home=home,
        perm=perm,
    )


def _split3(x):
    hi = x.astype(BF)
    rest = x - hi.astype(F32)
    mid = rest.astype(BF)
    low = (rest - mid.astype(F32)).astype(BF)
    return hi, mid, low


def _dot(x, y):
    return jnp.dot(x, y, preferred_element_type=F32)


def _kernel(
    pr_ref, cnt_ref, img_ref, sh_ref, fr_ref, ends_ref, stiff_ref, w1_ref, b1_ref, w2_ref, b2_ref,
    wsel_ref, wconst_ref, extra_ref, cmask_ref, home_ref, perm_ref, ep_hbm, eo_hbm, unflat_hbm,
    corr_ref, mis_ref, force_ref,
    j_ref, i_ref, ask_out, ask_in, sbuf, rbuf, anch, gbuf, pbuf, pstage, ep_ref, eo_ref, unflat_ref,
    tall, qp, qo, p4, cpt, obuf, cbuf, wq, bias2, tbuf, px, mpx, fown, cown,
    send_sem, recv_sem, load_sem,
):
    sec = lax.axis_index("sec")
    tile = lax.axis_index("tile")
    back1 = lax.rem(sec + 15, 16)
    back2 = lax.rem(sec + 14, 16)
    fwd1 = lax.rem(sec + 1, 16)
    fwd2 = lax.rem(sec + 2, 16)
    peers = [lax.rem(tile + r, 8) for r in range(8)]
    has_down = tile < 7
    has_up = tile > 0
    tk = jnp.where(tile == 0, 0, jnp.where(tile == 7, 2, 1))

    barrier = pltpu.get_barrier_semaphore()
    for other in (back1, back2, fwd1, fwd2):
        pl.semaphore_signal(barrier, inc=1, device_id=(other, tile), device_id_type=MESH)
    for r in range(1, 8):
        pl.semaphore_signal(barrier, inc=1, device_id=(sec, peers[r]), device_id_type=MESH)

    loads = [
        pltpu.make_async_copy(src, dst, load_sem.at[k])
        for k, (src, dst) in enumerate(((eo_hbm, eo_ref), (ep_hbm, ep_ref), (unflat_hbm, unflat_ref)))
    ]
    for c in loads:
        c.start()

    rows = [sh_ref[s, k, 0:1, :].astype(F32) + fr_ref[s, k, 0:1, :] for s in range(2) for k in range(2)]
    rows = jnp.concatenate(rows + [jnp.zeros((4, 512), F32)], axis=0)
    x_at = lax.broadcasted_iota(jnp.int32, (512, 256), 0)
    v_at = lax.broadcasted_iota(jnp.int32, (512, 256), 1)
    select = jnp.where(x_at == 16 * (v_at - 32 * tile), 1.0, 0.0).astype(BF)
    got = _dot(jnp.concatenate(_split3(rows), axis=0).astype(BF), select)
    anch[...] = (got[16:24] + got[8:16]) + got[0:8]

    lane = lax.broadcasted_iota(jnp.int32, (64, 112), 1)
    bias1 = jnp.broadcast_to(b1_ref[...], (128, 64)).T[:, 0:112]
    hi, mid, low = (x.astype(F32) for x in _split3(bias1))
    base = (
        jnp.where(lane == 104, hi, 0.0) + jnp.where(lane == 105, mid, 0.0) + jnp.where(lane == 106, low, 0.0)
    )
    for m in range(8):
        spread = lax.dot_general(
            w1_ref[...], wsel_ref[m], (((0,), (0,)), ((), ())), preferred_element_type=F32
        )
        wq[64 * m : 64 * m + 64, :] = (spread + base + wconst_ref[m]).astype(BF)
    bias2[...] = jnp.broadcast_to(b2_ref[...], (128, 64)).T

    lane128 = lax.broadcasted_iota(jnp.int32, (1, 128), 1)
    x_bit = [lax.bitwise_and(lax.shift_right_logical(lane128, 3 + k), 1) == 1 for k in range(4)]
    y_bit = [lax.bitwise_and(lax.shift_right_logical(lane128, k), 1) == 1 for k in range(3)]
    row16 = lax.broadcasted_iota(jnp.int32, (16, 256), 0)

    def pixels(s, carry):
        planes = [sh_ref[s, k].astype(F32) for k in range(2)] + [fr_ref[s, k] for k in range(2)]
        tbuf[:, 0:64] = jnp.concatenate(planes, axis=0).T
        runs = [tbuf[pl.ds(x, 32, stride=16), :] for x in range(16)]
        planes = [jnp.concatenate([r[:, 16 * k : 16 * k + 16] for r in runs], axis=1) for k in range(4)]
        parts = [planes[0].astype(BF), planes[1].astype(BF), *_split3(planes[2]), *_split3(planes[3])]
        got = _dot(jnp.concatenate(parts, axis=0), perm_ref[...])
        px[s, 0] = got[0:32] + home_ref[0:1, :]
        px[s, 1] = got[32:64] + home_ref[1:2, :]
        px[s, 2] = (got[128:160] + got[96:128]) + got[64:96]
        px[s, 3] = (got[224:256] + got[192:224]) + got[160:192]
        return carry


    pl.semaphore_wait(barrier, 11)

    def remote(src, dst, k, target):
        return pltpu.make_async_remote_copy(
            src_ref=src, dst_ref=dst, send_sem=send_sem.at[k], recv_sem=recv_sem.at[k],
            device_id=target, device_id_type=MESH,
        )

    first_near = lax.shift_right_logical(pr_ref[0], 1) == fwd1
    slots = [lax.bitwise_and(pr_ref[s], 1) for s in range(2)]
    ask_out[0] = jnp.full((8, 128), jnp.where(first_near, slots[0], slots[1]), jnp.int32)
    ask_out[1] = jnp.full((8, 128), jnp.where(first_near, slots[1], slots[0]), jnp.int32)
    asks = [remote(ask_out.at[k], ask_in.at[k], 22 + k, (ahead, tile)) for k, ahead in enumerate((fwd1, fwd2))]
    for c in asks:
        c.start()
    near = remote(sbuf.at[0], rbuf.at[0], 0, (back1, tile))
    far = remote(sbuf.at[1], rbuf.at[1], 1, (back2, tile))
    down_tile = (sec, lax.rem(tile + 1, 8))
    up_tile = (sec, lax.rem(tile + 7, 8))
    own_down = remote(img_ref.at[:, 16:32], i_ref.at[:, 0:16], 2, down_tile)
    own_up = remote(img_ref.at[:, 0:16], i_ref.at[:, 48:64], 3, up_tile)
    pl.when(has_down)(own_down.start)
    pl.when(has_up)(own_up.start)
    anchor_sends = [remote(anch, gbuf.at[r], 4 + r, (sec, peers[r])) for r in range(1, 8)]
    for c in anchor_sends:
        c.start()

    i_ref[:, 16:48, :] = img_ref[...]

    @pl.when(tile == 0)
    def _():
        i_ref[:, 0:16, :] = jnp.zeros((2, 16, 1024), BF)
        j_ref[:, 0:32, :] = jnp.zeros((2, 32, 1024), BF)

    @pl.when(tile == 7)
    def _():
        i_ref[:, 48:64, :] = jnp.zeros((2, 16, 1024), BF)
        j_ref[:, 64:96, :] = jnp.zeros((2, 32, 1024), BF)

    lax.fori_loop(0, 2, pixels, 0)

    for k, copy in ((1, far), (0, near)):
        asks[k].wait()
        slot = jnp.broadcast_to(jnp.concatenate([ask_in[k, 0:1, :]] * 8, axis=1), (32, 1024))
        sbuf[k] = jnp.where(slot == 0, img_ref[0].astype(F32), img_ref[1].astype(F32)).astype(BF)
        copy.start()

    for c in anchor_sends:
        c.wait()
    disp = anch[...]
    for r in range(1, 8):
        disp = disp + gbuf[r]
    vert = lax.broadcasted_iota(jnp.int32, (256, 256), 0)
    slot_at = lax.broadcasted_iota(jnp.int32, (1, 256), 1)
    row_of = lax.broadcasted_iota(jnp.int32, (8, 256), 0)
    parts = jnp.concatenate(_split3(disp), axis=0)
    total = jnp.zeros((8, 256), F32)
    for s in range(2):
        table = (vert == ends_ref[s, 1:2, :]).astype(F32) - (vert == ends_ref[s, 0:1, :]).astype(F32)
        table = table.astype(BF)
        got = _dot(parts, table)
        spread = (got[16:24] + got[8:16]) + got[0:8]
        pull = jnp.where(slot_at < cnt_ref[0, s], stiff_ref[s : s + 1, :], 0.0) * spread
        back = lax.dot_general(
            jnp.concatenate(_split3(pull), axis=0), table, (((1,), (1,)), ((), ())),
            preferred_element_type=F32,
        )
        back = (back[16:24] + back[8:16]) + back[0:8]
        total = total - jnp.where(lax.shift_right_logical(row_of, 1) == s, back, 0.0)
    pstage[...] = total
    force_sends = [remote(pstage, pbuf.at[r], 14 + r, (sec, peers[r])) for r in range(1, 8)]
    for c in force_sends:
        c.start()

    pl.when(has_down)(own_down.wait_send)
    pl.when(has_up)(own_up.wait_send)
    pl.when(has_up)(own_down.wait_recv)
    pl.when(has_down)(own_up.wait_recv)
    loads[0].wait()

    def side_by_side(left, right, more):
        return jnp.concatenate(
            [
                jnp.concatenate([left[:, 128 * p : 128 * p + 128], right[:, 128 * p : 128 * p + 128]], axis=1)
                for p in range(6)
            ]
            + [more],
            axis=0,
        )

    def own(s, carry):
        wide = jnp.concatenate([i_ref[s].astype(F32), jnp.zeros((64, 128), F32)], axis=1)
        turned = jnp.concatenate([pltpu.roll(wide, 1, 1), pltpu.roll(wide, 1151, 1)], axis=0)
        tall[...] = turned.T
        stack = jnp.concatenate([tall[4 * k : 4 * k + 1024, :].astype(BF) for k in range(4)], axis=1)
        qo[...] = _dot(stack, eo_ref[...]).astype(BF)

        def encode(c, carry):
            small = []
            for n in range(4):
                r0 = pl.multiple_of(128 * c + 32 * n, 32)
                patches = side_by_side(qo[pl.ds(r0, 16), :], qo[pl.ds(r0 + 16, 16), :], extra_ref[1, 1])
                got = jnp.maximum(_dot(wq[0:64, :], patches).astype(BF), 0)
                fown[s, :, pl.ds(pl.multiple_of(1024 * c + 256 * n, 256), 256)] = got
                small += [patches[:, 0:32], patches[:, 128:160]]
            own4 = jnp.maximum(_dot(wq[0:256, :], jnp.concatenate(small, axis=1)).astype(BF), 0)
            pre = _dot(w2_ref[...], own4)
            pre = jnp.maximum(pre + jnp.concatenate([bias2[...]] * 2, axis=1), 0.0)
            cown[s, :, pl.ds(pl.multiple_of(256 * c, 256), 256)] = pre.astype(BF)
            return carry

        return lax.fori_loop(0, 8, encode, carry, unroll=4)

    own(0, 0)

    near.wait()
    far.wait()
    for s in range(2):
        which = jnp.where(lax.shift_right_logical(pr_ref[s], 1) == fwd1, 0, 1)
        j_ref[s, 32:64, :] = rbuf[which]
    part_down = remote(j_ref.at[:, 32:64], j_ref.at[:, 0:32], 12, down_tile)
    part_up = remote(j_ref.at[:, 32:64], j_ref.at[:, 64:96], 13, up_tile)
    pl.when(has_down)(part_down.start)
    pl.when(has_up)(part_up.start)

    own(1, 0)

    for c in force_sends:
        c.wait()
    total = pstage[...]
    for r in range(1, 8):
        total = total + pbuf[r]
    turned = pltpu.roll(total, lax.rem(256 - 32 * tile, 256), 1)
    for s in range(2):
        force_ref[s] = turned[2 * s : 2 * s + 2, 0:32]

    pl.when(has_down)(part_down.wait_send)
    pl.when(has_up)(part_up.wait_send)
    pl.when(has_up)(part_down.wait_recv)
    pl.when(has_down)(part_up.wait_recv)
    loads[1].wait()
    loads[2].wait()

    def section(s, carry):
        wide = jnp.concatenate([j_ref[s].astype(F32), jnp.zeros((96, 128), F32)], axis=1)
        turned = jnp.concatenate([pltpu.roll(wide, 17, 1), jnp.zeros((32, 1152), F32)], axis=0)
        tall[...] = turned.T
        stack = jnp.concatenate([tall[2 * k : 2 * k + 1056, :].astype(BF) for k in range(4)], axis=1)
        qp[...] = _dot(stack, ep_ref[...]).astype(BF)

        def partner(g, carry):
            r0 = pl.multiple_of(32 * g, 32)
            kind = jnp.where(g == 0, 0, jnp.where(g == QUADS - 1, 2, 1))
            patches = side_by_side(qp[pl.ds(r0, 16), :], qp[pl.ds(r0 + 16, 16), :], extra_ref[tk, kind])
            got = jnp.maximum(_dot(wq[...], patches).astype(BF), 0)
            l0 = pl.multiple_of(512 * g, 512)
            p4[:, pl.ds(l0, 512)] = jnp.concatenate(
                [got[0:256, 0:128], got[256:512, 0:128], got[0:256, 128:256], got[256:512, 128:256]], axis=1
            )
            return carry

        def coarsen(q, count):
            tiles = p4[:, pl.ds(pl.multiple_of(512 * q, 512), 512 * count)]
            tiles = jnp.concatenate([tiles[:, 128 * k : 128 * k + 32] for k in range(4 * count)], axis=1)
            pre = _dot(w2_ref[...], tiles)
            for n in range(count):
                kind = jnp.where(q + n == 0, 0, jnp.where(q + n == QUADS - 1, 2, 1))
                coarse = pre[:, 128 * n : 128 * n + 128] + bias2[...] + cmask_ref[tk, kind][0:1, :]
                coarse = jnp.maximum(coarse, 0.0).astype(BF).astype(F32)
                cpt[pl.ds(pl.multiple_of(128 * (q + n), 128), 128), 0:64] = coarse.T.astype(BF)

        def both(g, carry):
            coarsen(4 * g - 4, 4)
            for n in range(4):
                partner(4 * g + n, carry)
            return carry

        for n in range(4):
            partner(n, 0)
        lax.fori_loop(1, QUADS // 4, both, 0)
        coarsen(QUADS - 5, 4)
        partner(QUADS - 1, 0)
        coarsen(QUADS - 1, 1)

        def block(c, carry):
            for half in range(2):
                b = 2 * c + half
                own_map = fown[s, :, pl.ds(pl.multiple_of(256 * b, 256), 256)].astype(F32)
                row = px[s, 0, pl.ds(b, 1), :]
                col = px[s, 1, pl.ds(b, 1), :]
                fy = px[s, 2, pl.ds(b, 1), :]
                fx = px[s, 3, pl.ds(b, 1), :]
                row = jnp.broadcast_to(row.astype(jnp.int32), (16, 256))
                col = jnp.broadcast_to(col, (16, 256)).astype(BF)
                oy = [(row == 2 * row16 + a).astype(F32).astype(BF) for a in range(2)]
                zero = jnp.zeros((16, 256), BF)
                picks = []
                for k in range(6):
                    hit = {}
                    for bb in range(2):
                        for xx in range(2):
                            hit[bb, xx] = col == float(4 * k + 2 * xx + bb)
                    for a in range(2):
                        for bb in range(2):
                            for xx in range(2):
                                picks.append(jnp.where(hit[bb, xx], oy[a], zero))
                choose = jnp.concatenate(picks, axis=0)
                l0 = pl.multiple_of(512 * b + 128, 128)
                taps = _dot(p4[:, pl.ds(l0, 768)], choose)
                gy, gx = 1.0 - fy, 1.0 - fx
                warped = (
                    (gy * gx) * taps[0:64] + (gy * fx) * taps[64:128]
                    + (fy * gx) * taps[128:192] + (fy * fx) * taps[192:256]
                )
                differ = own_map - warped
                mpx[pl.ds(b, 1), :] = jnp.sum(differ * differ, axis=0, keepdims=True) * (1.0 / 64)

            coarse = cown[s, :, pl.ds(pl.multiple_of(128 * c, 128), 128)]
            there = cpt[pl.ds(pl.multiple_of(256 * c, 256), 384), 0:64]
            gram = _dot(there, coarse).reshape(24, 16, 128)
            for k, keep in ((3, 16), (2, 12), (1, 10), (0, 9)):
                step = 1 << k
                gram = jnp.where(x_bit[k][None], gram[step : step + keep], gram[0:keep])
            gram = gram.reshape(144, 128)
            cols = []
            for j in range(9):
                v = gram[16 * j : 16 * j + 16]
                for k in (2, 1, 0):
                    v = jnp.where(y_bit[k], pltpu.roll(v, 16 - (1 << k), 0), v)
                cols.append(v)
            gram = jnp.concatenate(cols, axis=0) * (1.0 / 64)
            obuf[pl.ds(pl.multiple_of(144 * s, 16), 144), pl.ds(pl.multiple_of(128 * c, 128), 128)] = gram.astype(BF)
            return carry

        lax.fori_loop(0, 16, block, 0, unroll=4)

        got = lax.dot_general(
            jnp.concatenate(_split3(mpx[...]), axis=0), perm_ref[...], (((1,), (1,)), ((), ())),
            preferred_element_type=F32,
        )
        got = (got[64:96] + got[32:64]) + got[0:32]
        for x in range(16):
            tbuf[pl.ds(x, 32, stride=16), 0:16] = got[:, 16 * x : 16 * x + 16]
        mis_ref[s] = tbuf[...].T[0:16, :]

        return carry

    lax.fori_loop(0, 2, section, 0)

    for h in range(2):
        flat = _dot(obuf[:, 1024 * h : 1024 * h + 1024], unflat_ref[...])
        for s in range(2):
            for j in range(9):
                r0 = 144 * s + 16 * j
                for y in range(8):
                    cbuf[s, pl.ds(8 * j + y, 9, stride=72), :] = flat[r0 : r0 + 9, 128 * y : 128 * y + 128]
        for s in range(2):
            corr_ref[s, :, :, 128 * h : 128 * h + 128] = cbuf[s].reshape(81, 8, 128).astype(BF)


def _hand_on(a, b, c, x, y, z):
    x[...] = a[...]
    y[...] = b[...]
    z[...] = c[...]


def local(
    section_image, partner_row, base_shift, bilinear_frac, first_kernel, initial_conv_bias,
    second_kernel, second_bias, edge_ends, edge_count, stiffness,
):
    t = _tables()
    vm = pl.BlockSpec(memory_space=pltpu.VMEM)
    sm = pl.BlockSpec(memory_space=pltpu.SMEM)
    hbm = pl.BlockSpec(memory_space=pl.ANY)
    consts = [
        jnp.asarray(t["wsel"], BF), jnp.asarray(t["wconst"], F32), jnp.asarray(t["extra"], BF),
        jnp.asarray(t["cmask"], F32), jnp.asarray(t["home"], F32), jnp.asarray(t["perm"], BF),
        jnp.asarray(t["ep"], BF), jnp.asarray(t["eo"], BF), jnp.asarray(t["unflat"], BF),
    ]
    results = pl.pallas_call(
        _kernel,
        out_shape=(
            jax.ShapeDtypeStruct((2, 81, 8, 256), BF),
            jax.ShapeDtypeStruct((2, 16, 512), F32),
            jax.ShapeDtypeStruct((2, 2, 32), F32),
        ),
        in_specs=[sm, sm] + [vm] * 15 + [hbm] * 3,
        out_specs=(vm, vm, vm),
        scratch_shapes=[
            pltpu.VMEM((2, 96, 1024), BF),
            pltpu.VMEM((2, 64, 1024), BF),
            pltpu.VMEM((2, 8, 128), jnp.int32),
            pltpu.VMEM((2, 8, 128), jnp.int32),
            pltpu.VMEM((2, 32, 1024), BF),
            pltpu.VMEM((2, 32, 1024), BF),
            pltpu.VMEM((8, 256), F32),
            pltpu.VMEM((8, 8, 256), F32),
            pltpu.VMEM((8, 8, 256), F32),
            pltpu.VMEM((8, 256), F32),
            pltpu.VMEM((512, 768), BF),
            pltpu.VMEM((512, 768), BF),
            pltpu.VMEM((1024, 1024), BF),
            pltpu.VMEM((1152, 128), F32),
            pltpu.VMEM((1056, 768), BF),
            pltpu.VMEM((1024, 768), BF),
            pltpu.VMEM((256, PT * 128), BF),
            pltpu.VMEM((PT * 32, 128), BF),
            pltpu.VMEM((288, 2048), BF),
            pltpu.VMEM((2, 648, 128), F32),
            pltpu.VMEM((512, 112), BF),
            pltpu.VMEM((64, 128), F32),
            pltpu.VMEM((512, 128), F32),
            pltpu.VMEM((2, 4, 32, 256), F32),
            pltpu.VMEM((32, 256), F32),
            pltpu.VMEM((2, 64, 8192), BF),
            pltpu.VMEM((2, 64, 2048), BF),
            pltpu.SemaphoreType.DMA((24,)),
            pltpu.SemaphoreType.DMA((24,)),
            pltpu.SemaphoreType.DMA((3,)),
        ],
        compiler_params=pltpu.CompilerParams(
            collective_id=0, has_side_effects=True, vmem_limit_bytes=VMEM_BYTES
        ),
        name="align",
    )(
        partner_row, edge_count.T, section_image, base_shift, bilinear_frac, edge_ends, stiffness,
        first_kernel.T, initial_conv_bias.reshape(1, 64), second_kernel, second_bias.reshape(1, 64), *consts,
    )
    return pl.pallas_call(
        _hand_on,
        out_shape=tuple(jax.ShapeDtypeStruct(r.shape, r.dtype) for r in results),
        in_specs=[vm] * 3,
        out_specs=(vm,) * 3,
        name="hand_on",
    )(*results)


def solution(mesh):
    in_specs = (
        P("sec", "tile", None), P("sec"), P("sec", None, "tile", None), P("sec", None, "tile", None),
        P(), P(), P(), P(), P("sec", None, "tile"), P("sec", "tile"), P("sec", "tile"),
    )
    out_specs = (P("sec", None, "tile", None), P("sec", "tile", None), P("sec", None, "tile"))
    return jax.shard_map(local, mesh=mesh, in_specs=in_specs, out_specs=out_specs, check_vma=False)
```

```python
import jax
import jax.numpy as jnp
import numpy as np
from jax import lax
from jax.experimental import pallas as pl
from jax.experimental.pallas import tpu as pltpu
from jax.sharding import PartitionSpec as P

BF = jnp.bfloat16
F32 = jnp.float32
MESH = pl.DeviceIdType.MESH
BIG = -1e30
VMEM_BYTES = 56 * 1024 * 1024

PT = 132
QUADS = PT // 4


def _tables():
    lane = np.arange(128)
    a, b, xx, yy = lane // 64, (lane // 32) % 2, (lane // 16) % 2, lane % 16
    x4, y2 = 2 * xx + b, 2 * yy + a
    ep = np.zeros((4, 128, 6, 128), np.float32)
    for p in range(6):
        ep[x4, 2 * y2 + 15 + p, p, lane] = 1
    oa, ob, ox, oy = lane // 64, (lane // 32) % 2, (lane // 8) % 4, lane % 8
    x8, y1 = 2 * ox + ob, 2 * oy + oa
    eo = np.zeros((8, 64, 6, 128), np.float32)
    for p in range(6):
        eo[x8, 2 * y1 + 15 + p, p, lane] = 1
    wsel = np.zeros((2, 2, 2, 16, 112), np.float32)
    wconst = np.zeros((2, 2, 2, 1, 112), np.float32)
    for e in range(2):
        for ta in range(2):
            for tb in range(2):
                for u in range(4):
                    for v in range(4):
                        wsel[e, ta, tb, 4 * u + v, (u + 2 * ta) * 16 + 8 * e + 2 * tb + v] = 1
                wconst[e, ta, tb, 0, 96 + 4 * e + 2 * ta + tb] = BIG
    wown = np.zeros((2, 2, 16, 64), np.float32)
    for ta in range(2):
        for tb in range(2):
            for u in range(4):
                for v in range(4):
                    wown[ta, tb, 4 * u + v, (u + 2 * ta) * 8 + 2 * tb + v] = 1
    extra = np.zeros((3, 3, 16, 256), np.float32)
    cmask = np.zeros((3, 3, 8, 128), np.float32)
    for tk in range(3):
        for gk, g in enumerate((0, 1, QUADS - 1)):
            for half in range(2):
                for e in range(2):
                    for ta in range(2):
                        for tb in range(2):
                            col = 4 * (4 * g + 2 * half + e) - 8 + x4 + tb
                            row = y2 - 8 + ta
                            bad = (col < 0) | (col > 511)
                            if tk == 0:
                                bad = bad | (row < 0)
                            if tk == 2:
                                bad = bad | (row > 15)
                            extra[tk, gk, 4 * e + 2 * ta + tb, 128 * half : 128 * half + 128] = bad
            extra[tk, gk, 8:11] = 1
            ccol, crow = 8 * g - 4 + lane // 16, lane % 16 - 4
            bad = (ccol < 0) | (ccol > 255)
            if tk == 0:
                bad = bad | (crow < 0)
            if tk == 2:
                bad = bad | (crow > 7)
            cmask[tk, gk] = np.where(bad, BIG, 0.0)
    src = np.arange(1024)
    unflat = np.zeros((1024, 1024), np.float32)
    unflat[src, (src % 8) * 128 + src // 8] = 1
    l2 = np.arange(256)
    lx = 8 * (l2 // 128) + 2 * ((l2 // 8) % 4) + (l2 // 32) % 2
    ly = 2 * (l2 % 8) + (l2 // 64) % 2
    perm = np.zeros((256, 256), np.float32)
    perm[16 * lx + ly, l2] = 1
    home = np.stack([ly + 8, lx + 4]).astype(np.float32)
    return dict(
        ep=ep.reshape(512, 768),
        eo=eo.reshape(512, 768),
        wsel=wsel.reshape(8, 16, 112),
        wconst=wconst.reshape(8, 1, 112),
        extra=extra,
        wown=wown.reshape(4, 16, 64),
        cmask=cmask,
        unflat=unflat,
        home=home,
        perm=perm,
    )


def _split3(x):
    hi = x.astype(BF)
    rest = x - hi.astype(F32)
    mid = rest.astype(BF)
    low = (rest - mid.astype(F32)).astype(BF)
    return hi, mid, low


def _dot(x, y):
    return jnp.dot(x, y, preferred_element_type=F32)


def _kernel(
    pr_ref, cnt_ref, img_ref, sh_ref, fr_ref, ends_ref, stiff_ref, w1_ref, b1_ref, w2_ref, b2_ref,
    wsel_ref, wown_ref, wconst_ref, extra_ref, cmask_ref, home_ref, perm_ref, ep_hbm, eo_hbm, unflat_hbm,
    corr_ref, mis_ref, force_ref,
    j_ref, i_ref, rbuf, anch, gbuf, pbuf, pstage, ep_ref, eo_ref, unflat_ref,
    tall, qp, qo, p4, cpt, obuf, cbuf, wq, wo, bias2, tbuf, px, mpx, fown, cown,
    send_sem, recv_sem, load_sem,
):
    sec = lax.axis_index("sec")
    tile = lax.axis_index("tile")
    back1 = lax.rem(sec + 15, 16)
    back2 = lax.rem(sec + 14, 16)
    fwd1 = lax.rem(sec + 1, 16)
    fwd2 = lax.rem(sec + 2, 16)
    peers = [lax.rem(tile + r, 8) for r in range(8)]
    has_down = tile < 7
    has_up = tile > 0
    tk = jnp.where(tile == 0, 0, jnp.where(tile == 7, 2, 1))

    barrier = pltpu.get_barrier_semaphore()
    for other in (back1, back2, fwd1, fwd2):
        pl.semaphore_signal(barrier, inc=1, device_id=(other, tile), device_id_type=MESH)
    for r in range(1, 8):
        pl.semaphore_signal(barrier, inc=1, device_id=(sec, peers[r]), device_id_type=MESH)

    loads = [
        pltpu.make_async_copy(src, dst, load_sem.at[k])
        for k, (src, dst) in enumerate(((eo_hbm, eo_ref), (ep_hbm, ep_ref), (unflat_hbm, unflat_ref)))
    ]
    for c in loads:
        c.start()

    rows = [sh_ref[s, k, 0:1, :].astype(F32) + fr_ref[s, k, 0:1, :] for s in range(2) for k in range(2)]
    rows = jnp.concatenate(rows + [jnp.zeros((4, 512), F32)], axis=0)
    x_at = lax.broadcasted_iota(jnp.int32, (512, 256), 0)
    v_at = lax.broadcasted_iota(jnp.int32, (512, 256), 1)
    select = jnp.where(x_at == 16 * (v_at - 32 * tile), 1.0, 0.0).astype(BF)
    got = _dot(jnp.concatenate(_split3(rows), axis=0).astype(BF), select)
    anch[...] = (got[16:24] + got[8:16]) + got[0:8]

    lane = lax.broadcasted_iota(jnp.int32, (64, 112), 1)
    bias1 = jnp.broadcast_to(b1_ref[...], (128, 64)).T[:, 0:112]
    hi, mid, low = (x.astype(F32) for x in _split3(bias1))
    base = (
        jnp.where(lane == 104, hi, 0.0) + jnp.where(lane == 105, mid, 0.0) + jnp.where(lane == 106, low, 0.0)
    )
    for m in range(8):
        spread = lax.dot_general(
            w1_ref[...], wsel_ref[m], (((0,), (0,)), ((), ())), preferred_element_type=F32
        )
        wq[64 * m : 64 * m + 64, :] = (spread + base + wconst_ref[m]).astype(BF)
    for m in range(4):
        spread = lax.dot_general(
            w1_ref[...], wown_ref[m], (((0,), (0,)), ((), ())), preferred_element_type=F32
        )
        wo[64 * m : 64 * m + 64, :] = (spread + base[:, 48:112]).astype(BF)
    bias2[...] = jnp.broadcast_to(b2_ref[...], (128, 64)).T

    lane128 = lax.broadcasted_iota(jnp.int32, (1, 128), 1)
    x_bit = [lax.bitwise_and(lax.shift_right_logical(lane128, 3 + k), 1) == 1 for k in range(4)]
    y_bit = [lax.bitwise_and(lax.shift_right_logical(lane128, k), 1) == 1 for k in range(3)]
    row16 = lax.broadcasted_iota(jnp.int32, (16, 256), 0)

    def pixels(s, carry):
        planes = [sh_ref[s, k].astype(F32) for k in range(2)] + [fr_ref[s, k] for k in range(2)]
        tbuf[:, 0:64] = jnp.concatenate(planes, axis=0).T
        runs = [tbuf[pl.ds(x, 32, stride=16), :] for x in range(16)]
        planes = [jnp.concatenate([r[:, 16 * k : 16 * k + 16] for r in runs], axis=1) for k in range(4)]
        parts = [planes[0].astype(BF), planes[1].astype(BF), *_split3(planes[2]), *_split3(planes[3])]
        got = _dot(jnp.concatenate(parts, axis=0), perm_ref[...])
        px[s, 0] = got[0:32] + home_ref[0:1, :]
        px[s, 1] = got[32:64] + home_ref[1:2, :]
        px[s, 2] = (got[128:160] + got[96:128]) + got[64:96]
        px[s, 3] = (got[224:256] + got[192:224]) + got[160:192]
        return carry

    lax.fori_loop(0, 2, pixels, 0)

    pl.semaphore_wait(barrier, 11)

    def remote(src, dst, k, target):
        return pltpu.make_async_remote_copy(
            src_ref=src, dst_ref=dst, send_sem=send_sem.at[k], recv_sem=recv_sem.at[k],
            device_id=target, device_id_type=MESH,
        )

    near = remote(img_ref, rbuf.at[0], 0, (back1, tile))
    far = remote(img_ref, rbuf.at[1], 1, (back2, tile))
    far.start()
    near.start()
    down_tile = (sec, lax.rem(tile + 1, 8))
    up_tile = (sec, lax.rem(tile + 7, 8))
    own_down = remote(img_ref.at[:, 16:32], i_ref.at[:, 0:16], 2, down_tile)
    own_up = remote(img_ref.at[:, 0:16], i_ref.at[:, 48:64], 3, up_tile)
    pl.when(has_down)(own_down.start)
    pl.when(has_up)(own_up.start)
    anchor_sends = [remote(anch, gbuf.at[r], 4 + r, (sec, peers[r])) for r in range(1, 8)]
    for c in anchor_sends:
        c.start()

    i_ref[:, 16:48, :] = img_ref[...]

    @pl.when(tile == 0)
    def _():
        i_ref[:, 0:16, :] = jnp.zeros((2, 16, 1024), BF)
        j_ref[:, 0:32, :] = jnp.zeros((2, 32, 1024), BF)

    @pl.when(tile == 7)
    def _():
        i_ref[:, 48:64, :] = jnp.zeros((2, 16, 1024), BF)
        j_ref[:, 64:96, :] = jnp.zeros((2, 32, 1024), BF)

    for c in anchor_sends:
        c.wait()
    disp = anch[...]
    for r in range(1, 8):
        disp = disp + gbuf[r]
    vert = lax.broadcasted_iota(jnp.int32, (256, 256), 0)
    slot_at = lax.broadcasted_iota(jnp.int32, (1, 256), 1)
    row_of = lax.broadcasted_iota(jnp.int32, (8, 256), 0)
    parts = jnp.concatenate(_split3(disp), axis=0)
    total = jnp.zeros((8, 256), F32)
    for s in range(2):
        table = (vert == ends_ref[s, 1:2, :]).astype(F32) - (vert == ends_ref[s, 0:1, :]).astype(F32)
        table = table.astype(BF)
        got = _dot(parts, table)
        spread = (got[16:24] + got[8:16]) + got[0:8]
        pull = jnp.where(slot_at < cnt_ref[0, s], stiff_ref[s : s + 1, :], 0.0) * spread
        back = lax.dot_general(
            jnp.concatenate(_split3(pull), axis=0), table, (((1,), (1,)), ((), ())),
            preferred_element_type=F32,
        )
        back = (back[16:24] + back[8:16]) + back[0:8]
        total = total - jnp.where(lax.shift_right_logical(row_of, 1) == s, back, 0.0)
    pstage[...] = total
    force_sends = [remote(pstage, pbuf.at[r], 14 + r, (sec, peers[r])) for r in range(1, 8)]
    for c in force_sends:
        c.start()

    pl.when(has_down)(own_down.wait_send)
    pl.when(has_up)(own_up.wait_send)
    pl.when(has_up)(own_down.wait_recv)
    pl.when(has_down)(own_up.wait_recv)
    loads[0].wait()

    def side_by_side(left, right, more):
        return jnp.concatenate(
            [
                jnp.concatenate([left[:, 128 * p : 128 * p + 128], right[:, 128 * p : 128 * p + 128]], axis=1)
                for p in range(6)
            ]
            + [more],
            axis=0,
        )

    def own(s, carry):
        wide = jnp.concatenate([i_ref[s].astype(F32), jnp.zeros((64, 128), F32)], axis=1)
        turned = jnp.concatenate([pltpu.roll(wide, 1, 1), pltpu.roll(wide, 1151, 1)], axis=0)
        tall[...] = turned.T
        stack = [tall[4 * k : 4 * k + 1024, :].reshape(64, 16, 128)[:, 0:8, :].reshape(512, 128) for k in range(4)]
        stack = jnp.concatenate([x.astype(BF) for x in stack], axis=1)
        qo[...] = _dot(stack, eo_ref[...])

        ones = extra_ref[1, 1].astype(F32)

        def encode(c, carry):
            small = []
            for n in range(4):
                r0 = pl.multiple_of(64 * c + 16 * n, 16)
                patches = side_by_side(qo[pl.ds(r0, 8), :], qo[pl.ds(r0 + 8, 8), :], ones).astype(BF)
                got = jnp.maximum(_dot(wo[0:64, :], patches).astype(BF), 0)
                fown[s, :, pl.ds(pl.multiple_of(1024 * c + 256 * n, 256), 256)] = got
                small += [patches[:, 0:32], patches[:, 128:160]]
            own4 = jnp.maximum(_dot(wo[...], jnp.concatenate(small, axis=1)).astype(BF), 0)
            pre = _dot(w2_ref[...], own4)
            pre = jnp.maximum(pre + jnp.concatenate([bias2[...]] * 2, axis=1), 0.0)
            cown[s, :, pl.ds(pl.multiple_of(256 * c, 256), 256)] = pre.astype(BF)
            return carry

        return lax.fori_loop(0, 8, encode, carry, unroll=8)

    own(0, 0)

    near.wait()
    far.wait()
    for s in range(2):
        p = pr_ref[s]
        which = jnp.where(lax.shift_right_logical(p, 1) == fwd1, 0, 1)
        slot = lax.bitwise_and(p, 1)
        j_ref[s, 32:64, :] = rbuf[which, slot]
    part_down = remote(j_ref.at[:, 32:64], j_ref.at[:, 0:32], 12, down_tile)
    part_up = remote(j_ref.at[:, 32:64], j_ref.at[:, 64:96], 13, up_tile)
    pl.when(has_down)(part_down.start)
    pl.when(has_up)(part_up.start)

    own(1, 0)

    for c in force_sends:
        c.wait()
    total = pstage[...]
    for r in range(1, 8):
        total = total + pbuf[r]
    turned = pltpu.roll(total, lax.rem(256 - 32 * tile, 256), 1)
    for s in range(2):
        force_ref[s] = turned[2 * s : 2 * s + 2, 0:32]

    pl.when(has_down)(part_down.wait_send)
    pl.when(has_up)(part_up.wait_send)
    pl.when(has_up)(part_down.wait_recv)
    pl.when(has_down)(part_up.wait_recv)
    loads[1].wait()
    loads[2].wait()

    def section(s, carry):
        wide = jnp.concatenate([j_ref[s].astype(F32), jnp.zeros((96, 128), F32)], axis=1)
        turned = jnp.concatenate([pltpu.roll(wide, 17, 1), jnp.zeros((32, 1152), F32)], axis=0)
        tall[...] = turned.T
        stack = jnp.concatenate([tall[2 * k : 2 * k + 1056, :].astype(BF) for k in range(4)], axis=1)
        qp[...] = _dot(stack, ep_ref[...]).astype(BF)

        def partner(g, carry):
            r0 = pl.multiple_of(32 * g, 32)
            kind = jnp.where(g == 0, 0, jnp.where(g == QUADS - 1, 2, 1))
            patches = side_by_side(qp[pl.ds(r0, 16), :], qp[pl.ds(r0 + 16, 16), :], extra_ref[tk, kind])
            got = jnp.maximum(_dot(wq[...], patches).astype(BF), 0)
            l0 = pl.multiple_of(512 * g, 512)
            p4[:, pl.ds(l0, 512)] = jnp.concatenate(
                [got[0:256, 0:128], got[256:512, 0:128], got[0:256, 128:256], got[256:512, 128:256]], axis=1
            )
            return carry

        def coarsen(q, count):
            tiles = p4[:, pl.ds(pl.multiple_of(512 * q, 512), 512 * count)]
            tiles = jnp.concatenate([tiles[:, 128 * k : 128 * k + 32] for k in range(4 * count)], axis=1)
            pre = _dot(w2_ref[...], tiles)
            for n in range(count):
                kind = jnp.where(q + n == 0, 0, jnp.where(q + n == QUADS - 1, 2, 1))
                coarse = pre[:, 128 * n : 128 * n + 128] + bias2[...] + cmask_ref[tk, kind][0:1, :]
                coarse = jnp.maximum(coarse, 0.0).astype(BF).astype(F32)
                cpt[pl.ds(pl.multiple_of(128 * (q + n), 128), 128), 0:64] = coarse.T.astype(BF)

        def both(g, carry):
            coarsen(4 * g - 4, 4)
            for n in range(4):
                partner(4 * g + n, carry)
            return carry

        for n in range(4):
            partner(n, 0)
        lax.fori_loop(1, QUADS // 4, both, 0, unroll=7)
        coarsen(QUADS - 5, 4)
        partner(QUADS - 1, 0)
        coarsen(QUADS - 1, 1)

        def block(c, carry):
            for half in range(2):
                b = 2 * c + half
                own_map = fown[s, :, pl.ds(pl.multiple_of(256 * b, 256), 256)].astype(F32)
                row = px[s, 0, pl.ds(b, 1), :]
                col = px[s, 1, pl.ds(b, 1), :]
                fy = px[s, 2, pl.ds(b, 1), :]
                fx = px[s, 3, pl.ds(b, 1), :]
                row = jnp.broadcast_to(row.astype(jnp.int32), (16, 256))
                col = jnp.broadcast_to(col, (16, 256)).astype(BF)
                oy = [(row == 2 * row16 + a).astype(F32).astype(BF) for a in range(2)]
                zero = jnp.zeros((16, 256), BF)
                picks = []
                for k in range(6):
                    hit = {}
                    for bb in range(2):
                        for xx in range(2):
                            hit[bb, xx] = col == float(4 * k + 2 * xx + bb)
                    for a in range(2):
                        for bb in range(2):
                            for xx in range(2):
                                picks.append(jnp.where(hit[bb, xx], oy[a], zero))
                choose = jnp.concatenate(picks, axis=0)
                l0 = pl.multiple_of(512 * b + 128, 128)
                taps = _dot(p4[:, pl.ds(l0, 768)], choose)
                gy, gx = 1.0 - fy, 1.0 - fx
                warped = (
                    (gy * gx) * taps[0:64] + (gy * fx) * taps[64:128]
                    + (fy * gx) * taps[128:192] + (fy * fx) * taps[192:256]
                )
                differ = own_map - warped
                mpx[pl.ds(b, 1), :] = jnp.sum(differ * differ, axis=0, keepdims=True) * (1.0 / 64)

            coarse = cown[s, :, pl.ds(pl.multiple_of(128 * c, 128), 128)]
            there = cpt[pl.ds(pl.multiple_of(256 * c, 256), 384), 0:64]
            gram = _dot(there, coarse).reshape(24, 16, 128)
            for k, keep in ((3, 16), (2, 12), (1, 10), (0, 9)):
                step = 1 << k
                gram = jnp.where(x_bit[k][None], gram[step : step + keep], gram[0:keep])
            gram = gram.reshape(144, 128)
            cols = []
            for j in range(9):
                v = gram[16 * j : 16 * j + 16]
                for k in (2, 1, 0):
                    v = jnp.where(y_bit[k], pltpu.roll(v, 16 - (1 << k), 0), v)
                cols.append(v)
            gram = jnp.concatenate(cols, axis=0) * (1.0 / 64)
            obuf[pl.ds(pl.multiple_of(144 * s, 16), 144), pl.ds(pl.multiple_of(128 * c, 128), 128)] = gram.astype(BF)
            return carry

        lax.fori_loop(0, 16, block, 0, unroll=4)

        got = lax.dot_general(
            jnp.concatenate(_split3(mpx[...]), axis=0), perm_ref[...], (((1,), (1,)), ((), ())),
            preferred_element_type=F32,
        )
        got = (got[64:96] + got[32:64]) + got[0:32]
        for x in range(16):
            tbuf[pl.ds(x, 32, stride=16), 0:16] = got[:, 16 * x : 16 * x + 16]
        mis_ref[s] = tbuf[...].T[0:16, :]

        return carry

    lax.fori_loop(0, 2, section, 0)

    for h in range(2):
        flat = _dot(obuf[:, 1024 * h : 1024 * h + 1024], unflat_ref[...])
        for s in range(2):
            for j in range(9):
                r0 = 144 * s + 16 * j
                for y in range(8):
                    cbuf[s, pl.ds(8 * j + y, 9, stride=72), :] = flat[r0 : r0 + 9, 128 * y : 128 * y + 128]
        for s in range(2):
            corr_ref[s, :, :, 128 * h : 128 * h + 128] = cbuf[s].reshape(81, 8, 128).astype(BF)


def _hand_on(a, b, c, x, y, z):
    x[...] = a[...]
    y[...] = b[...]
    z[...] = c[...]


def local(
    section_image, partner_row, base_shift, bilinear_frac, first_kernel, initial_conv_bias,
    second_kernel, second_bias, edge_ends, edge_count, stiffness,
):
    t = _tables()
    vm = pl.BlockSpec(memory_space=pltpu.VMEM)
    sm = pl.BlockSpec(memory_space=pltpu.SMEM)
    hbm = pl.BlockSpec(memory_space=pl.ANY)
    consts = [
        jnp.asarray(t["wsel"], BF), jnp.asarray(t["wown"], BF), jnp.asarray(t["wconst"], F32), jnp.asarray(t["extra"], BF),
        jnp.asarray(t["cmask"], F32), jnp.asarray(t["home"], F32), jnp.asarray(t["perm"], BF),
        jnp.asarray(t["ep"], BF), jnp.asarray(t["eo"], BF), jnp.asarray(t["unflat"], BF),
    ]
    results = pl.pallas_call(
        _kernel,
        out_shape=(
            jax.ShapeDtypeStruct((2, 81, 8, 256), BF),
            jax.ShapeDtypeStruct((2, 16, 512), F32),
            jax.ShapeDtypeStruct((2, 2, 32), F32),
        ),
        in_specs=[sm, sm] + [vm] * 16 + [hbm] * 3,
        out_specs=(vm, vm, vm),
        scratch_shapes=[
            pltpu.VMEM((2, 96, 1024), BF),
            pltpu.VMEM((2, 64, 1024), BF),
            pltpu.VMEM((2, 2, 32, 1024), BF),
            pltpu.VMEM((8, 256), F32),
            pltpu.VMEM((8, 8, 256), F32),
            pltpu.VMEM((8, 8, 256), F32),
            pltpu.VMEM((8, 256), F32),
            pltpu.VMEM((512, 768), BF),
            pltpu.VMEM((512, 768), BF),
            pltpu.VMEM((1024, 1024), BF),
            pltpu.VMEM((1152, 128), F32),
            pltpu.VMEM((1056, 768), BF),
            pltpu.VMEM((512, 768), F32),
            pltpu.VMEM((256, PT * 128), BF),
            pltpu.VMEM((PT * 32, 128), BF),
            pltpu.VMEM((288, 2048), BF),
            pltpu.VMEM((2, 648, 128), F32),
            pltpu.VMEM((512, 112), BF),
            pltpu.VMEM((256, 64), BF),
            pltpu.VMEM((64, 128), F32),
            pltpu.VMEM((512, 128), F32),
            pltpu.VMEM((2, 4, 32, 256), F32),
            pltpu.VMEM((32, 256), F32),
            pltpu.VMEM((2, 64, 8192), BF),
            pltpu.VMEM((2, 64, 2048), BF),
            pltpu.SemaphoreType.DMA((22,)),
            pltpu.SemaphoreType.DMA((22,)),
            pltpu.SemaphoreType.DMA((3,)),
        ],
        compiler_params=pltpu.CompilerParams(
            collective_id=0, has_side_effects=True, vmem_limit_bytes=VMEM_BYTES
        ),
        name="align",
    )(
        partner_row, edge_count.T, section_image, base_shift, bilinear_frac, edge_ends, stiffness,
        first_kernel.T, initial_conv_bias.reshape(1, 64), second_kernel, second_bias.reshape(1, 64), *consts,
    )
    return pl.pallas_call(
        _hand_on,
        out_shape=tuple(jax.ShapeDtypeStruct(r.shape, r.dtype) for r in results),
        in_specs=[vm] * 3,
        out_specs=(vm,) * 3,
        name="hand_on",
    )(*results)


def solution(mesh):
    in_specs = (
        P("sec", "tile", None), P("sec"), P("sec", None, "tile", None), P("sec", None, "tile", None),
        P(), P(), P(), P(), P("sec", None, "tile"), P("sec", "tile"), P("sec", "tile"),
    )
    out_specs = (P("sec", None, "tile", None), P("sec", "tile", None), P("sec", None, "tile"))
    return jax.shard_map(local, mesh=mesh, in_specs=in_specs, out_specs=out_specs, check_vma=False)
```

```python
import jax
import jax.numpy as jnp
import numpy as np
from jax import lax
from jax.experimental import pallas as pl
from jax.experimental.pallas import tpu as pltpu
from jax.sharding import PartitionSpec as P

BF = jnp.bfloat16
F32 = jnp.float32
MESH = pl.DeviceIdType.MESH
BIG = -1e30
VMEM_BYTES = 56 * 1024 * 1024

PT = 132
QUADS = PT // 4


def _tables():
    lane = np.arange(128)
    a, b, xx, yy = lane // 64, (lane // 32) % 2, (lane // 16) % 2, lane % 16
    x4, y2 = 2 * xx + b, 2 * yy + a
    ep = np.zeros((4, 128, 6, 128), np.float32)
    for p in range(6):
        ep[x4, 2 * y2 + 15 + p, p, lane] = 1
    oa, ob, ox, oy = lane // 64, (lane // 32) % 2, (lane // 8) % 4, lane % 8
    x8, y1 = 2 * ox + ob, 2 * oy + oa
    eo = np.zeros((8, 64, 6, 128), np.float32)
    for p in range(6):
        eo[x8, 2 * y1 + 15 + p, p, lane] = 1
    wsel = np.zeros((2, 2, 2, 16, 112), np.float32)
    wconst = np.zeros((2, 2, 2, 1, 112), np.float32)
    for e in range(2):
        for ta in range(2):
            for tb in range(2):
                for u in range(4):
                    for v in range(4):
                        wsel[e, ta, tb, 4 * u + v, (u + 2 * ta) * 16 + 8 * e + 2 * tb + v] = 1
                wconst[e, ta, tb, 0, 96 + 4 * e + 2 * ta + tb] = BIG
    wown = np.zeros((2, 2, 16, 64), np.float32)
    for ta in range(2):
        for tb in range(2):
            for u in range(4):
                for v in range(4):
                    wown[ta, tb, 4 * u + v, (u + 2 * ta) * 8 + 2 * tb + v] = 1
    extra = np.zeros((3, 3, 16, 256), np.float32)
    cmask = np.zeros((3, 3, 8, 128), np.float32)
    for tk in range(3):
        for gk, g in enumerate((0, 1, QUADS - 1)):
            for half in range(2):
                for e in range(2):
                    for ta in range(2):
                        for tb in range(2):
                            col = 4 * (4 * g + 2 * half + e) - 8 + x4 + tb
                            row = y2 - 8 + ta
                            bad = (col < 0) | (col > 511)
                            if tk == 0:
                                bad = bad | (row < 0)
                            if tk == 2:
                                bad = bad | (row > 15)
                            extra[tk, gk, 4 * e + 2 * ta + tb, 128 * half : 128 * half + 128] = bad
            extra[tk, gk, 8:11] = 1
            ccol, crow = 8 * g - 4 + lane // 16, lane % 16 - 4
            bad = (ccol < 0) | (ccol > 255)
            if tk == 0:
                bad = bad | (crow < 0)
            if tk == 2:
                bad = bad | (crow > 7)
            cmask[tk, gk] = np.where(bad, BIG, 0.0)
    src = np.arange(1024)
    unflat = np.zeros((1024, 1024), np.float32)
    unflat[src, (src % 8) * 128 + src // 8] = 1
    l2 = np.arange(256)
    lx = 8 * (l2 // 128) + 2 * ((l2 // 8) % 4) + (l2 // 32) % 2
    ly = 2 * (l2 % 8) + (l2 // 64) % 2
    perm = np.zeros((256, 256), np.float32)
    perm[16 * lx + ly, l2] = 1
    home = np.stack([ly + 8, lx + 4]).astype(np.float32)
    return dict(
        ep=ep.reshape(512, 768),
        eo=eo.reshape(512, 768),
        wsel=wsel.reshape(8, 16, 112),
        wconst=wconst.reshape(8, 1, 112),
        extra=extra,
        wown=wown.reshape(4, 16, 64),
        cmask=cmask,
        unflat=unflat,
        home=home,
        perm=perm,
    )


def _split3(x):
    hi = x.astype(BF)
    rest = x - hi.astype(F32)
    mid = rest.astype(BF)
    low = (rest - mid.astype(F32)).astype(BF)
    return hi, mid, low


def _dot(x, y):
    return jnp.dot(x, y, preferred_element_type=F32)


def _kernel(
    pr_ref, cnt_ref, img_ref, sh_ref, fr_ref, ends_ref, stiff_ref, w1_ref, b1_ref, w2_ref, b2_ref,
    wsel_ref, wown_ref, wconst_ref, extra_ref, cmask_ref, home_ref, perm_ref, ep_hbm, eo_hbm, unflat_hbm,
    corr_ref, mis_ref, force_ref,
    j_ref, i_ref, rbuf, anch, gbuf, pbuf, pstage, ep_ref, eo_ref, unflat_ref,
    tall, qp, qo, p4, cpt, obuf, cbuf, wq, wo, bias2, tbuf, px, mpx, fown, cown,
    send_sem, recv_sem, load_sem,
):
    sec = lax.axis_index("sec")
    tile = lax.axis_index("tile")
    back1 = lax.rem(sec + 15, 16)
    back2 = lax.rem(sec + 14, 16)
    fwd1 = lax.rem(sec + 1, 16)
    fwd2 = lax.rem(sec + 2, 16)
    peers = [lax.rem(tile + r, 8) for r in range(8)]
    has_down = tile < 7
    has_up = tile > 0
    tk = jnp.where(tile == 0, 0, jnp.where(tile == 7, 2, 1))

    barrier = pltpu.get_barrier_semaphore()
    for other in (back1, back2, fwd1, fwd2):
        pl.semaphore_signal(barrier, inc=1, device_id=(other, tile), device_id_type=MESH)
    for r in range(1, 8):
        pl.semaphore_signal(barrier, inc=1, device_id=(sec, peers[r]), device_id_type=MESH)

    loads = [
        pltpu.make_async_copy(src, dst, load_sem.at[k])
        for k, (src, dst) in enumerate(((eo_hbm, eo_ref), (ep_hbm, ep_ref), (unflat_hbm, unflat_ref)))
    ]
    for c in loads:
        c.start()

    rows = [sh_ref[s, k, 0:1, :].astype(F32) + fr_ref[s, k, 0:1, :] for s in range(2) for k in range(2)]
    rows = jnp.concatenate(rows + [jnp.zeros((4, 512), F32)], axis=0)
    x_at = lax.broadcasted_iota(jnp.int32, (512, 256), 0)
    v_at = lax.broadcasted_iota(jnp.int32, (512, 256), 1)
    select = jnp.where(x_at == 16 * (v_at - 32 * tile), 1.0, 0.0).astype(BF)
    got = _dot(jnp.concatenate(_split3(rows), axis=0).astype(BF), select)
    anch[...] = (got[16:24] + got[8:16]) + got[0:8]

    lane = lax.broadcasted_iota(jnp.int32, (64, 112), 1)
    bias1 = jnp.broadcast_to(b1_ref[...], (128, 64)).T[:, 0:112]
    hi, mid, low = (x.astype(F32) for x in _split3(bias1))
    base = (
        jnp.where(lane == 104, hi, 0.0) + jnp.where(lane == 105, mid, 0.0) + jnp.where(lane == 106, low, 0.0)
    )
    for m in range(8):
        spread = lax.dot_general(
            w1_ref[...], wsel_ref[m], (((0,), (0,)), ((), ())), preferred_element_type=F32
        )
        wq[64 * m : 64 * m + 64, :] = (spread + base + wconst_ref[m]).astype(BF)
    for m in range(4):
        spread = lax.dot_general(
            w1_ref[...], wown_ref[m], (((0,), (0,)), ((), ())), preferred_element_type=F32
        )
        wo[64 * m : 64 * m + 64, :] = (spread + base[:, 48:112]).astype(BF)
    bias2[...] = jnp.broadcast_to(b2_ref[...], (128, 64)).T

    lane128 = lax.broadcasted_iota(jnp.int32, (1, 128), 1)
    x_bit = [lax.bitwise_and(lax.shift_right_logical(lane128, 3 + k), 1) == 1 for k in range(4)]
    y_bit = [lax.bitwise_and(lax.shift_right_logical(lane128, k), 1) == 1 for k in range(3)]
    row16 = lax.broadcasted_iota(jnp.int32, (16, 256), 0)

    def pixels(s, carry):
        planes = [sh_ref[s, k].astype(F32) for k in range(2)] + [fr_ref[s, k] for k in range(2)]
        tbuf[:, 0:64] = jnp.concatenate(planes, axis=0).T
        runs = [tbuf[pl.ds(x, 32, stride=16), :] for x in range(16)]
        planes = [jnp.concatenate([r[:, 16 * k : 16 * k + 16] for r in runs], axis=1) for k in range(4)]
        parts = [planes[0].astype(BF), planes[1].astype(BF), *_split3(planes[2]), *_split3(planes[3])]
        got = _dot(jnp.concatenate(parts, axis=0), perm_ref[...])
        px[s, 0] = got[0:32] + home_ref[0:1, :]
        px[s, 1] = got[32:64] + home_ref[1:2, :]
        px[s, 2] = (got[128:160] + got[96:128]) + got[64:96]
        px[s, 3] = (got[224:256] + got[192:224]) + got[160:192]
        return carry

    lax.fori_loop(0, 2, pixels, 0)

    pl.semaphore_wait(barrier, 11)

    def remote(src, dst, k, target):
        return pltpu.make_async_remote_copy(
            src_ref=src, dst_ref=dst, send_sem=send_sem.at[k], recv_sem=recv_sem.at[k],
            device_id=target, device_id_type=MESH,
        )

    near = remote(img_ref, rbuf.at[0], 0, (back1, tile))
    far = remote(img_ref, rbuf.at[1], 1, (back2, tile))
    far.start()
    near.start()
    down_tile = (sec, lax.rem(tile + 1, 8))
    up_tile = (sec, lax.rem(tile + 7, 8))
    own_down = remote(img_ref.at[:, 16:32], i_ref.at[:, 0:16], 2, down_tile)
    own_up = remote(img_ref.at[:, 0:16], i_ref.at[:, 48:64], 3, up_tile)
    pl.when(has_down)(own_down.start)
    pl.when(has_up)(own_up.start)
    anchor_sends = [remote(anch, gbuf.at[r], 4 + r, (sec, peers[r])) for r in range(1, 8)]
    for c in anchor_sends:
        c.start()

    i_ref[:, 16:48, :] = img_ref[...]

    @pl.when(tile == 0)
    def _():
        i_ref[:, 0:16, :] = jnp.zeros((2, 16, 1024), BF)
        j_ref[:, 0:32, :] = jnp.zeros((2, 32, 1024), BF)

    @pl.when(tile == 7)
    def _():
        i_ref[:, 48:64, :] = jnp.zeros((2, 16, 1024), BF)
        j_ref[:, 64:96, :] = jnp.zeros((2, 32, 1024), BF)

    for c in anchor_sends:
        c.wait()
    disp = anch[...]
    for r in range(1, 8):
        disp = disp + gbuf[r]
    vert = lax.broadcasted_iota(jnp.int32, (256, 256), 0)
    slot_at = lax.broadcasted_iota(jnp.int32, (1, 256), 1)
    row_of = lax.broadcasted_iota(jnp.int32, (8, 256), 0)
    parts = jnp.concatenate(_split3(disp), axis=0)
    total = jnp.zeros((8, 256), F32)
    for s in range(2):
        table = (vert == ends_ref[s, 1:2, :]).astype(F32) - (vert == ends_ref[s, 0:1, :]).astype(F32)
        table = table.astype(BF)
        got = _dot(parts, table)
        spread = (got[16:24] + got[8:16]) + got[0:8]
        pull = jnp.where(slot_at < cnt_ref[0, s], stiff_ref[s : s + 1, :], 0.0) * spread
        back = lax.dot_general(
            jnp.concatenate(_split3(pull), axis=0), table, (((1,), (1,)), ((), ())),
            preferred_element_type=F32,
        )
        back = (back[16:24] + back[8:16]) + back[0:8]
        total = total - jnp.where(lax.shift_right_logical(row_of, 1) == s, back, 0.0)
    pstage[...] = total
    force_sends = [remote(pstage, pbuf.at[r], 14 + r, (sec, peers[r])) for r in range(1, 8)]
    for c in force_sends:
        c.start()

    pl.when(has_down)(own_down.wait_send)
    pl.when(has_up)(own_up.wait_send)
    pl.when(has_up)(own_down.wait_recv)
    pl.when(has_down)(own_up.wait_recv)
    loads[0].wait()

    def side_by_side(left, right, more):
        return jnp.concatenate(
            [
                jnp.concatenate([left[:, 128 * p : 128 * p + 128], right[:, 128 * p : 128 * p + 128]], axis=1)
                for p in range(6)
            ]
            + [more],
            axis=0,
        )

    def own(s, carry):
        wide = jnp.concatenate([i_ref[s].astype(F32), jnp.zeros((64, 128), F32)], axis=1)
        turned = jnp.concatenate([pltpu.roll(wide, 1, 1), pltpu.roll(wide, 1151, 1)], axis=0)
        tall[...] = turned.T
        stack = [tall[4 * k : 4 * k + 1024, :].reshape(64, 16, 128)[:, 0:8, :].reshape(512, 128) for k in range(4)]
        stack = jnp.concatenate([x.astype(BF) for x in stack], axis=1)
        qo[...] = _dot(stack, eo_ref[...])

        ones = extra_ref[1, 1].astype(F32)

        def encode(c, carry):
            small = []
            for n in range(4):
                r0 = pl.multiple_of(64 * c + 16 * n, 16)
                patches = side_by_side(qo[pl.ds(r0, 8), :], qo[pl.ds(r0 + 8, 8), :], ones).astype(BF)
                got = jnp.maximum(_dot(wo[0:64, :], patches).astype(BF), 0)
                fown[s, :, pl.ds(pl.multiple_of(1024 * c + 256 * n, 256), 256)] = got
                small += [patches[:, 0:32], patches[:, 128:160]]
            own4 = jnp.maximum(_dot(wo[...], jnp.concatenate(small, axis=1)).astype(BF), 0)
            pre = _dot(w2_ref[...], own4)
            pre = jnp.maximum(pre + jnp.concatenate([bias2[...]] * 2, axis=1), 0.0)
            cown[s, :, pl.ds(pl.multiple_of(256 * c, 256), 256)] = pre.astype(BF)
            return carry

        return lax.fori_loop(0, 8, encode, carry, unroll=8)

    own(0, 0)

    near.wait()
    far.wait()
    for s in range(2):
        p = pr_ref[s]
        which = jnp.where(lax.shift_right_logical(p, 1) == fwd1, 0, 1)
        slot = lax.bitwise_and(p, 1)
        j_ref[s, 32:64, :] = rbuf[which, slot]
    part_down = remote(j_ref.at[:, 32:64], j_ref.at[:, 0:32], 12, down_tile)
    part_up = remote(j_ref.at[:, 32:64], j_ref.at[:, 64:96], 13, up_tile)
    pl.when(has_down)(part_down.start)
    pl.when(has_up)(part_up.start)

    own(1, 0)

    for c in force_sends:
        c.wait()
    total = pstage[...]
    for r in range(1, 8):
        total = total + pbuf[r]
    turned = pltpu.roll(total, lax.rem(256 - 32 * tile, 256), 1)
    for s in range(2):
        force_ref[s] = turned[2 * s : 2 * s + 2, 0:32]

    pl.when(has_down)(part_down.wait_send)
    pl.when(has_up)(part_up.wait_send)
    pl.when(has_up)(part_down.wait_recv)
    pl.when(has_down)(part_up.wait_recv)
    loads[1].wait()
    loads[2].wait()

    def section(s, carry):
        wide = jnp.concatenate([j_ref[s].astype(F32), jnp.zeros((96, 128), F32)], axis=1)
        turned = jnp.concatenate([pltpu.roll(wide, 17, 1), jnp.zeros((32, 1152), F32)], axis=0)
        tall[...] = turned.T
        stack = jnp.concatenate([tall[2 * k : 2 * k + 1056, :].astype(BF) for k in range(4)], axis=1)
        qp[...] = _dot(stack, ep_ref[...]).astype(BF)

        def partner(g, carry):
            r0 = pl.multiple_of(32 * g, 32)
            kind = jnp.where(g == 0, 0, jnp.where(g == QUADS - 1, 2, 1))
            patches = side_by_side(qp[pl.ds(r0, 16), :], qp[pl.ds(r0 + 16, 16), :], extra_ref[tk, kind])
            got = jnp.maximum(_dot(wq[...], patches).astype(BF), 0)
            l0 = pl.multiple_of(512 * g, 512)
            p4[:, pl.ds(l0, 512)] = jnp.concatenate(
                [got[0:256, 0:128], got[256:512, 0:128], got[0:256, 128:256], got[256:512, 128:256]], axis=1
            )
            return carry

        def coarsen(q, count):
            tiles = p4[:, pl.ds(pl.multiple_of(512 * q, 512), 512 * count)]
            tiles = jnp.concatenate([tiles[:, 128 * k : 128 * k + 32] for k in range(4 * count)], axis=1)
            pre = _dot(w2_ref[...], tiles)
            for n in range(count):
                kind = jnp.where(q + n == 0, 0, jnp.where(q + n == QUADS - 1, 2, 1))
                coarse = pre[:, 128 * n : 128 * n + 128] + bias2[...] + cmask_ref[tk, kind][0:1, :]
                coarse = jnp.maximum(coarse, 0.0).astype(BF).astype(F32)
                cpt[pl.ds(pl.multiple_of(128 * (q + n), 128), 128), 0:64] = coarse.T.astype(BF)

        def both(g, carry):
            coarsen(4 * g - 4, 4)
            for n in range(4):
                partner(4 * g + n, carry)
            return carry

        for n in range(4):
            partner(n, 0)
        lax.fori_loop(1, QUADS // 4, both, 0, unroll=7)
        coarsen(QUADS - 5, 4)
        partner(QUADS - 1, 0)
        coarsen(QUADS - 1, 1)

        def block(c, carry):
            for half in range(2):
                b = 2 * c + half
                own_map = fown[s, :, pl.ds(pl.multiple_of(256 * b, 256), 256)].astype(F32)
                row = px[s, 0, pl.ds(b, 1), :]
                col = px[s, 1, pl.ds(b, 1), :]
                fy = px[s, 2, pl.ds(b, 1), :]
                fx = px[s, 3, pl.ds(b, 1), :]
                row = jnp.broadcast_to(row.astype(jnp.int32), (16, 256))
                col = jnp.broadcast_to(col, (16, 256)).astype(BF)
                oy = [(row == 2 * row16 + a).astype(F32).astype(BF) for a in range(2)]
                zero = jnp.zeros((16, 256), BF)
                picks = []
                for k in range(6):
                    hit = {}
                    for bb in range(2):
                        for xx in range(2):
                            hit[bb, xx] = col == float(4 * k + 2 * xx + bb)
                    for a in range(2):
                        for bb in range(2):
                            for xx in range(2):
                                picks.append(jnp.where(hit[bb, xx], oy[a], zero))
                choose = jnp.concatenate(picks, axis=0)
                l0 = pl.multiple_of(512 * b + 128, 128)
                taps = _dot(p4[:, pl.ds(l0, 768)], choose)
                gy, gx = 1.0 - fy, 1.0 - fx
                warped = (
                    (gy * gx) * taps[0:64] + (gy * fx) * taps[64:128]
                    + (fy * gx) * taps[128:192] + (fy * fx) * taps[192:256]
                )
                differ = own_map - warped
                mpx[pl.ds(b, 1), :] = jnp.sum(differ * differ, axis=0, keepdims=True) * (1.0 / 64)

            coarse = cown[s, :, pl.ds(pl.multiple_of(128 * c, 128), 128)]
            there = cpt[pl.ds(pl.multiple_of(256 * c, 256), 384), 0:64]
            gram = _dot(there, coarse).reshape(24, 16, 128)
            for k, keep in ((3, 16), (2, 12), (1, 10), (0, 9)):
                step = 1 << k
                gram = jnp.where(x_bit[k][None], gram[step : step + keep], gram[0:keep])
            gram = gram.reshape(144, 128)
            cols = []
            for j in range(9):
                v = gram[16 * j : 16 * j + 16]
                for k in (2, 1, 0):
                    v = jnp.where(y_bit[k], pltpu.roll(v, 16 - (1 << k), 0), v)
                cols.append(v)
            gram = jnp.concatenate(cols, axis=0) * (1.0 / 64)
            obuf[pl.ds(pl.multiple_of(144 * s, 16), 144), pl.ds(pl.multiple_of(128 * c, 128), 128)] = gram.astype(BF)
            return carry

        lax.fori_loop(0, 16, block, 0, unroll=16)

        got = lax.dot_general(
            jnp.concatenate(_split3(mpx[...]), axis=0), perm_ref[...], (((1,), (1,)), ((), ())),
            preferred_element_type=F32,
        )
        got = (got[64:96] + got[32:64]) + got[0:32]
        for x in range(16):
            tbuf[pl.ds(x, 32, stride=16), 0:16] = got[:, 16 * x : 16 * x + 16]
        mis_ref[s] = tbuf[...].T[0:16, :]

        return carry

    lax.fori_loop(0, 2, section, 0)

    for h in range(2):
        flat = _dot(obuf[:, 1024 * h : 1024 * h + 1024], unflat_ref[...])
        for s in range(2):
            for j in range(9):
                r0 = 144 * s + 16 * j
                for y in range(8):
                    cbuf[s, pl.ds(8 * j + y, 9, stride=72), :] = flat[r0 : r0 + 9, 128 * y : 128 * y + 128]
        for s in range(2):
            corr_ref[s, :, :, 128 * h : 128 * h + 128] = cbuf[s].reshape(81, 8, 128).astype(BF)


def _hand_on(a, b, c, x, y, z):
    x[...] = a[...]
    y[...] = b[...]
    z[...] = c[...]


def local(
    section_image, partner_row, base_shift, bilinear_frac, first_kernel, initial_conv_bias,
    second_kernel, second_bias, edge_ends, edge_count, stiffness,
):
    t = _tables()
    vm = pl.BlockSpec(memory_space=pltpu.VMEM)
    sm = pl.BlockSpec(memory_space=pltpu.SMEM)
    hbm = pl.BlockSpec(memory_space=pl.ANY)
    consts = [
        jnp.asarray(t["wsel"], BF), jnp.asarray(t["wown"], BF), jnp.asarray(t["wconst"], F32), jnp.asarray(t["extra"], BF),
        jnp.asarray(t["cmask"], F32), jnp.asarray(t["home"], F32), jnp.asarray(t["perm"], BF),
        jnp.asarray(t["ep"], BF), jnp.asarray(t["eo"], BF), jnp.asarray(t["unflat"], BF),
    ]
    results = pl.pallas_call(
        _kernel,
        out_shape=(
            jax.ShapeDtypeStruct((2, 81, 8, 256), BF),
            jax.ShapeDtypeStruct((2, 16, 512), F32),
            jax.ShapeDtypeStruct((2, 2, 32), F32),
        ),
        in_specs=[sm, sm] + [vm] * 16 + [hbm] * 3,
        out_specs=(vm, vm, vm),
        scratch_shapes=[
            pltpu.VMEM((2, 96, 1024), BF),
            pltpu.VMEM((2, 64, 1024), BF),
            pltpu.VMEM((2, 2, 32, 1024), BF),
            pltpu.VMEM((8, 256), F32),
            pltpu.VMEM((8, 8, 256), F32),
            pltpu.VMEM((8, 8, 256), F32),
            pltpu.VMEM((8, 256), F32),
            pltpu.VMEM((512, 768), BF),
            pltpu.VMEM((512, 768), BF),
            pltpu.VMEM((1024, 1024), BF),
            pltpu.VMEM((1152, 128), F32),
            pltpu.VMEM((1056, 768), BF),
            pltpu.VMEM((512, 768), F32),
            pltpu.VMEM((256, PT * 128), BF),
            pltpu.VMEM((PT * 32, 128), BF),
            pltpu.VMEM((288, 2048), BF),
            pltpu.VMEM((2, 648, 128), F32),
            pltpu.VMEM((512, 112), BF),
            pltpu.VMEM((256, 64), BF),
            pltpu.VMEM((64, 128), F32),
            pltpu.VMEM((512, 128), F32),
            pltpu.VMEM((2, 4, 32, 256), F32),
            pltpu.VMEM((32, 256), F32),
            pltpu.VMEM((2, 64, 8192), BF),
            pltpu.VMEM((2, 64, 2048), BF),
            pltpu.SemaphoreType.DMA((22,)),
            pltpu.SemaphoreType.DMA((22,)),
            pltpu.SemaphoreType.DMA((3,)),
        ],
        compiler_params=pltpu.CompilerParams(
            collective_id=0, has_side_effects=True, vmem_limit_bytes=VMEM_BYTES
        ),
        name="align",
    )(
        partner_row, edge_count.T, section_image, base_shift, bilinear_frac, edge_ends, stiffness,
        first_kernel.T, initial_conv_bias.reshape(1, 64), second_kernel, second_bias.reshape(1, 64), *consts,
    )
    return pl.pallas_call(
        _hand_on,
        out_shape=tuple(jax.ShapeDtypeStruct(r.shape, r.dtype) for r in results),
        in_specs=[vm] * 3,
        out_specs=(vm,) * 3,
        name="hand_on",
    )(*results)


def solution(mesh):
    in_specs = (
        P("sec", "tile", None), P("sec"), P("sec", None, "tile", None), P("sec", None, "tile", None),
        P(), P(), P(), P(), P("sec", None, "tile"), P("sec", "tile"), P("sec", "tile"),
    )
    out_specs = (P("sec", None, "tile", None), P("sec", "tile", None), P("sec", None, "tile"))
    return jax.shard_map(local, mesh=mesh, in_specs=in_specs, out_specs=out_specs, check_vma=False)
```

```python
import jax
import jax.numpy as jnp
import numpy as np
from jax import lax
from jax.experimental import pallas as pl
from jax.experimental.pallas import tpu as pltpu
from jax.sharding import PartitionSpec as P

BF = jnp.bfloat16
F32 = jnp.float32
MESH = pl.DeviceIdType.MESH
BIG = -1e30
VMEM_BYTES = 56 * 1024 * 1024

PT = 132
QUADS = PT // 4


def _tables():
    lane = np.arange(128)
    a, b, xx, yy = lane // 64, (lane // 32) % 2, (lane // 16) % 2, lane % 16
    x4, y2 = 2 * xx + b, 2 * yy + a
    ep = np.zeros((4, 128, 6, 128), np.float32)
    for p in range(6):
        ep[x4, 2 * y2 + 15 + p, p, lane] = 1
    oa, ob, ox, oy = lane // 64, (lane // 32) % 2, (lane // 8) % 4, lane % 8
    x8, y1 = 2 * ox + ob, 2 * oy + oa
    eo = np.zeros((8, 64, 6, 128), np.float32)
    for p in range(6):
        eo[x8, 2 * y1 + 15 + p, p, lane] = 1
    wsel = np.zeros((2, 2, 2, 16, 112), np.float32)
    wconst = np.zeros((2, 2, 2, 1, 112), np.float32)
    for e in range(2):
        for ta in range(2):
            for tb in range(2):
                for u in range(4):
                    for v in range(4):
                        wsel[e, ta, tb, 4 * u + v, (u + 2 * ta) * 16 + 8 * e + 2 * tb + v] = 1
                wconst[e, ta, tb, 0, 96 + 4 * e + 2 * ta + tb] = BIG
    wown = np.zeros((2, 2, 16, 64), np.float32)
    for ta in range(2):
        for tb in range(2):
            for u in range(4):
                for v in range(4):
                    wown[ta, tb, 4 * u + v, (u + 2 * ta) * 8 + 2 * tb + v] = 1
    extra = np.zeros((3, 3, 16, 256), np.float32)
    cmask = np.zeros((3, 3, 8, 128), np.float32)
    for tk in range(3):
        for gk, g in enumerate((0, 1, QUADS - 1)):
            for half in range(2):
                for e in range(2):
                    for ta in range(2):
                        for tb in range(2):
                            col = 4 * (4 * g + 2 * half + e) - 8 + x4 + tb
                            row = y2 - 8 + ta
                            bad = (col < 0) | (col > 511)
                            if tk == 0:
                                bad = bad | (row < 0)
                            if tk == 2:
                                bad = bad | (row > 15)
                            extra[tk, gk, 4 * e + 2 * ta + tb, 128 * half : 128 * half + 128] = bad
            extra[tk, gk, 8:11] = 1
            ccol, crow = 8 * g - 4 + lane // 16, lane % 16 - 4
            bad = (ccol < 0) | (ccol > 255)
            if tk == 0:
                bad = bad | (crow < 0)
            if tk == 2:
                bad = bad | (crow > 7)
            cmask[tk, gk] = np.where(bad, BIG, 0.0)
    src = np.arange(1024)
    unflat = np.zeros((1024, 1024), np.float32)
    unflat[src, (src % 8) * 128 + src // 8] = 1
    l2 = np.arange(256)
    lx = 8 * (l2 // 128) + 2 * ((l2 // 8) % 4) + (l2 // 32) % 2
    ly = 2 * (l2 % 8) + (l2 // 64) % 2
    perm = np.zeros((256, 256), np.float32)
    perm[16 * lx + ly, l2] = 1
    home = np.stack([ly + 8, lx + 4]).astype(np.float32)
    return dict(
        ep=ep.reshape(512, 768),
        eo=eo.reshape(512, 768),
        wsel=wsel.reshape(8, 16, 112),
        wconst=wconst.reshape(8, 1, 112),
        extra=extra,
        wown=wown.reshape(4, 16, 64),
        cmask=cmask,
        unflat=unflat,
        home=home,
        perm=perm,
    )


def _split3(x):
    hi = x.astype(BF)
    rest = x - hi.astype(F32)
    mid = rest.astype(BF)
    low = (rest - mid.astype(F32)).astype(BF)
    return hi, mid, low


def _dot(x, y):
    return jnp.dot(x, y, preferred_element_type=F32)


def _kernel(
    pr_ref, cnt_ref, img_ref, sh_ref, fr_ref, ends_ref, stiff_ref, w1_ref, b1_ref, w2_ref, b2_ref,
    wsel_ref, wown_ref, wconst_ref, extra_ref, cmask_ref, home_ref, perm_ref, ep_hbm, eo_hbm, unflat_hbm,
    corr_ref, mis_ref, force_ref,
    j_ref, i_ref, rbuf, anch, gbuf, pbuf, pstage, ep_ref, eo_ref, unflat_ref,
    tall, qp, qo, p4, cpt, obuf, cbuf, wq, wo, bias2, tbuf, px, mpx, fown, cown,
    send_sem, recv_sem, load_sem,
):
    sec = lax.axis_index("sec")
    tile = lax.axis_index("tile")
    back1 = lax.rem(sec + 15, 16)
    back2 = lax.rem(sec + 14, 16)
    fwd1 = lax.rem(sec + 1, 16)
    fwd2 = lax.rem(sec + 2, 16)
    peers = [lax.rem(tile + r, 8) for r in range(8)]
    has_down = tile < 7
    has_up = tile > 0
    tk = jnp.where(tile == 0, 0, jnp.where(tile == 7, 2, 1))

    barrier = pltpu.get_barrier_semaphore()
    for other in (back1, back2, fwd1, fwd2):
        pl.semaphore_signal(barrier, inc=1, device_id=(other, tile), device_id_type=MESH)
    for r in range(1, 8):
        pl.semaphore_signal(barrier, inc=1, device_id=(sec, peers[r]), device_id_type=MESH)

    loads = [
        pltpu.make_async_copy(src, dst, load_sem.at[k])
        for k, (src, dst) in enumerate(((eo_hbm, eo_ref), (ep_hbm, ep_ref), (unflat_hbm, unflat_ref)))
    ]
    for c in loads:
        c.start()

    rows = [sh_ref[s, k, 0:1, :].astype(F32) + fr_ref[s, k, 0:1, :] for s in range(2) for k in range(2)]
    rows = jnp.concatenate(rows + [jnp.zeros((4, 512), F32)], axis=0)
    x_at = lax.broadcasted_iota(jnp.int32, (512, 256), 0)
    v_at = lax.broadcasted_iota(jnp.int32, (512, 256), 1)
    select = jnp.where(x_at == 16 * (v_at - 32 * tile), 1.0, 0.0).astype(BF)
    got = _dot(jnp.concatenate(_split3(rows), axis=0).astype(BF), select)
    anch[...] = (got[16:24] + got[8:16]) + got[0:8]

    lane = lax.broadcasted_iota(jnp.int32, (64, 112), 1)
    bias1 = jnp.broadcast_to(b1_ref[...], (128, 64)).T[:, 0:112]
    hi, mid, low = (x.astype(F32) for x in _split3(bias1))
    base = (
        jnp.where(lane == 104, hi, 0.0) + jnp.where(lane == 105, mid, 0.0) + jnp.where(lane == 106, low, 0.0)
    )
    for m in range(8):
        spread = lax.dot_general(
            w1_ref[...], wsel_ref[m], (((0,), (0,)), ((), ())), preferred_element_type=F32
        )
        wq[64 * m : 64 * m + 64, :] = (spread + base + wconst_ref[m]).astype(BF)
    for m in range(4):
        spread = lax.dot_general(
            w1_ref[...], wown_ref[m], (((0,), (0,)), ((), ())), preferred_element_type=F32
        )
        wo[64 * m : 64 * m + 64, :] = (spread + base[:, 48:112]).astype(BF)
    bias2[...] = jnp.broadcast_to(b2_ref[...], (128, 64)).T

    lane128 = lax.broadcasted_iota(jnp.int32, (1, 128), 1)
    x_bit = [lax.bitwise_and(lax.shift_right_logical(lane128, 3 + k), 1) == 1 for k in range(4)]
    y_bit = [lax.bitwise_and(lax.shift_right_logical(lane128, k), 1) == 1 for k in range(3)]
    row16 = lax.broadcasted_iota(jnp.int32, (16, 256), 0)

    def pixels(s, carry):
        planes = [sh_ref[s, k].astype(F32) for k in range(2)] + [fr_ref[s, k] for k in range(2)]
        tbuf[:, 0:64] = jnp.concatenate(planes, axis=0).T
        runs = [tbuf[pl.ds(x, 32, stride=16), :] for x in range(16)]
        planes = [jnp.concatenate([r[:, 16 * k : 16 * k + 16] for r in runs], axis=1) for k in range(4)]
        parts = [planes[0].astype(BF), planes[1].astype(BF), *_split3(planes[2]), *_split3(planes[3])]
        got = _dot(jnp.concatenate(parts, axis=0), perm_ref[...])
        px[s, 0] = got[0:32] + home_ref[0:1, :]
        px[s, 1] = got[32:64] + home_ref[1:2, :]
        px[s, 2] = (got[128:160] + got[96:128]) + got[64:96]
        px[s, 3] = (got[224:256] + got[192:224]) + got[160:192]
        return carry

    lax.fori_loop(0, 2, pixels, 0, unroll=2)

    pl.semaphore_wait(barrier, 11)

    def remote(src, dst, k, target):
        return pltpu.make_async_remote_copy(
            src_ref=src, dst_ref=dst, send_sem=send_sem.at[k], recv_sem=recv_sem.at[k],
            device_id=target, device_id_type=MESH,
        )

    near = remote(img_ref, rbuf.at[0], 0, (back1, tile))
    far = remote(img_ref, rbuf.at[1], 1, (back2, tile))
    far.start()
    near.start()
    down_tile = (sec, lax.rem(tile + 1, 8))
    up_tile = (sec, lax.rem(tile + 7, 8))
    own_down = remote(img_ref.at[:, 16:32], i_ref.at[:, 0:16], 2, down_tile)
    own_up = remote(img_ref.at[:, 0:16], i_ref.at[:, 48:64], 3, up_tile)
    pl.when(has_down)(own_down.start)
    pl.when(has_up)(own_up.start)
    anchor_sends = [remote(anch, gbuf.at[r], 4 + r, (sec, peers[r])) for r in range(1, 8)]
    for c in anchor_sends:
        c.start()

    i_ref[:, 16:48, :] = img_ref[...]

    @pl.when(tile == 0)
    def _():
        i_ref[:, 0:16, :] = jnp.zeros((2, 16, 1024), BF)
        j_ref[:, 0:32, :] = jnp.zeros((2, 32, 1024), BF)

    @pl.when(tile == 7)
    def _():
        i_ref[:, 48:64, :] = jnp.zeros((2, 16, 1024), BF)
        j_ref[:, 64:96, :] = jnp.zeros((2, 32, 1024), BF)

    for c in anchor_sends:
        c.wait()
    disp = anch[...]
    for r in range(1, 8):
        disp = disp + gbuf[r]
    vert = lax.broadcasted_iota(jnp.int32, (256, 256), 0)
    slot_at = lax.broadcasted_iota(jnp.int32, (1, 256), 1)
    row_of = lax.broadcasted_iota(jnp.int32, (8, 256), 0)
    parts = jnp.concatenate(_split3(disp), axis=0)
    total = jnp.zeros((8, 256), F32)
    for s in range(2):
        table = (vert == ends_ref[s, 1:2, :]).astype(F32) - (vert == ends_ref[s, 0:1, :]).astype(F32)
        table = table.astype(BF)
        got = _dot(parts, table)
        spread = (got[16:24] + got[8:16]) + got[0:8]
        pull = jnp.where(slot_at < cnt_ref[0, s], stiff_ref[s : s + 1, :], 0.0) * spread
        back = lax.dot_general(
            jnp.concatenate(_split3(pull), axis=0), table, (((1,), (1,)), ((), ())),
            preferred_element_type=F32,
        )
        back = (back[16:24] + back[8:16]) + back[0:8]
        total = total - jnp.where(lax.shift_right_logical(row_of, 1) == s, back, 0.0)
    pstage[...] = total
    force_sends = [remote(pstage, pbuf.at[r], 14 + r, (sec, peers[r])) for r in range(1, 8)]
    for c in force_sends:
        c.start()

    pl.when(has_down)(own_down.wait_send)
    pl.when(has_up)(own_up.wait_send)
    pl.when(has_up)(own_down.wait_recv)
    pl.when(has_down)(own_up.wait_recv)
    loads[0].wait()

    def side_by_side(left, right, more):
        return jnp.concatenate(
            [
                jnp.concatenate([left[:, 128 * p : 128 * p + 128], right[:, 128 * p : 128 * p + 128]], axis=1)
                for p in range(6)
            ]
            + [more],
            axis=0,
        )

    def own(s, carry):
        wide = jnp.concatenate([i_ref[s].astype(F32), jnp.zeros((64, 128), F32)], axis=1)
        turned = jnp.concatenate([pltpu.roll(wide, 1, 1), pltpu.roll(wide, 1151, 1)], axis=0)
        tall[...] = turned.T
        stack = [tall[4 * k : 4 * k + 1024, :].reshape(64, 16, 128)[:, 0:8, :].reshape(512, 128) for k in range(4)]
        stack = jnp.concatenate([x.astype(BF) for x in stack], axis=1)
        qo[...] = _dot(stack, eo_ref[...])

        ones = extra_ref[1, 1].astype(F32)

        def encode(c, carry):
            small = []
            for n in range(4):
                r0 = pl.multiple_of(64 * c + 16 * n, 16)
                patches = side_by_side(qo[pl.ds(r0, 8), :], qo[pl.ds(r0 + 8, 8), :], ones).astype(BF)
                got = jnp.maximum(_dot(wo[0:64, :], patches).astype(BF), 0)
                fown[s, :, pl.ds(pl.multiple_of(1024 * c + 256 * n, 256), 256)] = got
                small += [patches[:, 0:32], patches[:, 128:160]]
            own4 = jnp.maximum(_dot(wo[...], jnp.concatenate(small, axis=1)).astype(BF), 0)
            pre = _dot(w2_ref[...], own4)
            pre = jnp.maximum(pre + jnp.concatenate([bias2[...]] * 2, axis=1), 0.0)
            cown[s, :, pl.ds(pl.multiple_of(256 * c, 256), 256)] = pre.astype(BF)
            return carry

        return lax.fori_loop(0, 8, encode, carry, unroll=8)

    own(0, 0)

    near.wait()
    far.wait()
    for s in range(2):
        p = pr_ref[s]
        which = jnp.where(lax.shift_right_logical(p, 1) == fwd1, 0, 1)
        slot = lax.bitwise_and(p, 1)
        j_ref[s, 32:64, :] = rbuf[which, slot]
    part_down = remote(j_ref.at[:, 32:64], j_ref.at[:, 0:32], 12, down_tile)
    part_up = remote(j_ref.at[:, 32:64], j_ref.at[:, 64:96], 13, up_tile)
    pl.when(has_down)(part_down.start)
    pl.when(has_up)(part_up.start)

    own(1, 0)

    for c in force_sends:
        c.wait()
    total = pstage[...]
    for r in range(1, 8):
        total = total + pbuf[r]
    turned = pltpu.roll(total, lax.rem(256 - 32 * tile, 256), 1)
    for s in range(2):
        force_ref[s] = turned[2 * s : 2 * s + 2, 0:32]

    pl.when(has_down)(part_down.wait_send)
    pl.when(has_up)(part_up.wait_send)
    pl.when(has_up)(part_down.wait_recv)
    pl.when(has_down)(part_up.wait_recv)
    loads[1].wait()
    loads[2].wait()

    def section(s, carry):
        wide = jnp.concatenate([j_ref[s].astype(F32), jnp.zeros((96, 128), F32)], axis=1)
        turned = jnp.concatenate([pltpu.roll(wide, 17, 1), jnp.zeros((32, 1152), F32)], axis=0)
        tall[...] = turned.T
        stack = jnp.concatenate([tall[2 * k : 2 * k + 1056, :].astype(BF) for k in range(4)], axis=1)
        qp[...] = _dot(stack, ep_ref[...]).astype(BF)

        def partner(g, carry):
            r0 = pl.multiple_of(32 * g, 32)
            kind = jnp.where(g == 0, 0, jnp.where(g == QUADS - 1, 2, 1))
            patches = side_by_side(qp[pl.ds(r0, 16), :], qp[pl.ds(r0 + 16, 16), :], extra_ref[tk, kind])
            got = jnp.maximum(_dot(wq[...], patches).astype(BF), 0)
            l0 = pl.multiple_of(512 * g, 512)
            p4[:, pl.ds(l0, 512)] = jnp.concatenate(
                [got[0:256, 0:128], got[256:512, 0:128], got[0:256, 128:256], got[256:512, 128:256]], axis=1
            )
            return carry

        def coarsen(q, count):
            tiles = p4[:, pl.ds(pl.multiple_of(512 * q, 512), 512 * count)]
            tiles = jnp.concatenate([tiles[:, 128 * k : 128 * k + 32] for k in range(4 * count)], axis=1)
            pre = _dot(w2_ref[...], tiles)
            for n in range(count):
                kind = jnp.where(q + n == 0, 0, jnp.where(q + n == QUADS - 1, 2, 1))
                coarse = pre[:, 128 * n : 128 * n + 128] + bias2[...] + cmask_ref[tk, kind][0:1, :]
                coarse = jnp.maximum(coarse, 0.0).astype(BF).astype(F32)
                cpt[pl.ds(pl.multiple_of(128 * (q + n), 128), 128), 0:64] = coarse.T.astype(BF)

        def both(g, carry):
            coarsen(4 * g - 4, 4)
            for n in range(4):
                partner(4 * g + n, carry)
            return carry

        for n in range(4):
            partner(n, 0)
        lax.fori_loop(1, QUADS // 4, both, 0, unroll=7)
        coarsen(QUADS - 5, 4)
        partner(QUADS - 1, 0)
        coarsen(QUADS - 1, 1)

        def block(c, carry):
            for half in range(2):
                b = 2 * c + half
                own_map = fown[s, :, pl.ds(pl.multiple_of(256 * b, 256), 256)].astype(F32)
                row = px[s, 0, pl.ds(b, 1), :]
                col = px[s, 1, pl.ds(b, 1), :]
                fy = px[s, 2, pl.ds(b, 1), :]
                fx = px[s, 3, pl.ds(b, 1), :]
                row = jnp.broadcast_to(row.astype(jnp.int32), (16, 256))
                col = jnp.broadcast_to(col, (16, 256)).astype(BF)
                oy = [(row == 2 * row16 + a).astype(F32).astype(BF) for a in range(2)]
                zero = jnp.zeros((16, 256), BF)
                picks = []
                for k in range(6):
                    hit = {}
                    for bb in range(2):
                        for xx in range(2):
                            hit[bb, xx] = col == float(4 * k + 2 * xx + bb)
                    for a in range(2):
                        for bb in range(2):
                            for xx in range(2):
                                picks.append(jnp.where(hit[bb, xx], oy[a], zero))
                choose = jnp.concatenate(picks, axis=0)
                l0 = pl.multiple_of(512 * b + 128, 128)
                taps = _dot(p4[:, pl.ds(l0, 768)], choose)
                gy, gx = 1.0 - fy, 1.0 - fx
                warped = (
                    (gy * gx) * taps[0:64] + (gy * fx) * taps[64:128]
                    + (fy * gx) * taps[128:192] + (fy * fx) * taps[192:256]
                )
                differ = own_map - warped
                mpx[pl.ds(b, 1), :] = jnp.sum(differ * differ, axis=0, keepdims=True) * (1.0 / 64)

            coarse = cown[s, :, pl.ds(pl.multiple_of(128 * c, 128), 128)]
            there = cpt[pl.ds(pl.multiple_of(256 * c, 256), 384), 0:64]
            gram = _dot(there, coarse).reshape(24, 16, 128)
            for k, keep in ((3, 16), (2, 12), (1, 10), (0, 9)):
                step = 1 << k
                gram = jnp.where(x_bit[k][None], gram[step : step + keep], gram[0:keep])
            gram = gram.reshape(144, 128)
            cols = []
            for j in range(9):
                v = gram[16 * j : 16 * j + 16]
                for k in (2, 1, 0):
                    v = jnp.where(y_bit[k], pltpu.roll(v, 16 - (1 << k), 0), v)
                cols.append(v)
            gram = jnp.concatenate(cols, axis=0) * (1.0 / 64)
            obuf[pl.ds(pl.multiple_of(144 * s, 16), 144), pl.ds(pl.multiple_of(128 * c, 128), 128)] = gram.astype(BF)
            return carry

        lax.fori_loop(0, 16, block, 0, unroll=16)

        got = lax.dot_general(
            jnp.concatenate(_split3(mpx[...]), axis=0), perm_ref[...], (((1,), (1,)), ((), ())),
            preferred_element_type=F32,
        )
        got = (got[64:96] + got[32:64]) + got[0:32]
        for x in range(16):
            tbuf[pl.ds(x, 32, stride=16), 0:16] = got[:, 16 * x : 16 * x + 16]
        mis_ref[s] = tbuf[...].T[0:16, :]

        return carry

    lax.fori_loop(0, 2, section, 0, unroll=2)

    for h in range(2):
        flat = _dot(obuf[:, 1024 * h : 1024 * h + 1024], unflat_ref[...])
        for s in range(2):
            for j in range(9):
                r0 = 144 * s + 16 * j
                for y in range(8):
                    cbuf[s, pl.ds(8 * j + y, 9, stride=72), :] = flat[r0 : r0 + 9, 128 * y : 128 * y + 128]
        for s in range(2):
            corr_ref[s, :, :, 128 * h : 128 * h + 128] = cbuf[s].reshape(81, 8, 128).astype(BF)


def _hand_on(a, b, c, x, y, z):
    x[...] = a[...]
    y[...] = b[...]
    z[...] = c[...]


def local(
    section_image, partner_row, base_shift, bilinear_frac, first_kernel, initial_conv_bias,
    second_kernel, second_bias, edge_ends, edge_count, stiffness,
):
    t = _tables()
    vm = pl.BlockSpec(memory_space=pltpu.VMEM)
    sm = pl.BlockSpec(memory_space=pltpu.SMEM)
    hbm = pl.BlockSpec(memory_space=pl.ANY)
    consts = [
        jnp.asarray(t["wsel"], BF), jnp.asarray(t["wown"], BF), jnp.asarray(t["wconst"], F32), jnp.asarray(t["extra"], BF),
        jnp.asarray(t["cmask"], F32), jnp.asarray(t["home"], F32), jnp.asarray(t["perm"], BF),
        jnp.asarray(t["ep"], BF), jnp.asarray(t["eo"], BF), jnp.asarray(t["unflat"], BF),
    ]
    results = pl.pallas_call(
        _kernel,
        out_shape=(
            jax.ShapeDtypeStruct((2, 81, 8, 256), BF),
            jax.ShapeDtypeStruct((2, 16, 512), F32),
            jax.ShapeDtypeStruct((2, 2, 32), F32),
        ),
        in_specs=[sm, sm] + [vm] * 16 + [hbm] * 3,
        out_specs=(vm, vm, vm),
        scratch_shapes=[
            pltpu.VMEM((2, 96, 1024), BF),
            pltpu.VMEM((2, 64, 1024), BF),
            pltpu.VMEM((2, 2, 32, 1024), BF),
            pltpu.VMEM((8, 256), F32),
            pltpu.VMEM((8, 8, 256), F32),
            pltpu.VMEM((8, 8, 256), F32),
            pltpu.VMEM((8, 256), F32),
            pltpu.VMEM((512, 768), BF),
            pltpu.VMEM((512, 768), BF),
            pltpu.VMEM((1024, 1024), BF),
            pltpu.VMEM((1152, 128), F32),
            pltpu.VMEM((1056, 768), BF),
            pltpu.VMEM((512, 768), F32),
            pltpu.VMEM((256, PT * 128), BF),
            pltpu.VMEM((PT * 32, 128), BF),
            pltpu.VMEM((288, 2048), BF),
            pltpu.VMEM((2, 648, 128), F32),
            pltpu.VMEM((512, 112), BF),
            pltpu.VMEM((256, 64), BF),
            pltpu.VMEM((64, 128), F32),
            pltpu.VMEM((512, 128), F32),
            pltpu.VMEM((2, 4, 32, 256), F32),
            pltpu.VMEM((32, 256), F32),
            pltpu.VMEM((2, 64, 8192), BF),
            pltpu.VMEM((2, 64, 2048), BF),
            pltpu.SemaphoreType.DMA((22,)),
            pltpu.SemaphoreType.DMA((22,)),
            pltpu.SemaphoreType.DMA((3,)),
        ],
        compiler_params=pltpu.CompilerParams(
            collective_id=0, has_side_effects=True, vmem_limit_bytes=VMEM_BYTES
        ),
        name="align",
    )(
        partner_row, edge_count.T, section_image, base_shift, bilinear_frac, edge_ends, stiffness,
        first_kernel.T, initial_conv_bias.reshape(1, 64), second_kernel, second_bias.reshape(1, 64), *consts,
    )
    return pl.pallas_call(
        _hand_on,
        out_shape=tuple(jax.ShapeDtypeStruct(r.shape, r.dtype) for r in results),
        in_specs=[vm] * 3,
        out_specs=(vm,) * 3,
        name="hand_on",
    )(*results)


def solution(mesh):
    in_specs = (
        P("sec", "tile", None), P("sec"), P("sec", None, "tile", None), P("sec", None, "tile", None),
        P(), P(), P(), P(), P("sec", None, "tile"), P("sec", "tile"), P("sec", "tile"),
    )
    out_specs = (P("sec", None, "tile", None), P("sec", "tile", None), P("sec", None, "tile"))
    return jax.shard_map(local, mesh=mesh, in_specs=in_specs, out_specs=out_specs, check_vma=False)
```
